32 devices in a mesh: fsdp: 16 (over z, y, x), tp: 2 (over core).
Axes of the slice: x: 2, y: 2, z: 4, core: 2. Of those that a mesh axis runs over, the one named last changes fastest.
Arguments:
- tokens: bfloat16 [8192, 2048], P(('fsdp', 'tp'))
- cotangent: bfloat16 [8192, 2048], P(('fsdp', 'tp')), may hold values from -6 to 6
- seg_ids: int32 [8192], P('fsdp'), may hold values from 0 to 12, as said below
- parents: int32 [16, 13], P('fsdp'), may hold values from 0 to 11, as said below
- valid_mask: int32 [8192], P('fsdp'), may hold values from 0 to 1, as said below
- ln1_gain: float32 [2048], replicated, may hold values from 0.5 to 1.5
- ln1_bias: float32 [2048], replicated, may hold values from -1.5 to 1.5
- w_qkv: bfloat16 [2048, 3, 2048], P('fsdp', None, 'tp')
- qkv_bias: float32 [3, 2048], P(None, 'tp'), may hold values from -1.5 to 1.5
- w_out: bfloat16 [2048, 2048], P('fsdp', 'tp'), may hold values from -0.25 to 0.25
- ln2_gain: float32 [2048], replicated, may hold values from 0.5 to 1.5
- ln2_bias: float32 [2048], replicated, may hold values from -1.5 to 1.5
- w_gate_up: bfloat16 [2048, 2, 5632], P('fsdp', None, 'tp')
- w_down: bfloat16 [2048, 5632], P('fsdp', 'tp'), may hold values from -0.15625 to 0.15625
Outputs:
- output: bfloat16 [8192, 2048], P(('fsdp', 'tp'))
- tokens_grad: float32 [8192, 2048], P(('fsdp', 'tp'))
- ln1_gain_grad: float32 [2048], replicated
- ln1_bias_grad: float32 [2048], replicated
- qkv_grad: float32 [2048, 3, 2048], P('fsdp', None, 'tp')
- qkv_bias_grad: float32 [3, 2048], P(None, 'tp')
- out_grad: float32 [2048, 2048], P('fsdp', 'tp')
- ln2_gain_grad: float32 [2048], replicated
- ln2_bias_grad: float32 [2048], replicated
- gate_up_grad: float32 [2048, 2, 5632], P('fsdp', None, 'tp')
- down_grad: float32 [2048, 5632], P('fsdp', 'tp')
- stream_rms: float32 [3], replicated
The draws below stay inside these ranges and needn't reach their ends.
Inputs may be any that keep to these rules, and one draw needn't show every extreme that they name: `seg_ids`: in each group of 512 rows the segment numbers never fall, start at 0, and each of 0 to 12 occurs on some valid row. parents[g, 0] = 0 and parents[g, 1] = 0; any other segment's parent is 0 or an earlier segment whose parent is 0. `valid_mask`: padding slots of a group lie right after the tokens of its segment 0 and carry segment 0; the first and the last row of every group are valid.
All inputs are finite; a program needn't handle non-finite values.
Results may differ from the reference program's by a relative error of at most 0.015.
Values may be sent and summed in bfloat16 or wider, within the bound.
No kernel may reach another device: no remote copies, remote signals or barrier semaphores. Data moves between devices by JAX's collectives and lax.ppermute only.
A program may use at most 256 MiB of HBM per device.

```python
import math
import jax
import jax.numpy as jnp
from jax import lax

D = 2048
HD = 64
ROT = 16
FF = 5632
SEGS = 13
TOK_DEV = 256
TOKENS = 8192
N_FSDP = 16
N_TP = 2


def tree_layout(key):
    groups = N_FSDP
    group_rows = TOK_DEV * N_TP
    subkeys = jax.random.split(key, 5)
    group_index = jnp.arange(groups, dtype=jnp.int32)
    ceiling = 2 * group_rows // 3
    ramp_base = ceiling * (groups - 1 - group_index) // max(groups - 1, 1)
    jitter = jax.random.randint(subkeys[0], (groups,), 0, group_rows // 8 + 1)
    padding = jnp.minimum(ramp_base + jitter, ceiling)
    live_count = group_rows - padding
    weights = jax.random.randint(subkeys[1], (groups, SEGS), 1, 5)
    trunk_weight = jax.random.randint(subkeys[2], (groups,), 16, 33)
    weights = weights.at[:, 0].set(trunk_weight)
    running = jnp.cumsum(weights, axis=1)
    seg_ends = jnp.arange(1, SEGS + 1, dtype=jnp.int32)[None, :] + (live_count - SEGS)[:, None] * running // running[:, -1:]
    trunk_len = seg_ends[:, 0:1]
    position = jnp.arange(group_rows, dtype=jnp.int32)[None, :]
    in_trunk = position < trunk_len
    past_pad = position >= trunk_len + padding[:, None]
    counted = jnp.where(in_trunk, position, jnp.where(past_pad, position - padding[:, None], 0))
    segment = jnp.sum((seg_ends[:, None, :] <= counted[:, :, None]).astype(jnp.int32), axis=2)
    valid_rows = (in_trunk | past_pad).astype(jnp.int32)
    labels = jnp.arange(SEGS, dtype=jnp.int32)
    branch = jax.random.randint(subkeys[3], (groups, SEGS), 0, 3) == 0
    branch = branch & (labels[None, :] >= 1) | (labels[None, :] == 1) | (labels[None, :] == SEGS - 2)
    branch = branch & (labels[None, :] != SEGS - 1)
    through = jnp.cumsum(branch.astype(jnp.int32), axis=1)
    earlier = through - branch.astype(jnp.int32)
    chosen = jax.random.randint(subkeys[4], (groups, SEGS), 0, 1 << 20) % jnp.maximum(earlier, 1)
    matches = branch[:, None, :] & (through[:, None, :] == (chosen + 1)[:, :, None])
    leaf_parent = jnp.sum(jnp.where(matches, labels[None, None, :], 0), axis=2)
    leaf_parent = jnp.where(labels[None, :] == SEGS - 1, SEGS - 2, leaf_parent)
    parent_table = jnp.where(branch | (labels[None, :] == 0), 0, leaf_parent).astype(jnp.int32)
    return (segment.reshape(-1).astype(jnp.int32), parent_table, valid_rows.reshape(-1))


def draw_seg_ids(key, part):
    return tree_layout(key)[0]


def draw_parents(key, part):
    return tree_layout(key)[1]


def draw_valid_mask(key, part):
    return tree_layout(key)[2]


def draw_tokens(key, part):
    key = jax.random.fold_in(key, 11)
    subkeys = jax.random.split(key, 3)
    ramp = jnp.arange(TOKENS, dtype=jnp.float32)[:, None] / TOKENS
    row_scale = jnp.exp(math.log(3.0) * ramp + jax.random.uniform(subkeys[0], (TOKENS, 1), jnp.float32, -0.3, 0.3))
    col_scale = jnp.exp(jax.random.uniform(subkeys[1], (1, D), jnp.float32, math.log(0.5), math.log(5.0)))
    basis = jax.random.normal(subkeys[2], (TOKENS, D), jnp.float32)
    return (basis * row_scale * col_scale).astype(jnp.bfloat16)


def draw_w_qkv(key, part):
    key = jax.random.fold_in(key, 21)
    subkeys = jax.random.split(key, 2)
    random_part = jax.random.normal(subkeys[0], (D, 3, D), jnp.float32)
    column_shift = jax.random.uniform(subkeys[1], (1, 3, D), jnp.float32, -1.2, 1.2)
    return ((random_part + column_shift) * (1.0 / math.sqrt(D))).astype(jnp.bfloat16)


def draw_w_gate_up(key, part):
    key = jax.random.fold_in(key, 23)
    subkeys = jax.random.split(key, 2)
    random_part = jax.random.normal(subkeys[0], (D, 2, FF), jnp.float32)
    column_shift = jax.random.uniform(subkeys[1], (1, 2, FF), jnp.float32, -1.2, 1.2)
    return ((random_part + column_shift) * (1.0 / math.sqrt(D))).astype(jnp.bfloat16)


def steps_of(key, dims, cuts, smallest, high):
    def one(axis_at, blocks):
        heights = jax.random.uniform(jax.random.fold_in(jax.random.fold_in(key, 6), axis_at), (blocks,), jnp.float32, smallest / len(cuts), high / len(cuts))
        return jnp.repeat(jnp.exp(heights), dims[axis_at] // blocks).reshape((-1,) + (1,) * (len(dims) - axis_at - 1))

    loudness = one(*cuts[0])
    for cut in cuts[1:]:
        loudness = loudness * one(*cut)
    return loudness


def centred(own_key, dims, width, limit, cuts=(), kind=jnp.bfloat16):
    entries = width * jax.random.normal(own_key, dims, jnp.float32)
    if cuts:
        entries = entries * steps_of(own_key, dims, cuts, -0.22, 0.18)
    return jnp.clip(entries, -limit, limit).astype(kind)


def setup_inputs(seed: int = 0) -> dict:
    key_list = jax.random.split(jax.random.key(seed), 15)
    return {
        "tokens": draw_tokens(jax.random.fold_in(key_list[14], 71), 0),
        "cotangent": centred(key_list[1], (TOKENS, D), 1.0, 6.0, ((0, 32),)),
        "seg_ids": draw_seg_ids(jax.random.fold_in(key_list[14], 71), 0),
        "parents": draw_parents(jax.random.fold_in(key_list[14], 71), 0),
        "valid_mask": draw_valid_mask(jax.random.fold_in(key_list[14], 71), 0),
        "ln1_gain": jnp.clip(1.0 + 0.1 * jax.random.normal(key_list[5], (D,), jnp.float32), 0.5, 1.5),
        "ln1_bias": centred(key_list[6], (D,), 0.3, 1.5, (), jnp.float32),
        "w_qkv": draw_w_qkv(jax.random.fold_in(key_list[14], 71), 0),
        "qkv_bias": centred(key_list[8], (3, D), 0.3, 1.5, ((1, 2),), jnp.float32),
        "w_out": centred(key_list[9], (D, D), (D // 4) ** -0.5, 0.25, ((0, 16), (1, 2))),
        "ln2_gain": jnp.clip(1.0 + 0.1 * jax.random.normal(key_list[10], (D,), jnp.float32), 0.5, 1.5),
        "ln2_bias": centred(key_list[11], (D,), 0.3, 1.5, (), jnp.float32),
        "w_gate_up": draw_w_gate_up(jax.random.fold_in(key_list[14], 71), 0),
        "w_down": centred(key_list[13], (D, FF), (FF // 4) ** -0.5, 0.15625, ((0, 16), (1, 2))),
    }


epsilon = 1e-05
score_scale = 0.125
masked_fill = -1e+30
highest = lax.Precision.HIGHEST

@jax.custom_vjp
def low(v):
    return lax.optimization_barrier(v.astype(jnp.bfloat16)).astype(jnp.float32)

@jax.custom_vjp
def low_back(v):
    return v

def low_keep(v):
    return (low(v), None)

def low_pass(kept, grad):
    return (grad,)

def back_keep(v):
    return (v, None)

def back_low(kept, grad):
    return (low(grad),)
low.defvjp(low_keep, low_pass)
low_back.defvjp(back_keep, back_low)

def tree_mask(seg_ids, parents, valid_mask):
    row_count = seg_ids.shape[0]
    labels = jnp.arange(parents.shape[0], dtype=jnp.int32)
    parent_one = lax.optimization_barrier(jnp.sum(jnp.where(seg_ids[:, None] == labels[None, :], parents[None, :], 0), axis=1)).astype(jnp.int32)
    parent_two = lax.optimization_barrier(jnp.sum(jnp.where(parent_one[:, None] == labels[None, :], parents[None, :], 0), axis=1)).astype(jnp.int32)
    row_ids = jnp.arange(row_count, dtype=jnp.int32)
    key_segs = seg_ids[None, :]
    related = (key_segs == seg_ids[:, None]) | (key_segs == parent_one[:, None]) | (key_segs == parent_two[:, None])
    allowed = related & (row_ids[None, :] <= row_ids[:, None]) & (valid_mask[None, :] > 0)
    allowed = allowed | (row_ids[None, :] == row_ids[:, None])
    positions = (lax.optimization_barrier(jnp.sum(allowed.astype(jnp.int32), axis=1)) - 1).astype(jnp.int32)
    return (allowed, positions)

def rotary_tables(positions, rot_width):
    half_width = rot_width // 2
    inverse_freq = jnp.exp(jnp.arange(half_width, dtype=jnp.float32) * (-2.0 * math.log(10000.0) / rot_width))
    angles = positions.astype(jnp.float32)[:, None] * inverse_freq[None, :]
    return (jnp.cos(angles), jnp.sin(angles))

def rotate(values, cosine, sine):
    half_width = cosine.shape[1]
    first_half = values[..., :half_width]
    second_half = values[..., half_width:2 * half_width]
    remainder = values[..., 2 * half_width:]
    cos_b = cosine[:, None, :]
    sin_b = sine[:, None, :]
    return jnp.concatenate([first_half * cos_b - second_half * sin_b, second_half * cos_b + first_half * sin_b, remainder], axis=-1)

def layer_norm(values, gain, shift):
    centre = values - lax.optimization_barrier(jnp.mean(values, axis=-1, keepdims=True))
    normed = centre * lax.rsqrt(lax.optimization_barrier(jnp.mean(centre * centre, axis=-1, keepdims=True)) + epsilon)
    return normed * gain + shift

def attend_group(packed):
    query_rows, key_rows, value_rows, segments, parent_row, valid_rows = packed
    allowed = tree_mask(segments, parent_row, valid_rows)[0]
    scores = low_back(jnp.einsum('rhe,khe->hrk', query_rows, key_rows, precision=highest) * score_scale)
    scores = jnp.where(allowed[None], scores, masked_fill)
    attn_probs = low(jax.nn.softmax(scores, axis=-1))
    return jnp.einsum('hrk,khe->rhe', attn_probs, value_rows, precision=highest)

def reference(tokens, cotangent, seg_ids, parents, valid_mask, ln1_gain, ln1_bias, w_qkv, qkv_bias, w_out, ln2_gain, ln2_bias, w_gate_up, w_down):
    groups = parents.shape[0]
    group_rows = seg_ids.shape[0] // groups
    model_width = tokens.shape[1]
    head_count = model_width // HD
    seg_groups = seg_ids.reshape(groups, group_rows)
    valid_groups = valid_mask.reshape(groups, group_rows)

    def group_positions(packed):
        return tree_mask(packed[0], packed[1], packed[2])[1]
    positions = lax.map(group_positions, (seg_groups, parents, valid_groups)).reshape(-1)
    cosine, sine = rotary_tables(positions, ROT)
    keep_rows = valid_mask.astype(jnp.float32)[:, None]

    def grouped(values):
        return values.reshape(groups, group_rows, head_count, HD)

    def forward(stream, gain_one, bias_one, qkv_weight, qkv_shift, out_weight, gain_two, bias_two, gate_up_weight, down_weight):
        normed1 = low(layer_norm(stream, gain_one, bias_one))
        linear = low_back(jnp.einsum('td,dcf->tcf', normed1, qkv_weight, precision=highest) + qkv_shift[None])
        queries = low(rotate(linear[:, 0].reshape(-1, head_count, HD), cosine, sine))
        keys_all = low(rotate(linear[:, 1].reshape(-1, head_count, HD), cosine, sine))
        values_all = low(linear[:, 2].reshape(-1, head_count, HD))
        context = lax.map(jax.checkpoint(attend_group), (grouped(queries), grouped(keys_all), grouped(values_all), seg_groups, parents, valid_groups))
        context = low_back(low(context.reshape(-1, model_width) * keep_rows))
        attn_out = low_back(jnp.dot(context, out_weight.T, precision=highest))
        residual = stream + attn_out
        normed2 = low(layer_norm(residual, gain_two, bias_two))
        gate_up = low_back(jnp.einsum('td,dcf->tcf', normed2, gate_up_weight, precision=highest))
        hidden = low(jax.nn.silu(gate_up[:, 0]) * gate_up[:, 1])
        mlp_out = jnp.dot(hidden, down_weight.T, precision=highest)
        return (residual + mlp_out, (attn_out, mlp_out))
    params = (tokens.astype(jnp.float32), ln1_gain, ln1_bias, w_qkv.astype(jnp.float32), qkv_bias, w_out.astype(jnp.float32), ln2_gain, ln2_bias, w_gate_up.astype(jnp.float32), w_down.astype(jnp.float32))
    stream_out, pullback, extras = jax.vjp(forward, *params, has_aux=True)
    grads = pullback(cotangent.astype(jnp.float32))
    attn_out, mlp_out = extras
    totals = jnp.stack([jnp.sum(keep_rows * stream_out * stream_out), jnp.sum(keep_rows * attn_out * attn_out), jnp.sum(keep_rows * mlp_out * mlp_out)])
    stream_rms = jnp.sqrt(totals / (jnp.sum(keep_rows) * model_width))
    return (stream_out.astype(jnp.bfloat16), grads[0], grads[1], grads[2], grads[3], grads[4], grads[5], grads[6], grads[7], grads[8], grads[9], stream_rms)
```

```python
from functools import partial
import math

import jax
import jax.numpy as jnp
from jax import lax
from jax.sharding import Mesh, PartitionSpec as P

HD = 64
ROT = 16

epsilon = 1e-05
score_scale = 0.125
masked_fill = -1e30

FAR, MID, NEAR, TP = "far", "mid", "near", "tp"
ALL = (FAR, MID, NEAR, TP)
f32 = jnp.float32
bf16 = jnp.bfloat16


def swap(values, axis):
    return lax.ppermute(values, axis, [(0, 1), (1, 0)])


def ordered(axis, mine, other):
    first = lax.axis_index(axis) == 0
    return jnp.where(first, mine, other), jnp.where(first, other, mine)


def mine_of(axis, pair):
    return ordered(axis, pair[0], pair[1])


def spread_columns(kinds):
    width = kinds[0].shape[1] // 4

    def quarters(index):
        return jnp.concatenate(
            [kind[:, q * width : (q + 1) * width] for q in (index, 2 + index) for kind in kinds], axis=1
        )

    keep, send = mine_of(NEAR, (quarters(0), quarters(1)))
    rows = jnp.concatenate(ordered(NEAR, keep, swap(send, NEAR)), axis=0)
    half = rows.shape[1] // 2
    keep, send = mine_of(MID, (rows[:, :half], rows[:, half:]))
    return jnp.concatenate(ordered(MID, keep, swap(send, MID)), axis=0)


def return_columns(values, count):
    rows = values.shape[0] // 4
    width = values.shape[1] // count
    keep, send = mine_of(MID, (values[: 2 * rows], values[2 * rows :]))
    both = jnp.concatenate(ordered(MID, keep, swap(send, MID)), axis=1)
    keep, send = mine_of(NEAR, (both[:rows], both[rows:]))
    near = ordered(NEAR, keep, swap(send, NEAR))
    kinds = []
    for kind in range(count):
        pieces = []
        for q in range(4):
            start = (q // 2) * count * width + kind * width
            pieces.append(near[q % 2][:, start : start + width])
        kinds.append(jnp.concatenate(pieces, axis=1).astype(f32))
    return kinds


def gather_rows(own):
    half = own.shape[0] // 2
    near = swap(own, NEAR)
    mid = swap(own, MID)
    diagonal_low = swap(near[:half], MID)
    diagonal_high = swap(mid[half:], NEAR)
    core = jnp.concatenate([own, near, mid, diagonal_low, diagonal_high], axis=0)
    return jnp.concatenate([core, swap(core, TP)], axis=0)


def add_low(a, b):
    return (a.astype(f32) + b.astype(f32)).astype(bf16)


def scatter_rows(total):
    core_rows = total.shape[0] // 2
    rows = core_rows // 4
    half = rows // 2
    core = add_low(total[:core_rows], swap(total[core_rows:], TP))
    own, near, mid, diagonal = [core[i * rows : (i + 1) * rows] for i in range(4)]
    to_mid = swap(diagonal[:half], MID)
    to_near = swap(diagonal[half:], NEAR)
    near = jnp.concatenate([add_low(near[:half], to_mid), near[half:]], axis=0)
    mid = jnp.concatenate([mid[:half], add_low(mid[half:], to_near)], axis=0)
    return own.astype(f32) + swap(near, NEAR).astype(f32) + swap(mid, MID).astype(f32)


def gather_far(values):
    return lax.all_gather(values, FAR, axis=0, tiled=True)


def scatter_far(values):
    return lax.psum_scatter(values, FAR, scatter_dimension=0, tiled=True)


def plane_trees(values):
    trees = lax.all_gather(values, (MID, NEAR), axis=0, tiled=False)
    trees = trees.reshape((2, 2) + values.shape)
    trees = jnp.where(lax.axis_index(MID) == 0, trees, trees[::-1])
    trees = jnp.where(lax.axis_index(NEAR) == 0, trees, trees[:, ::-1])
    return trees.reshape((4,) + values.shape)


def tree_mask(seg_ids, parents, valid_mask, row_ids):
    labels = jnp.arange(parents.shape[0], dtype=jnp.int32)
    parent_one = jnp.sum(
        jnp.where(seg_ids[:, None] == labels[None, :], parents[None, :], 0), axis=1
    )
    parent_two = jnp.sum(
        jnp.where(parent_one[:, None] == labels[None, :], parents[None, :], 0), axis=1
    )
    key_segs = seg_ids[None, :]
    related = (
        (key_segs == seg_ids[:, None])
        | (key_segs == parent_one[:, None])
        | (key_segs == parent_two[:, None])
    )
    allowed = related & (row_ids[None, :] <= row_ids[:, None]) & (valid_mask[None, :] > 0)
    allowed = allowed | (row_ids[None, :] == row_ids[:, None])
    positions = jnp.sum(allowed.astype(jnp.int32), axis=1) - 1
    return (allowed, positions)


def rotary_tables(positions, rot_width):
    half_width = rot_width // 2
    inverse_freq = jnp.exp(
        jnp.arange(half_width, dtype=f32) * (-2.0 * math.log(10000.0) / rot_width)
    )
    angles = positions.astype(f32)[:, None] * inverse_freq[None, :]
    return (jnp.cos(angles), jnp.sin(angles))


def rotate(values, cosine, sine):
    half_width = cosine.shape[1]
    first_half = values[..., :half_width]
    second_half = values[..., half_width : 2 * half_width]
    remainder = values[..., 2 * half_width :]
    cos_b = cosine[:, None, :]
    sin_b = sine[:, None, :]
    return jnp.concatenate(
        [
            first_half * cos_b - second_half * sin_b,
            second_half * cos_b + first_half * sin_b,
            remainder,
        ],
        axis=-1,
    )


def layer_norm(values, gain, shift):
    centre = values - jnp.mean(values, axis=-1, keepdims=True)
    inverse = lax.rsqrt(jnp.mean(centre * centre, axis=-1, keepdims=True) + epsilon)
    normed = centre * inverse
    return (normed * gain + shift, normed, inverse)


def norm_back(grad_out, normed, inverse, gain):
    scaled = grad_out * gain
    centred = (
        scaled
        - jnp.mean(scaled, axis=-1, keepdims=True)
        - normed * jnp.mean(scaled * normed, axis=-1, keepdims=True)
    )
    return (inverse * centred, jnp.sum(grad_out * normed, axis=0), jnp.sum(grad_out, axis=0))


def by_trees(values):
    rows = values.shape[0] // 8
    return values.reshape(2, 4, rows, -1).transpose(1, 0, 2, 3).reshape(4, 2 * rows, -1)


def from_trees(values):
    rows = values.shape[1] // 2
    return values.reshape(4, 2, rows, -1).transpose(1, 0, 2, 3).reshape(8 * rows, -1)


def pair_heads(values):
    return values.reshape(values.shape[0], -1, HD)


def flat_heads(values):
    return values.reshape(values.shape[0], -1)


def attend_forward(packed):
    allowed = packed[3]
    query_rows = pair_heads(packed[0])
    key_rows = pair_heads(packed[1])
    value_rows = pair_heads(packed[2])
    scores = (
        jnp.einsum("rhe,khe->hrk", query_rows, key_rows, preferred_element_type=f32) * score_scale
    )
    scores = jnp.where(allowed[None], scores, masked_fill)
    row_max = jnp.max(scores, axis=-1, keepdims=True)
    exponent = jnp.exp(scores - row_max)
    row_sum = jnp.sum(exponent, axis=-1, keepdims=True)
    attn_probs = (exponent / row_sum).astype(bf16)
    context = jnp.einsum("hrk,khe->rhe", attn_probs, value_rows, preferred_element_type=f32)
    return (flat_heads(context), (row_max + jnp.log(row_sum))[..., 0])


def attend_backward(packed):
    allowed = packed[5]
    query_rows = pair_heads(packed[0])
    key_rows = pair_heads(packed[1])
    value_rows = pair_heads(packed[2])
    grad_rows = pair_heads(packed[3])
    log_total = packed[4]
    scores = (
        jnp.einsum("rhe,khe->hrk", query_rows, key_rows, preferred_element_type=f32) * score_scale
    )
    scores = jnp.where(allowed[None], scores, masked_fill)
    attn_probs = jnp.exp(scores - log_total[..., None])
    grad_probs = jnp.einsum("rhe,khe->hrk", grad_rows, value_rows, preferred_element_type=f32)
    grad_values = jnp.einsum(
        "hrk,rhe->khe", attn_probs.astype(bf16), grad_rows, preferred_element_type=f32
    )
    inner_sum = jnp.sum(attn_probs * grad_probs, axis=-1, keepdims=True)
    grad_scores = (attn_probs * (grad_probs - inner_sum)).astype(bf16)
    grad_queries = (
        jnp.einsum("hrk,khe->rhe", grad_scores, key_rows, preferred_element_type=f32) * score_scale
    )
    grad_keys = (
        jnp.einsum("hrk,rhe->khe", grad_scores, query_rows, preferred_element_type=f32)
        * score_scale
    )
    return (flat_heads(grad_queries), flat_heads(grad_keys), flat_heads(grad_values))


def shards(
    tokens,
    cotangent,
    seg_ids,
    parents,
    valid_mask,
    ln1_gain,
    ln1_bias,
    w_qkv,
    qkv_bias,
    w_out,
    ln2_gain,
    ln2_bias,
    w_gate_up,
    w_down,
):
    own_rows, model_width = tokens.shape
    tp_index = lax.axis_index(TP)
    quarter = lax.axis_index(MID) * 2 + lax.axis_index(NEAR)
    local_width = w_qkv.shape[2]
    width = local_width // 4
    units = w_down.shape[1] // 4

    own_ints = jnp.concatenate([seg_ids, valid_mask, parents[0]])
    plane_ints = plane_trees(own_ints)
    group_rows = seg_ids.shape[0]

    def halves(values):
        parts = values.reshape(4, 2, own_rows)
        return jnp.where(tp_index == 0, parts, parts[:, ::-1]).reshape(4, group_rows)

    plane_segs = halves(plane_ints[:, :group_rows])
    plane_valid = halves(plane_ints[:, group_rows : 2 * group_rows])
    plane_parents = plane_ints[:, 2 * group_rows :]
    row_ids = (jnp.arange(group_rows, dtype=jnp.int32) + tp_index * own_rows) % group_rows
    allowed, positions = jax.vmap(tree_mask, in_axes=(0, 0, 0, None))(
        plane_segs, plane_parents, plane_valid, row_ids
    )
    cosine, sine = rotary_tables(from_trees(positions[..., None])[:, 0], ROT)
    keep_rows = from_trees(plane_valid.astype(f32)[..., None])
    own_valid = keep_rows[:own_rows]

    attn_spread = spread_columns([w_qkv[:, 0], w_qkv[:, 1], w_qkv[:, 2], w_out])
    attn_full = gather_far(attn_spread)
    mlp_spread = spread_columns([w_gate_up[:, 0], w_gate_up[:, 1], w_down])
    mlp_full = gather_far(mlp_spread)
    qkv_full = attn_full[:, : 3 * width]
    out_full = attn_full[:, 3 * width :]
    gate_up_full = mlp_full[:, : 2 * units]
    down_full = mlp_full[:, 2 * units :]

    stream = tokens.astype(f32)
    normed1, norm_hat1, inv_std1 = layer_norm(stream, ln1_gain, ln1_bias)
    spread1 = gather_rows(normed1.astype(bf16))
    own_bias = lax.dynamic_slice(qkv_bias, (0, quarter * width), (3, width))
    linear = jnp.dot(spread1, qkv_full, preferred_element_type=f32) + own_bias.reshape(1, -1)
    queries = flat_heads(rotate(pair_heads(linear[:, :width]), cosine, sine)).astype(bf16)
    keys_all = flat_heads(rotate(pair_heads(linear[:, width : 2 * width]), cosine, sine)).astype(
        bf16
    )
    values_all = linear[:, 2 * width :].astype(bf16)
    trees = (by_trees(queries), by_trees(keys_all), by_trees(values_all))
    context_trees, log_totals = lax.map(attend_forward, trees + (allowed,))
    context = (from_trees(context_trees) * keep_rows).astype(bf16)
    attn_partial = jnp.einsum("rf,df->rd", context, out_full, preferred_element_type=f32)
    attn_out = scatter_rows(attn_partial.astype(bf16))
    residual = stream + attn_out

    normed2, norm_hat2, inv_std2 = layer_norm(residual, ln2_gain, ln2_bias)
    cot_full = gather_rows(cotangent)
    spread2 = gather_rows(normed2.astype(bf16))
    gate_up = jnp.dot(spread2, gate_up_full, preferred_element_type=f32)
    gate_part = gate_up[:, :units]
    up_part = gate_up[:, units:]
    sigmoid_gate = jax.nn.sigmoid(gate_part)
    activated = gate_part * sigmoid_gate
    hidden = (activated * up_part).astype(bf16)
    mlp_partial = jnp.einsum("rf,df->rd", hidden, down_full, preferred_element_type=f32)
    mlp_out = scatter_rows(mlp_partial.astype(bf16))
    stream_out = residual + mlp_out
    output = stream_out.astype(bf16)

    d_hidden = jnp.dot(cot_full, down_full, preferred_element_type=f32)
    d_gate = d_hidden * up_part * sigmoid_gate * (1.0 + gate_part * (1.0 - sigmoid_gate))
    d_up = d_hidden * activated
    d_gate_up = jnp.concatenate([d_gate, d_up], axis=1).astype(bf16)
    d_normed2 = scatter_rows(
        jnp.einsum("rf,df->rd", d_gate_up, gate_up_full, preferred_element_type=f32).astype(bf16)
    )
    down_term = jnp.einsum("rd,rf->df", cot_full, hidden, preferred_element_type=f32)
    gate_up_term = jnp.einsum("rd,rf->df", spread2, d_gate_up, preferred_element_type=f32)
    mlp_grads = return_columns(
        scatter_far(
            jnp.concatenate([gate_up_term.astype(bf16), down_term.astype(bf16)], axis=1)
        ),
        3,
    )
    gate_up_grad = jnp.stack(mlp_grads[:2], axis=1)
    down_grad = mlp_grads[2]

    d_resid_norm, gain_two_grad, bias_two_grad = norm_back(d_normed2, norm_hat2, inv_std2, ln2_gain)
    d_residual = cotangent.astype(f32) + d_resid_norm
    spread_grad = gather_rows(d_residual.astype(bf16))
    out_term = jnp.einsum("rd,rf->df", spread_grad, context, preferred_element_type=f32)
    d_context = (
        jnp.dot(spread_grad, out_full, preferred_element_type=f32) * keep_rows
    ).astype(bf16)
    grad_trees = lax.map(
        attend_backward, trees + (by_trees(d_context), log_totals, allowed)
    )
    d_queries = flat_heads(rotate(pair_heads(from_trees(grad_trees[0])), cosine, -sine))
    d_keys = flat_heads(rotate(pair_heads(from_trees(grad_trees[1])), cosine, -sine))
    d_values = from_trees(grad_trees[2])
    d_linear = jnp.concatenate([d_queries, d_keys, d_values], axis=1).astype(bf16)
    d_normed1 = scatter_rows(
        jnp.einsum("rf,df->rd", d_linear, qkv_full, preferred_element_type=f32).astype(bf16)
    )
    qkv_term = jnp.einsum("rd,rf->df", spread1, d_linear, preferred_element_type=f32)
    attn_grads = return_columns(
        scatter_far(jnp.concatenate([qkv_term.astype(bf16), out_term.astype(bf16)], axis=1)), 4
    )
    qkv_grad = jnp.stack(attn_grads[:3], axis=1)
    out_grad = attn_grads[3]
    bias_local = jnp.sum(d_linear.astype(f32), axis=0).reshape(3, width)
    d_stream_norm, gain_one_grad, bias_one_grad = norm_back(
        d_normed1, norm_hat1, inv_std1, ln1_gain
    )
    tokens_grad = d_residual + d_stream_norm

    squares = jnp.stack(
        [
            jnp.sum(own_valid * stream_out * stream_out),
            jnp.sum(own_valid * attn_out * attn_out),
            jnp.sum(own_valid * mlp_out * mlp_out),
            jnp.sum(own_valid),
        ]
    )
    norm_terms = jnp.stack([gain_one_grad, bias_one_grad, gain_two_grad, bias_two_grad])
    bias_spread = lax.dynamic_update_slice(
        jnp.zeros((3, model_width), f32), bias_local, (0, tp_index * local_width + quarter * width)
    )
    norm_sums, bias_sums, square_sums = lax.psum((norm_terms, bias_spread, squares), ALL)
    stream_rms = jnp.sqrt(square_sums[:3] / (square_sums[3] * model_width))
    qkv_bias_grad = lax.dynamic_slice(bias_sums, (0, tp_index * local_width), (3, local_width))
    return (
        output,
        tokens_grad,
        norm_sums[0],
        norm_sums[1],
        qkv_grad,
        qkv_bias_grad,
        out_grad,
        norm_sums[2],
        norm_sums[3],
        gate_up_grad,
        down_grad,
        stream_rms,
    )


def solution(mesh):
    planes = mesh.shape["fsdp"] // 4
    grid = Mesh(mesh.devices.reshape(planes, 2, 2, mesh.shape["tp"]), ALL)
    fsdp = (FAR, MID, NEAR)
    return jax.shard_map(
        shards,
        mesh=grid,
        in_specs=(
            P(ALL, None),
            P(ALL, None),
            P(fsdp),
            P(fsdp, None),
            P(fsdp),
            P(),
            P(),
            P(fsdp, None, TP),
            P(None, TP),
            P(fsdp, TP),
            P(),
            P(),
            P(fsdp, None, TP),
            P(fsdp, TP),
        ),
        out_specs=(
            P(ALL, None),
            P(ALL, None),
            P(),
            P(),
            P(fsdp, None, TP),
            P(None, TP),
            P(fsdp, TP),
            P(),
            P(),
            P(fsdp, None, TP),
            P(fsdp, TP),
            P(),
        ),
        check_vma=False,
    )
```

```python
from functools import partial
import math

import jax
import jax.numpy as jnp
from jax import lax
from jax.experimental import pallas as pl
from jax.experimental.pallas import tpu as pltpu
from jax.sharding import Mesh, PartitionSpec as P

HD = 64
ROT = 16

epsilon = 1e-05
score_scale = 0.125
masked_fill = -1e30

FAR, MID, NEAR, TP = "far", "mid", "near", "tp"
ALL = (FAR, MID, NEAR, TP)
f32 = jnp.float32
bf16 = jnp.bfloat16
LIGHT = pl.CostEstimate(flops=0, bytes_accessed=0, transcendentals=0)


def swap(values, axis):
    return lax.ppermute(values, axis, [(0, 1), (1, 0)])


def place():
    return lax.axis_index(MID) * 2 + lax.axis_index(NEAR)


def swap_diagonal(values):
    return lax.ppermute(values, (MID, NEAR), [(0, 3), (1, 2), (2, 1), (3, 0)])


def after(values, *others):
    return lax.optimization_barrier((values,) + others)[0]


def crossed(pieces):
    other = lax.axis_index(NEAR) == 1
    p = [jnp.where(other, pieces[i ^ 1], pieces[i]) for i in range(4)]
    other = lax.axis_index(MID) == 1
    return [jnp.where(other, p[i ^ 2], p[i]) for i in range(4)]


def exchange(pieces):
    return [pieces[0], swap(pieces[1], NEAR), swap(pieces[2], MID), swap_diagonal(pieces[3])]


def place():
    return lax.axis_index(MID) * 2 + lax.axis_index(NEAR)


def quarter_parts(width):
    tiles, rest = divmod(width // 4, 128)
    return tiles - tiles // 2, tiles // 2, rest


def half_tile(values, odd):
    values = values.astype(f32)
    return jnp.where(odd, pltpu.roll(values, 64, 1), values)


def low_lanes(low, high):
    lane = lax.broadcasted_iota(jnp.int32, (1, 128), 1)
    return jnp.where(lane < 64, low, high)


def pack_heads_kernel(place_ref, stack_ref, last_ref, *piece_refs):
    width = last_ref.shape[1] // 4
    for i, piece_ref in enumerate(piece_refs):
        part = pl.ds(pl.multiple_of((place_ref[0] ^ i) * width, 128), width)
        for kind in range(4):
            piece_ref[:, kind * width : (kind + 1) * width] = (
                stack_ref[:, kind, part] if kind < 3 else last_ref[:, part]
            )


def unpack_heads_kernel(place_ref, *refs):
    piece_refs, stack_ref, last_ref = refs[:4], refs[4], refs[5]
    width = last_ref.shape[1] // 4
    for i, piece_ref in enumerate(piece_refs):
        part = pl.ds(pl.multiple_of((place_ref[0] ^ i) * width, 128), width)
        for kind in range(4):
            piece = piece_ref[:, kind * width : (kind + 1) * width].astype(f32)
            if kind < 3:
                stack_ref[:, kind, part] = piece
            else:
                last_ref[:, part] = piece


def unit_columns(width):
    first, second, rest = quarter_parts(width)
    return first * 128, second * 128, rest, 4 * 128 * (first + second)


def pack_units_kernel(place_ref, stack_ref, last_ref, *piece_refs):
    first, second, rest, rest_start = unit_columns(last_ref.shape[1])

    def read(kind, part):
        return stack_ref[:, kind, part] if kind < 2 else last_ref[:, part]

    for i in range(4):
        chip = place_ref[0] ^ i
        first_ref, second_ref = piece_refs[i], piece_refs[4 + i]
        part = pl.ds(pl.multiple_of(chip * first, 128), first)
        for kind in range(3):
            first_ref[:, kind * first : (kind + 1) * first] = read(kind, part)
        part = pl.ds(pl.multiple_of(4 * first + chip * second, 128), second)
        mixed = 2 * second
        down = mixed + (128 if rest else 0)
        for kind, start in enumerate((0, second, down)):
            second_ref[:, start : start + second] = read(kind, part)
        if rest:
            part = pl.ds(pl.multiple_of(rest_start + (chip // 2) * 128, 128), 128)
            gate, up, last = [half_tile(read(kind, part), chip % 2 == 1) for kind in range(3)]
            second_ref[:, mixed : mixed + 128] = low_lanes(gate, pltpu.roll(up, 64, 1)).astype(bf16)
            second_ref[:, down + second :] = low_lanes(last, 0.0).astype(bf16)


def unpack_units_kernel(place_ref, *refs):
    piece_refs, stack_ref, last_ref = refs[:8], refs[8], refs[9]
    first, second, rest, rest_start = unit_columns(last_ref.shape[1])

    def write(kind, part, values):
        if kind < 2:
            stack_ref[:, kind, part] = values
        else:
            last_ref[:, part] = values

    for i in range(4):
        chip = place_ref[0] ^ i
        first_ref, second_ref = piece_refs[i], piece_refs[4 + i]
        part = pl.ds(pl.multiple_of(chip * first, 128), first)
        for kind in range(3):
            write(kind, part, first_ref[:, kind * first : (kind + 1) * first].astype(f32))
        part = pl.ds(pl.multiple_of(4 * first + chip * second, 128), second)
        mixed = 2 * second
        down = mixed + (128 if rest else 0)
        for kind, start in enumerate((0, second, down)):
            write(kind, part, second_ref[:, start : start + second].astype(f32))
        if rest:
            part = pl.ds(pl.multiple_of(rest_start + (chip // 2) * 128, 128), 128)
            odd = chip % 2 == 1
            lane = lax.broadcasted_iota(jnp.int32, (1, 128), 1)
            mine = (lane >= 64) == odd
            both = second_ref[:, mixed : mixed + 128].astype(f32)
            turned = pltpu.roll(both, 64, 1)
            last = second_ref[:, down + second :].astype(f32)
            last = jnp.where(odd, pltpu.roll(last, 64, 1), last)
            for kind, values in enumerate(
                (jnp.where(odd, turned, both), jnp.where(odd, both, turned), last)
            ):
                held = stack_ref[:, kind, part] if kind < 2 else last_ref[:, part]
                write(kind, part, jnp.where(mine, values, held))


def on_place(kernel, name, operands, outs):
    vmem = pl.BlockSpec(memory_space=pltpu.VMEM)
    return pl.pallas_call(
        kernel,
        in_specs=[pl.BlockSpec(memory_space=pltpu.SMEM)] + [vmem] * len(operands),
        out_specs=[vmem] * len(outs),
        out_shape=[jax.ShapeDtypeStruct(*out) for out in outs],
        compiler_params=pltpu.CompilerParams(vmem_limit_bytes=32 << 20),
        cost_estimate=LIGHT,
        name=name,
    )(place().reshape(1), *operands)


def collected(pieces):
    return jnp.concatenate(crossed(pieces), axis=0)


def spread(pieces):
    return collected(exchange(pieces))


def returned(values):
    rows = values.shape[0] // 4
    return exchange(
        [lax.dynamic_slice_in_dim(values, (place() ^ i) * rows, rows, 0) for i in range(4)]
    )


def gather_begin(own):
    return own, swap(own, NEAR), swap(own, MID)


def gather_end(state):
    own, near, mid = state
    half = own.shape[0] // 2
    diagonal_low = swap(near[:half], MID)
    diagonal_high = swap(mid[half:], NEAR)
    core = jnp.concatenate([own, near, mid, diagonal_low, diagonal_high], axis=0)
    return core, swap(core, TP)


def gather_rows(own):
    return gather_end(gather_begin(own))


def add_low(a, b):
    return (a.astype(f32) + b.astype(f32)).astype(bf16)


def scatter_begin(mine, others):
    return add_low(mine, swap(others, TP))


def scatter_middle(core):
    rows = core.shape[0] // 4
    half = rows // 2
    return swap(core[3 * rows : 3 * rows + half], MID), swap(core[3 * rows + half :], NEAR)


def scatter_end(core, middle):
    rows = core.shape[0] // 4
    half = rows // 2
    own, near, mid = [core[i * rows : (i + 1) * rows] for i in range(3)]
    near = jnp.concatenate([add_low(near[:half], middle[0]), near[half:]], axis=0)
    mid = jnp.concatenate([mid[:half], add_low(mid[half:], middle[1])], axis=0)
    return own, swap(near, NEAR), swap(mid, MID)


def scatter_rest(core):
    return scatter_end(core, scatter_middle(core))


def stage(always, step, *operands):
    shapes = jax.eval_shape(step, *operands)

    def never(*_):
        return jax.tree.map(lambda s: jnp.zeros(s.shape, s.dtype), shapes)

    return lax.cond(always, step, never, *operands)


def gather_far(values):
    return lax.all_gather(values, FAR, axis=0, tiled=True)


def scatter_far(values):
    return lax.psum_scatter(values, FAR, scatter_dimension=0, tiled=True)


def plane_trees(values):
    return jnp.stack(exchange([values] * 4))


def sum_over(values, axes):
    for axis in axes:
        size = lax.axis_size(axis)
        if size & (size - 1):
            values = lax.psum(values, axis)
            continue
        step = 1
        while step < size:
            values = values + lax.ppermute(values, axis, [(i, i ^ step) for i in range(size)])
            step *= 2
    return values


def tree_rows(seg_ids, parents, valid_mask, row_ids):
    labels = jnp.arange(parents.shape[0], dtype=jnp.int32)
    parent_one = jnp.sum(
        jnp.where(seg_ids[:, None] == labels[None, :], parents[None, :], 0), axis=1
    )
    parent_two = jnp.sum(
        jnp.where(parent_one[:, None] == labels[None, :], parents[None, :], 0), axis=1
    )
    key_segs = seg_ids[None, :]
    related = (
        (key_segs == seg_ids[:, None])
        | (key_segs == parent_one[:, None])
        | (key_segs == parent_two[:, None])
    )
    allowed = related & (row_ids[None, :] <= row_ids[:, None]) & (valid_mask[None, :] > 0)
    allowed = allowed | (row_ids[None, :] == row_ids[:, None])
    positions = jnp.sum(allowed.astype(jnp.int32), axis=1) - 1
    return (parent_one, parent_two, positions)


def normalised(values):
    centre = values - jnp.mean(values, axis=-1, keepdims=True)
    inverse = lax.rsqrt(jnp.mean(centre * centre, axis=-1, keepdims=True) + epsilon)
    return centre * inverse, inverse


def norm_kernel(*refs):
    row_ref, part_refs, gain_ref, shift_ref = refs[0], refs[1:-4], refs[-4], refs[-3]
    if len(refs) == 4:
        row_ref, gain_ref, shift_ref, normed_ref = refs
        part_refs = ()
    else:
        normed_ref, added_ref = refs[-2:]
    values = row_ref[...].astype(f32)
    if part_refs:
        added = sum(ref[...].astype(f32) for ref in part_refs)
        added_ref[...] = added
        values = values + added
    normed_ref[...] = (normalised(values)[0] * gain_ref[...] + shift_ref[...]).astype(bf16)


def norm_rows(tokens, parts, gain, shift):
    rows, width = tokens.shape
    block = min(64, rows)
    of_rows = pl.BlockSpec((block, width), lambda i: (i, 0))
    of_gain = pl.BlockSpec((1, width), lambda i: (0, 0))
    kinds = [bf16] + [f32] * bool(parts)
    return pl.pallas_call(
        norm_kernel,
        grid=(rows // block,),
        in_specs=[of_rows] * (1 + len(parts)) + [of_gain] * 2,
        out_specs=[of_rows] * len(kinds),
        out_shape=[jax.ShapeDtypeStruct((rows, width), kind) for kind in kinds],
        cost_estimate=LIGHT,
        name="norm_rows",
    )(tokens, *parts, gain[None], shift[None])


def norm_back_kernel(count, *refs):
    row_refs, part_refs = refs[:count], refs[count : count + 3]
    gain_ref, past_ref, grad_ref, low_ref, sum_ref = refs[count + 3 :]
    normed, inverse = normalised(sum(ref[...].astype(f32) for ref in row_refs))
    grad = sum(ref[...].astype(f32) for ref in part_refs)
    scaled = grad * gain_ref[...]
    centred = (
        scaled
        - jnp.mean(scaled, axis=-1, keepdims=True)
        - normed * jnp.mean(scaled * normed, axis=-1, keepdims=True)
    )
    total = past_ref[...].astype(f32) + inverse * centred
    grad_ref[...] = total
    low_ref[...] = total.astype(bf16)

    @pl.when(pl.program_id(0) == 0)
    def _():
        sum_ref[...] = jnp.zeros_like(sum_ref)

    sum_ref[0:1] += jnp.sum(grad * normed, axis=0, keepdims=True)
    sum_ref[1:2] += jnp.sum(grad, axis=0, keepdims=True)


def norm_back(summands, parts, gain, past):
    rows, width = past.shape
    block = min(64, rows)
    of_rows = pl.BlockSpec((block, width), lambda i: (i, 0))
    of_gain = pl.BlockSpec((1, width), lambda i: (0, 0))
    shape = jax.ShapeDtypeStruct
    return pl.pallas_call(
        partial(norm_back_kernel, len(summands)),
        grid=(rows // block,),
        in_specs=[of_rows] * (len(summands) + 3) + [of_gain, of_rows],
        out_specs=[of_rows, of_rows, pl.BlockSpec((2, width), lambda i: (0, 0))],
        out_shape=[shape((rows, width), f32), shape((rows, width), bf16), shape((2, width), f32)],
        cost_estimate=LIGHT,
        name="norm_back",
    )(*summands, *parts, gain[None], past)


def rope_tables(positions):
    half = ROT // 2
    lane = jnp.arange(2 * HD, dtype=jnp.int32) % HD
    power = (lane % half).astype(f32) * (-2.0 * math.log(10000.0) / ROT)
    inverse_freq = jnp.where(lane < ROT, jnp.exp(power), 0.0)
    angles = positions.astype(f32)[..., None] * inverse_freq
    return jnp.cos(angles), jnp.sin(angles)


def turn(values, cosine, sine):
    half = ROT // 2
    lane = lax.broadcasted_iota(jnp.int32, (1, 2 * HD), 1) % HD
    ahead = pltpu.roll(values, 2 * HD - half, 1)
    behind = pltpu.roll(values, half, 1)
    return values * cosine + jnp.where(lane < half, -ahead, behind) * sine


def allowed_keys(row_ref, col_ref):
    row_seg, parent_one, parent_two, row_id = [row_ref[0, i : i + 1, :] for i in range(4)]
    key_seg = col_ref[0, :, 0:1]
    key_id = col_ref[0, :, 1:2]
    related = (key_seg == row_seg) | (key_seg == parent_one) | (key_seg == parent_two)
    return (related & (key_id <= row_id)) | (key_id == row_id)


def dot_nt(a, b):
    return lax.dot_general(a, b, (((1,), (1,)), ((), ())), preferred_element_type=f32)


def dot_nn(a, b):
    return jnp.dot(a, b, preferred_element_type=f32)


def head_lanes(head):
    lane = lax.broadcasted_iota(jnp.int32, (1, 2 * HD), 1)
    return lane < HD if head == 0 else lane >= HD


def forward_kernel(
    core_ref, other_ref, weight_ref, bias_ref, row_ref, col_ref, keep_ref, cos_ref, sin_ref,
    qkv_ref, context_ref, log_ref, core_out_ref, other_out_ref, linear,
):
    half = core_ref.shape[0]
    width = context_ref.shape[3]
    linear[:half] = dot_nn(core_ref[...], weight_ref[:, : 3 * width]) + bias_ref[...]
    linear[half:] = dot_nn(other_ref[...], weight_ref[:, : 3 * width]) + bias_ref[...]
    mask = allowed_keys(row_ref, col_ref)
    cosine, sine = cos_ref[0], sin_ref[0]
    for pair in range(width // (2 * HD)):
        at = pair * 2 * HD
        lanes = slice(at, at + 2 * HD)
        query = turn(linear[:, lanes], cosine, sine).astype(bf16)
        key = turn(linear[:, width + at : width + at + 2 * HD], cosine, sine).astype(bf16)
        value = linear[:, 2 * width + at : 2 * width + at + 2 * HD]
        value_t = value.T.astype(bf16)
        value = value.astype(bf16)
        for core in range(2):
            rows = slice(core * half, (core + 1) * half)
            qkv_ref[core, 0, :, lanes] = query[rows]
            qkv_ref[core, 0, :, width + at : width + at + 2 * HD] = key[rows]
            qkv_ref[core, 0, :, 2 * width + at : 2 * width + at + 2 * HD] = value[rows]
        context_t = []
        for head in range(2):
            mine = jnp.where(head_lanes(head), query, jnp.zeros_like(query))
            scores = jnp.where(mask, dot_nt(key, mine) * score_scale, masked_fill)
            row_max = jnp.max(scores, axis=0, keepdims=True)
            exponent = jnp.exp(scores - row_max)
            row_sum = jnp.sum(exponent, axis=0, keepdims=True)
            log_ref[0, 2 * pair + head : 2 * pair + head + 1, :] = row_max + jnp.log(row_sum)
            context_t.append(
                dot_nn(value_t[head * HD : (head + 1) * HD], exponent.astype(bf16)) / row_sum
            )
        context = (jnp.concatenate(context_t, axis=0).T * keep_ref[0]).astype(bf16)
        for core in range(2):
            context_ref[core, 0, :, lanes] = context[core * half : (core + 1) * half]
    for core, out_ref in enumerate((core_out_ref, other_out_ref)):
        out_ref[...] = dot_nt(context_ref[core, 0], weight_ref[:, 3 * width :]).astype(bf16)


def backward_kernel(
    core_ref, other_ref, weight_ref, qkv_ref, row_ref, col_ref, keep_ref, cos_ref, sin_ref, log_ref,
    grad_ref, bias_ref, core_out_ref, other_out_ref, grads,
):
    half = core_ref.shape[0]
    width = weight_ref.shape[1] // 4
    grads[:half] = dot_nn(core_ref[...], weight_ref[:, 3 * width :])
    grads[half:] = dot_nn(other_ref[...], weight_ref[:, 3 * width :])
    mask = allowed_keys(row_ref, col_ref)
    cosine, sine = cos_ref[0], sin_ref[0]

    def both(at):
        return jnp.concatenate([qkv_ref[core, 0, :, at : at + 2 * HD] for core in range(2)], axis=0)

    for pair in range(width // (2 * HD)):
        at = pair * 2 * HD
        query, key, value = both(at), both(width + at), both(2 * width + at)
        key_t = key.astype(f32).T.astype(bf16)
        d_context = (grads[:, at : at + 2 * HD] * keep_ref[0]).astype(bf16)
        d_query_t = []
        d_key = jnp.zeros(query.shape, f32)
        d_value = jnp.zeros(query.shape, f32)
        for head in range(2):
            lanes = head_lanes(head)
            my_query = jnp.where(lanes, query, jnp.zeros_like(query))
            my_grad = jnp.where(lanes, d_context, jnp.zeros_like(d_context))
            log_total = log_ref[0, 2 * pair + head : 2 * pair + head + 1, :]
            scores = jnp.where(mask, dot_nt(key, my_query) * score_scale, masked_fill)
            probs = jnp.exp(scores - log_total)
            d_probs = dot_nt(value, my_grad)
            d_value = d_value + dot_nn(probs.astype(bf16), my_grad)
            inner = jnp.sum(probs * d_probs, axis=0, keepdims=True)
            d_scores = (probs * (d_probs - inner)).astype(bf16)
            d_key = d_key + dot_nn(d_scores, my_query)
            d_query_t.append(dot_nn(key_t[head * HD : (head + 1) * HD], d_scores))
        d_query = jnp.concatenate(d_query_t, axis=0).T * score_scale
        pieces = (
            turn(d_query, cosine, -sine).astype(bf16),
            turn(d_key * score_scale, cosine, -sine).astype(bf16),
            d_value.astype(bf16),
        )
        for kind, piece in enumerate(pieces):
            start = kind * width + at
            for core in range(2):
                grad_ref[core, 0, :, start : start + 2 * HD] = piece[core * half : (core + 1) * half]
            bias_ref[0, :, start : start + 2 * HD] = jnp.sum(
                piece.astype(f32), axis=0, keepdims=True
            )
    for core, out_ref in enumerate((core_out_ref, other_out_ref)):
        out_ref[...] = dot_nt(grad_ref[core, 0], weight_ref[:, : 3 * width]).astype(bf16)


def tree_block(*shape):
    return pl.BlockSpec((1,) + shape, lambda t: (t,) + (0,) * len(shape))


def row_block(rows, columns):
    return pl.BlockSpec((rows, columns), lambda t: (t, 0))


def core_block(rows, columns):
    return pl.BlockSpec((2, 1, rows, columns), lambda t: (0, t, 0, 0))


def whole_block(*shape):
    return pl.BlockSpec(shape, lambda t: (0,) * len(shape), pipeline_mode=pl.Buffered(1))


def attention_forward(cores, weights, bias, tree_info):
    row_info, col_info, keep, cosine, sine = tree_info
    model_width = weights.shape[0]
    width = weights.shape[1] // 4
    rows = cores[0].shape[0] // 4
    group = 2 * rows
    heads = width // HD
    shape = jax.ShapeDtypeStruct
    return pl.pallas_call(
        forward_kernel,
        grid=(4,),
        in_specs=[
            row_block(rows, model_width),
            row_block(rows, model_width),
            whole_block(*weights.shape),
            whole_block(1, 3 * width),
            tree_block(*row_info.shape[1:]),
            tree_block(*col_info.shape[1:]),
            tree_block(*keep.shape[1:]),
            tree_block(*cosine.shape[1:]),
            tree_block(*sine.shape[1:]),
        ],
        out_specs=[
            core_block(rows, 3 * width),
            core_block(rows, width),
            tree_block(heads, group),
            row_block(rows, model_width),
            row_block(rows, model_width),
        ],
        out_shape=[
            shape((2, 4, rows, 3 * width), bf16),
            shape((2, 4, rows, width), bf16),
            shape((4, heads, group), f32),
            shape((4 * rows, model_width), bf16),
            shape((4 * rows, model_width), bf16),
        ],
        scratch_shapes=[pltpu.VMEM((group, 3 * width), f32)],
        compiler_params=pltpu.CompilerParams(vmem_limit_bytes=48 << 20),
        cost_estimate=pl.CostEstimate(
            flops=16 * group * model_width * width * 2, bytes_accessed=32 << 20, transcendentals=4 << 20
        ),
        name="attention_forward",
    )(
        *cores,
        weights,
        bias,
        row_info,
        col_info,
        keep,
        cosine,
        sine,
    )


def attention_backward(cores, weights, qkv, log_totals, tree_info):
    row_info, col_info, keep, cosine, sine = tree_info
    model_width = weights.shape[0]
    width = weights.shape[1] // 4
    rows = cores[0].shape[0] // 4
    group = 2 * rows
    heads = width // HD
    shape = jax.ShapeDtypeStruct
    return pl.pallas_call(
        backward_kernel,
        grid=(4,),
        in_specs=[
            row_block(rows, model_width),
            row_block(rows, model_width),
            whole_block(*weights.shape),
            core_block(rows, 3 * width),
            tree_block(*row_info.shape[1:]),
            tree_block(*col_info.shape[1:]),
            tree_block(*keep.shape[1:]),
            tree_block(*cosine.shape[1:]),
            tree_block(*sine.shape[1:]),
            tree_block(heads, group),
        ],
        out_specs=[
            core_block(rows, 3 * width),
            tree_block(1, 3 * width),
            row_block(rows, model_width),
            row_block(rows, model_width),
        ],
        out_shape=[
            shape((2, 4, rows, 3 * width), bf16),
            shape((4, 1, 3 * width), f32),
            shape((4 * rows, model_width), bf16),
            shape((4 * rows, model_width), bf16),
        ],
        scratch_shapes=[pltpu.VMEM((group, width), f32)],
        compiler_params=pltpu.CompilerParams(vmem_limit_bytes=48 << 20),
        cost_estimate=pl.CostEstimate(
            flops=16 * group * model_width * width * 2, bytes_accessed=32 << 20, transcendentals=4 << 20
        ),
        name="attention_backward",
    )(
        *cores,
        weights,
        qkv,
        row_info,
        col_info,
        keep,
        cosine,
        sine,
        log_totals,
    )


def units_kernel(parts, *refs):
    main, mixed = parts
    count = 7 if len(refs) == 11 else 5
    x_refs, dy_refs, weight_ref = refs[0:2], refs[2:4], refs[4]
    before_refs = refs[5:count]
    grad_ref, hidden_ref = refs[count : count + 2]
    out_refs = refs[count + 2 :]
    wide = 2 * main + mixed
    for core in range(2):
        gate_up = dot_nn(x_refs[core][...], weight_ref[:, :wide])
        d_hidden = dot_nn(dy_refs[core][...], weight_ref[:, wide:])

        def unit(gate, up, grad):
            sigmoid = jax.nn.sigmoid(gate)
            active = gate * sigmoid
            d_gate = grad * up * sigmoid * (1.0 + gate * (1.0 - sigmoid))
            return active * up, d_gate, grad * active

        hidden, d_gate, d_up = unit(
            gate_up[:, :main], gate_up[:, main : 2 * main], d_hidden[:, :main]
        )
        hidden_ref[core, 0, :, :main] = hidden.astype(bf16)
        grad_ref[core, 0, :, :main] = d_gate.astype(bf16)
        grad_ref[core, 0, :, main : 2 * main] = d_up.astype(bf16)
        if mixed:
            both = gate_up[:, 2 * main :]
            hidden, d_gate, d_up = unit(both, pltpu.roll(both, 64, 1), d_hidden[:, main:])
            hidden_ref[core, 0, :, main:] = low_lanes(hidden, 0.0).astype(bf16)
            grad_ref[core, 0, :, 2 * main :] = low_lanes(d_gate, pltpu.roll(d_up, 64, 1)).astype(bf16)
        total = dot_nt(grad_ref[core, 0], weight_ref[:, :wide])
        if before_refs:
            total = total + before_refs[core][...].astype(f32)
        out_refs[core][...] = total.astype(bf16)


def hidden_units(xs, dys, weights, parts, before=()):
    model_width = weights.shape[0]
    main, mixed = parts
    wide = 2 * main + mixed
    rows = xs[0].shape[0] // 4
    shape = jax.ShapeDtypeStruct
    rows_of = row_block(rows, model_width)
    return pl.pallas_call(
        partial(units_kernel, parts),
        grid=(4,),
        in_specs=[rows_of] * 4 + [whole_block(*weights.shape)] + [rows_of] * len(before),
        out_specs=[core_block(rows, wide), core_block(rows, main + mixed), rows_of, rows_of],
        out_shape=[
            shape((2, 4, rows, wide), bf16),
            shape((2, 4, rows, main + mixed), bf16),
            shape((4 * rows, model_width), bf16),
            shape((4 * rows, model_width), bf16),
        ],
        compiler_params=pltpu.CompilerParams(vmem_limit_bytes=56 << 20),
        cost_estimate=pl.CostEstimate(
            flops=16 * rows * model_width * 5 * main, bytes_accessed=32 << 20, transcendentals=1 << 20
        ),
        name="hidden_units",
    )(*xs, *dys, weights, *before)


def dot_tn(a, b):
    return lax.dot_general(a, b, (((0,), (0,)), ((), ())), preferred_element_type=f32)


def weight_kernel(*refs):
    left_refs, right_refs, out_ref = (refs[0:2], refs[2:4]), refs[4:6], refs[6]
    start = 0
    for lefts, right_ref in zip(left_refs, right_refs):
        columns = right_ref.shape[-1]
        total = 0.0
        for core in range(2):
            total = total + dot_tn(lefts[core][...], right_ref[core].reshape(-1, columns))
        out_ref[:, start : start + columns] = total.astype(bf16)
        start += columns


def weight_terms(lefts, rights):
    rows, model_width = lefts[0][0].shape
    block = 256
    total = sum(right.shape[-1] for right in rights)
    left_block = pl.BlockSpec((rows, block), lambda i: (0, i))
    return pl.pallas_call(
        weight_kernel,
        grid=(model_width // block,),
        in_specs=[left_block] * 4 + [whole_block(*right.shape) for right in rights],
        out_specs=pl.BlockSpec((block, total), lambda i: (i, 0)),
        out_shape=jax.ShapeDtypeStruct((model_width, total), bf16),
        compiler_params=pltpu.CompilerParams(vmem_limit_bytes=48 << 20),
        cost_estimate=pl.CostEstimate(
            flops=4 * rows * model_width * total, bytes_accessed=32 << 20, transcendentals=0
        ),
        name="weight_terms",
    )(*lefts[0], *lefts[1], *rights)


def out_kernel(first_ref, second_ref, first_weight_ref, second_weight_ref, *out_refs):
    down = [first_ref.shape[-1], second_ref.shape[-1]]
    for core, out_ref in enumerate(out_refs):
        total = dot_nt(first_ref[core, 0], first_weight_ref[:, -down[0] :])
        total = total + dot_nt(second_ref[core, 0], second_weight_ref[:, -down[1] :])
        out_ref[...] = total.astype(bf16)


def units_out(hiddens, weights):
    rows = hiddens[0].shape[2]
    model_width = weights[0].shape[0]
    return pl.pallas_call(
        out_kernel,
        grid=(4,),
        in_specs=[core_block(rows, hidden.shape[-1]) for hidden in hiddens]
        + [whole_block(*weight.shape) for weight in weights],
        out_specs=[row_block(rows, model_width)] * 2,
        out_shape=[jax.ShapeDtypeStruct((4 * rows, model_width), bf16)] * 2,
        compiler_params=pltpu.CompilerParams(vmem_limit_bytes=48 << 20),
        cost_estimate=pl.CostEstimate(
            flops=16 * rows * model_width * sum(hidden.shape[-1] for hidden in hiddens),
            bytes_accessed=24 << 20,
            transcendentals=0,
        ),
        name="units_out",
    )(*hiddens, *weights)


def shards(
    tokens,
    cotangent,
    seg_ids,
    parents,
    valid_mask,
    ln1_gain,
    ln1_bias,
    w_qkv,
    qkv_bias,
    w_out,
    ln2_gain,
    ln2_bias,
    w_gate_up,
    w_down,
):
    own_rows, model_width = tokens.shape
    group_rows = seg_ids.shape[0]
    tp_index = lax.axis_index(TP)
    quarter = place()
    local_width = w_qkv.shape[2]
    width = local_width // 4
    weight_rows, local_units = w_down.shape
    main_a, main_b, rest, _ = unit_columns(local_units)
    mixed = 128 if rest else 0
    always = valid_mask[0] >= 0

    pieces = on_place(
        pack_heads_kernel, "pack_heads", (w_qkv, w_out), [((weight_rows, 4 * width), bf16)] * 4
    )
    attn_pieces = exchange(pieces)
    (normed1,) = norm_rows(tokens, (), ln1_gain, ln1_bias)
    unit_pieces = on_place(
        pack_units_kernel,
        "pack_units",
        (w_gate_up, w_down),
        [((weight_rows, 3 * main_a), bf16)] * 4
        + [((weight_rows, 3 * main_b + 2 * mixed), bf16)] * 4,
    )
    attn_pieces, normed1, unit_pieces = lax.optimization_barrier(
        (attn_pieces, normed1, unit_pieces)
    )
    attn_spread = collected(attn_pieces)
    attn_full = gather_far(attn_spread)

    def prepare(attn_spread, normed1, unit_pieces, cotangent, seg_ids, valid_mask, parents):
        spread1 = gather_rows(normed1)
        spread_a, spread_b = spread(unit_pieces[:4]), spread(unit_pieces[4:])
        cotangent, _, _ = lax.optimization_barrier((cotangent, spread1[0], spread_b))
        dy_state = gather_begin(cotangent)

        ints = jnp.concatenate([seg_ids, valid_mask, parents[0]])
        plane_ints = plane_trees(ints)

        def halves(values):
            parts = values.reshape(4, 2, own_rows)
            return jnp.where(tp_index == 0, parts, parts[:, ::-1]).reshape(4, group_rows)

        plane_segs = halves(plane_ints[:, :group_rows])
        plane_valid = halves(plane_ints[:, group_rows : 2 * group_rows])
        plane_parents = plane_ints[:, 2 * group_rows :]
        row_ids = (jnp.arange(group_rows, dtype=jnp.int32) + tp_index * own_rows) % group_rows
        parent_one, parent_two, positions = jax.vmap(tree_rows, in_axes=(0, 0, 0, None))(
            plane_segs, plane_parents, plane_valid, row_ids
        )
        all_ids = jnp.broadcast_to(row_ids, plane_segs.shape)
        row_info = jnp.stack([plane_segs, parent_one, parent_two, all_ids], axis=1)
        col_info = jnp.stack([jnp.where(plane_valid > 0, plane_segs, -1), all_ids], axis=2)
        keep = plane_valid.astype(f32)[..., None]
        tree_info = (row_info, col_info, keep, *rope_tables(positions))
        return spread1, spread_a, spread_b, dy_state[1:], tree_info

    spread1, spread_a, spread_b, dy_near, tree_info = stage(
        always, prepare, attn_spread, normed1, unit_pieces, cotangent, seg_ids, valid_mask, parents
    )
    own_valid = tree_info[2][0, :own_rows]
    units_a = gather_far(spread_a)
    units_b = gather_far(spread_b)

    def attend(spread1, attn_full, tree_info, tokens, cotangent, dy_near):
        own_bias = lax.dynamic_slice(qkv_bias, (0, quarter * width), (3, width))
        qkv, context, log_totals, *attn_partial = attention_forward(
            spread1, attn_full, own_bias.reshape(1, -1), tree_info
        )
        spread_dy = gather_end((cotangent, *dy_near))
        core = after(scatter_begin(*attn_partial), spread_dy[0])
        normed2, attn_out = norm_rows(tokens, scatter_rest(core), ln2_gain, ln2_bias)
        return qkv, context, log_totals, attn_out, gather_rows(normed2), spread_dy

    qkv, context, log_totals, attn_out, spread2, spread_dy = stage(
        always, attend, spread1, attn_full, tree_info, tokens, cotangent, dy_near
    )

    d_units_a, hidden_a, *d_normed2 = hidden_units(spread2, spread_dy, units_a, (main_a, 0))
    terms_a = weight_terms((spread2, spread_dy), (d_units_a, hidden_a))
    grads_a = scatter_far(terms_a)

    def finish_units(terms_a, spread2, spread_dy, units_a, units_b, d_normed2, hidden_a, attn_out, tokens, cotangent):
        d_units_b, hidden_b, *d_normed2 = hidden_units(
            spread2, spread_dy, units_b, (main_b, mixed), d_normed2
        )
        core = scatter_begin(*d_normed2)
        d_units_b, hidden_b, core = lax.optimization_barrier((d_units_b, hidden_b, core))
        middle = scatter_middle(core)
        mlp_partial = units_out((hidden_a, hidden_b), (units_a, units_b))
        middle, mlp_partial = lax.optimization_barrier((middle, mlp_partial))
        parts = scatter_end(core, middle)
        terms_b = weight_terms((spread2, spread_dy), (d_units_b, hidden_b))
        mlp_core = scatter_begin(*mlp_partial)
        parts, terms_b = lax.optimization_barrier((parts, terms_b))
        d_residual, d_low, norm2_grads = norm_back((tokens, attn_out), parts, ln2_gain, cotangent)
        return mlp_core, terms_b, d_residual, d_low, norm2_grads

    mlp_core, terms_b, d_residual, d_low, norm2_grads = stage(
        always, finish_units, terms_a, spread2, spread_dy, units_a, units_b, d_normed2, hidden_a, attn_out, tokens, cotangent
    )
    grads_a, d_low = lax.optimization_barrier((grads_a, d_low))
    grads_b = scatter_far(terms_b)

    def attend_back(terms_b, d_low, attn_full, qkv, log_totals, tree_info, spread1, context, mlp_core, grads_a):
        spread_grad = gather_rows(d_low)
        mlp_core, grads_a, spread_grad = lax.optimization_barrier((mlp_core, grads_a, spread_grad))
        mlp_middle = scatter_middle(mlp_core)
        pieces_a = returned(grads_a)
        d_linear, bias_terms, *d_normed1 = attention_backward(
            spread_grad, attn_full, qkv, log_totals, tree_info
        )
        mlp_middle, pieces_a, d_linear, d_normed1 = lax.optimization_barrier(
            (mlp_middle, pieces_a, d_linear, d_normed1)
        )
        mlp_parts = scatter_end(mlp_core, mlp_middle)
        core = scatter_begin(*d_normed1)
        terms = weight_terms((spread1, spread_grad), (d_linear, context))
        return terms, bias_terms, core, mlp_parts, pieces_a

    attn_terms, bias_terms, d_normed1_core, mlp_parts, pieces_a = stage(
        always, attend_back, terms_b, d_low, attn_full, qkv, log_totals, tree_info, spread1, context, mlp_core, grads_a
    )
    grads_b, d_normed1_core = lax.optimization_barrier((grads_b, d_normed1_core))
    attn_grads = scatter_far(attn_terms)

    def finish(attn_terms, core, mlp_parts, pieces_a, grads_b, d_residual, attn_out, tokens, bias_terms, norm2_grads, own_valid):
        tokens_grad, _, norm1_grads = norm_back(
            (tokens,), scatter_rest(core), ln1_gain, d_residual
        )
        mlp_out = sum(part.astype(f32) for part in mlp_parts)
        stream_out = tokens.astype(f32) + attn_out + mlp_out
        output = stream_out.astype(bf16)
        gate_up_grad, down_grad = on_place(
            unpack_units_kernel,
            "unpack_units",
            (*pieces_a, *returned(grads_b)),
            [(w_gate_up.shape, f32), (w_down.shape, f32)],
        )

        squares = jnp.stack(
            [
                jnp.sum(own_valid * stream_out * stream_out),
                jnp.sum(own_valid * attn_out * attn_out),
                jnp.sum(own_valid * mlp_out * mlp_out),
                jnp.sum(own_valid),
            ]
        )
        bias_spread = lax.dynamic_update_slice(
            jnp.zeros((3, model_width), f32),
            jnp.sum(bias_terms, axis=0).reshape(3, width),
            (0, tp_index * local_width + quarter * width),
        )
        sums = jnp.concatenate(
            [norm1_grads, norm2_grads, bias_spread, jnp.pad(squares, (0, model_width - 4))[None]]
        )
        return output, tokens_grad, gate_up_grad, down_grad, sums

    output, tokens_grad, gate_up_grad, down_grad, sums = stage(
        always, finish, attn_terms, d_normed1_core, mlp_parts, pieces_a, grads_b, d_residual, attn_out, tokens, bias_terms, norm2_grads, own_valid
    )
    sums = sum_over(sums, (TP, NEAR, MID))
    attn_grads, sums = lax.optimization_barrier((attn_grads, sums))
    sums = sum_over(sums, (FAR,))
    qkv_grad, out_grad = on_place(
        unpack_heads_kernel,
        "unpack_heads",
        returned(attn_grads),
        [(w_qkv.shape, f32), (w_out.shape, f32)],
    )
    norm_sums, bias_sums, square_sums = sums[:4], sums[4:7], sums[7]
    stream_rms = jnp.sqrt(square_sums[:3] / (square_sums[3] * model_width))
    qkv_bias_grad = lax.dynamic_slice(bias_sums, (0, tp_index * local_width), (3, local_width))
    return (
        output,
        tokens_grad,
        norm_sums[0],
        norm_sums[1],
        qkv_grad,
        qkv_bias_grad,
        out_grad,
        norm_sums[2],
        norm_sums[3],
        gate_up_grad,
        down_grad,
        stream_rms,
    )


def solution(mesh):
    planes = mesh.shape["fsdp"] // 4
    grid = Mesh(mesh.devices.reshape(planes, 2, 2, mesh.shape["tp"]), ALL)
    fsdp = (FAR, MID, NEAR)
    return jax.shard_map(
        shards,
        mesh=grid,
        in_specs=(
            P(ALL, None),
            P(ALL, None),
            P(fsdp),
            P(fsdp, None),
            P(fsdp),
            P(),
            P(),
            P(fsdp, None, TP),
            P(None, TP),
            P(fsdp, TP),
            P(),
            P(),
            P(fsdp, None, TP),
            P(fsdp, TP),
        ),
        out_specs=(
            P(ALL, None),
            P(ALL, None),
            P(),
            P(),
            P(fsdp, None, TP),
            P(None, TP),
            P(fsdp, TP),
            P(),
            P(),
            P(fsdp, None, TP),
            P(fsdp, TP),
            P(),
        ),
        check_vma=False,
    )
```

```python
from functools import partial
import math

import jax
import jax.numpy as jnp
from jax import lax
from jax.experimental import pallas as pl
from jax.experimental.pallas import tpu as pltpu
from jax.sharding import Mesh, PartitionSpec as P

HD = 64
ROT = 16

epsilon = 1e-05
score_scale = 0.125
masked_fill = -1e30

FAR, MID, NEAR, TP = "far", "mid", "near", "tp"
ALL = (FAR, MID, NEAR, TP)
f32 = jnp.float32
bf16 = jnp.bfloat16
LIGHT = pl.CostEstimate(flops=0, bytes_accessed=0, transcendentals=0)


def swap(values, axis):
    return lax.ppermute(values, axis, [(0, 1), (1, 0)])


def place():
    return lax.axis_index(MID) * 2 + lax.axis_index(NEAR)


def swap_diagonal(values):
    return lax.ppermute(values, (MID, NEAR), [(0, 3), (1, 2), (2, 1), (3, 0)])


def after(values, *others):
    return lax.optimization_barrier((values,) + others)[0]


def crossed(pieces):
    other = lax.axis_index(NEAR) == 1
    p = [jnp.where(other, pieces[i ^ 1], pieces[i]) for i in range(4)]
    other = lax.axis_index(MID) == 1
    return [jnp.where(other, p[i ^ 2], p[i]) for i in range(4)]


def exchange(pieces):
    return [pieces[0], swap(pieces[1], NEAR), swap(pieces[2], MID), swap_diagonal(pieces[3])]


def place():
    return lax.axis_index(MID) * 2 + lax.axis_index(NEAR)


def quarter_parts(width):
    tiles, rest = divmod(width // 4, 128)
    return tiles - tiles // 2, tiles // 2, rest


def half_tile(values, odd):
    values = values.astype(f32)
    return jnp.where(odd, pltpu.roll(values, 64, 1), values)


def low_lanes(low, high):
    lane = lax.broadcasted_iota(jnp.int32, (1, 128), 1)
    return jnp.where(lane < 64, low, high)


def pack_heads_kernel(place_ref, stack_ref, last_ref, *piece_refs):
    width = last_ref.shape[1] // 4
    for i, piece_ref in enumerate(piece_refs):
        part = pl.ds(pl.multiple_of((place_ref[0] ^ i) * width, 128), width)
        for kind in range(4):
            piece_ref[:, kind * width : (kind + 1) * width] = (
                stack_ref[kind, :, part] if kind < 3 else last_ref[:, part]
            )


def unpack_heads_kernel(place_ref, *refs):
    piece_refs, stack_ref, last_ref = refs[:4], refs[4], refs[5]
    width = last_ref.shape[1] // 4
    for i, piece_ref in enumerate(piece_refs):
        part = pl.ds(pl.multiple_of((place_ref[0] ^ i) * width, 128), width)
        for kind in range(4):
            piece = piece_ref[:, kind * width : (kind + 1) * width].astype(f32)
            if kind < 3:
                stack_ref[kind, :, part] = piece
            else:
                last_ref[:, part] = piece


def unit_columns(width):
    first, second, rest = quarter_parts(width)
    return first * 128, second * 128, rest, 4 * 128 * (first + second)


def pack_units_kernel(place_ref, stack_ref, last_ref, *piece_refs):
    first, second, rest, rest_start = unit_columns(last_ref.shape[1])

    def read(kind, part):
        return stack_ref[:, kind, part] if kind < 2 else last_ref[:, part]

    for i in range(4):
        chip = place_ref[0] ^ i
        first_ref, second_ref = piece_refs[i], piece_refs[4 + i]
        part = pl.ds(pl.multiple_of(chip * first, 128), first)
        for slot, kind in enumerate((2, 0, 1)):
            first_ref[:, slot * first : (slot + 1) * first] = read(kind, part)
        part = pl.ds(pl.multiple_of(4 * first + chip * second, 128), second)
        gates = second + (128 if rest else 0)
        mixed = gates + 2 * second
        for kind, start in enumerate((gates, gates + second, 0)):
            second_ref[:, start : start + second] = read(kind, part)
        if rest:
            part = pl.ds(pl.multiple_of(rest_start + (chip // 2) * 128, 128), 128)
            gate, up, last = [half_tile(read(kind, part), chip % 2 == 1) for kind in range(3)]
            second_ref[:, mixed : mixed + 128] = low_lanes(gate, pltpu.roll(up, 64, 1)).astype(bf16)
            second_ref[:, second:gates] = low_lanes(last, 0.0).astype(bf16)


def unpack_units_kernel(place_ref, *refs):
    piece_refs, stack_ref, last_ref = refs[:8], refs[8], refs[9]
    first, second, rest, rest_start = unit_columns(last_ref.shape[1])

    def write(kind, part, values):
        if kind < 2:
            stack_ref[:, kind, part] = values
        else:
            last_ref[:, part] = values

    for i in range(4):
        chip = place_ref[0] ^ i
        first_ref, second_ref = piece_refs[i], piece_refs[4 + i]
        part = pl.ds(pl.multiple_of(chip * first, 128), first)
        for slot, kind in enumerate((2, 0, 1)):
            write(kind, part, first_ref[:, slot * first : (slot + 1) * first].astype(f32))
        part = pl.ds(pl.multiple_of(4 * first + chip * second, 128), second)
        gates = second + (128 if rest else 0)
        mixed = gates + 2 * second
        for kind, start in enumerate((gates, gates + second, 0)):
            write(kind, part, second_ref[:, start : start + second].astype(f32))
        if rest:
            part = pl.ds(pl.multiple_of(rest_start + (chip // 2) * 128, 128), 128)
            odd = chip % 2 == 1
            lane = lax.broadcasted_iota(jnp.int32, (1, 128), 1)
            mine = (lane >= 64) == odd
            both = second_ref[:, mixed : mixed + 128].astype(f32)
            turned = pltpu.roll(both, 64, 1)
            last = second_ref[:, second:gates].astype(f32)
            last = jnp.where(odd, pltpu.roll(last, 64, 1), last)
            for kind, values in enumerate(
                (jnp.where(odd, turned, both), jnp.where(odd, both, turned), last)
            ):
                held = stack_ref[:, kind, part] if kind < 2 else last_ref[:, part]
                write(kind, part, jnp.where(mine, values, held))


def on_place(kernel, name, operands, outs):
    vmem = pl.BlockSpec(memory_space=pltpu.VMEM)
    return pl.pallas_call(
        kernel,
        in_specs=[pl.BlockSpec(memory_space=pltpu.SMEM)] + [vmem] * len(operands),
        out_specs=[vmem] * len(outs),
        out_shape=[jax.ShapeDtypeStruct(*out) for out in outs],
        compiler_params=pltpu.CompilerParams(vmem_limit_bytes=32 << 20),
        cost_estimate=LIGHT,
        name=name,
    )(place().reshape(1), *operands)


def collected(pieces):
    return jnp.concatenate(crossed(pieces), axis=0)


def spread(pieces):
    return collected(exchange(pieces))


def split_kernel(place_ref, values_ref, *piece_refs):
    rows = piece_refs[0].shape[0]
    for i, piece_ref in enumerate(piece_refs):
        start = pl.multiple_of((place_ref[0] ^ i) * rows, rows)
        piece_ref[...] = values_ref[pl.ds(start, rows), :]


def returned(values):
    shape = (values.shape[0] // 4, values.shape[1])
    return exchange(on_place(split_kernel, "split_rows", (values,), [(shape, bf16)] * 4))


def gather_begin(own):
    return own, swap(own, NEAR), swap(own, MID)


def gather_diagonal(state):
    own, near, mid = state
    half = own.shape[0] // 2
    return swap(near[:half], MID), swap(mid[half:], NEAR)


def gather_end(state, diagonal):
    core = jnp.concatenate([*state, *diagonal], axis=0)
    return core, swap(core, TP)


def halves_begin(halves):
    return [swap(half, axis) for axis in (NEAR, MID) for half in halves]


def halves_diagonal(sides):
    return swap(sides[0], MID), swap(sides[3], NEAR)


def joined(pieces):
    rows = jnp.concatenate(pieces, axis=0)
    return rows, swap(rows, TP)


def row_pieces(*pairs):
    return [pair[core] for core in range(2) for pair in pairs]


def gather_rows(own):
    state = gather_begin(own)
    return gather_end(state, gather_diagonal(state))


def add_low(*values):
    return sum(value.astype(f32) for value in values).astype(bf16)


def add_halves(mine, others):
    half = mine.shape[0] // 2
    return add_low(mine[:half], others[:half]), add_low(mine[half:], others[half:])


def scatter_cores(mine, others):
    others = swap(others, TP)
    start = 3 * (mine.shape[0] // 4)
    return others, *add_halves(mine[start:], others[start:])


def scatter_middle(low, high):
    return swap(low, MID), swap(high, NEAR)


def side_sums(mine, others, first, middle):
    half = middle[0].shape[0]
    start = 2 * half * first
    near, mid = slice(start, start + 2 * half), slice(start + 2 * half, start + 4 * half)
    near = add_low(mine[near], others[near], jnp.pad(middle[0], ((0, half), (0, 0))))
    mid = add_low(mine[mid], others[mid], jnp.pad(middle[1], ((half, 0), (0, 0))))
    return near, mid


def scatter_end(mine, others, first, middle):
    near, mid = side_sums(mine, others, first, middle)
    return swap(near, NEAR), swap(mid, MID)


def stage(always, step, *operands):
    shapes = jax.eval_shape(step, *operands)

    def never(*_):
        return jax.tree.map(lambda s: jnp.zeros(s.shape, s.dtype), shapes)

    return lax.cond(always, step, never, *operands)


def gather_far(values):
    return lax.all_gather(values, FAR, axis=0, tiled=True)


def scatter_far(values):
    return lax.psum_scatter(values, FAR, scatter_dimension=0, tiled=True)


def plane_trees(values):
    return jnp.stack(exchange([values] * 4))


def sum_over(values, axes):
    for axis in axes:
        size = lax.axis_size(axis)
        if size & (size - 1):
            values = lax.psum(values, axis)
            continue
        step = 1
        while step < size:
            values = values + lax.ppermute(values, axis, [(i, i ^ step) for i in range(size)])
            step *= 2
    return values


def tree_rows(seg_ids, parents, valid_mask, row_ids):
    labels = jnp.arange(parents.shape[0], dtype=jnp.int32)
    parent_one = jnp.sum(
        jnp.where(seg_ids[:, None] == labels[None, :], parents[None, :], 0), axis=1
    )
    parent_two = jnp.sum(
        jnp.where(parent_one[:, None] == labels[None, :], parents[None, :], 0), axis=1
    )
    key_segs = seg_ids[None, :]
    related = (
        (key_segs == seg_ids[:, None])
        | (key_segs == parent_one[:, None])
        | (key_segs == parent_two[:, None])
    )
    allowed = related & (row_ids[None, :] <= row_ids[:, None]) & (valid_mask[None, :] > 0)
    allowed = allowed | (row_ids[None, :] == row_ids[:, None])
    positions = jnp.sum(allowed.astype(jnp.int32), axis=1) - 1
    return (parent_one, parent_two, positions)


def normalised(values):
    centre = values - jnp.mean(values, axis=-1, keepdims=True)
    inverse = lax.rsqrt(jnp.mean(centre * centre, axis=-1, keepdims=True) + epsilon)
    return centre * inverse, inverse


def write_halves(refs, values):
    whole_ref, low_ref, high_ref = refs
    values = values.astype(bf16)
    whole_ref[...] = values
    half = pl.num_programs(0) // 2

    @pl.when(pl.program_id(0) < half)
    def _():
        low_ref[...] = values

    @pl.when(pl.program_id(0) >= half)
    def _():
        high_ref[...] = values


def halves_specs(block, width, steps):
    half = steps // 2
    return [
        pl.BlockSpec((block, width), lambda i: (i, 0)),
        pl.BlockSpec((block, width), lambda i: (jnp.minimum(i, half - 1), 0)),
        pl.BlockSpec((block, width), lambda i: (jnp.maximum(i - half, 0), 0)),
    ]


def halves_shapes(rows, width):
    return [jax.ShapeDtypeStruct((size, width), bf16) for size in (rows, rows // 2, rows // 2)]


def norm_kernel(*refs):
    row_ref, part_refs, gain_ref, shift_ref = refs[0], refs[1:-4], refs[-4], refs[-3]
    if len(refs) == 4:
        row_ref, gain_ref, shift_ref, normed_ref = refs
        part_refs = ()
    else:
        normed_ref, added_ref = refs[-2:]
    values = row_ref[...].astype(f32)
    if part_refs:
        added = sum(ref[...].astype(f32) for ref in part_refs)
        added_ref[...] = added
        values = values + added
    normed_ref[...] = (normalised(values)[0] * gain_ref[...] + shift_ref[...]).astype(bf16)


def norm_rows(tokens, parts, gain, shift):
    rows, width = tokens.shape
    block = min(64, rows)
    of_rows = pl.BlockSpec((block, width), lambda i: (i, 0))
    of_gain = pl.BlockSpec((1, width), lambda i: (0, 0))
    kinds = [bf16] + [f32] * bool(parts)
    return pl.pallas_call(
        norm_kernel,
        grid=(rows // block,),
        in_specs=[of_rows] * (1 + len(parts)) + [of_gain] * 2,
        out_specs=[of_rows] * len(kinds),
        out_shape=[jax.ShapeDtypeStruct((rows, width), kind) for kind in kinds],
        cost_estimate=LIGHT,
        name="norm_rows",
    )(tokens, *parts, gain[None], shift[None])


def norm_back_kernel(count, *refs):
    row_refs, part_refs = refs[:count], refs[count:-7]
    gain_ref, past_ref, *low_refs, grad_ref, sum_ref = refs[-7:]
    normed, inverse = normalised(sum(ref[...].astype(f32) for ref in row_refs))
    grad = sum(ref[...].astype(f32) for ref in part_refs)
    scaled = grad * gain_ref[...]
    centred = (
        scaled
        - jnp.mean(scaled, axis=-1, keepdims=True)
        - normed * jnp.mean(scaled * normed, axis=-1, keepdims=True)
    )
    total = past_ref[...].astype(f32) + inverse * centred
    grad_ref[...] = total
    write_halves(low_refs, total)

    @pl.when(pl.program_id(0) == 0)
    def _():
        sum_ref[...] = jnp.zeros_like(sum_ref)

    sum_ref[0:1] += jnp.sum(grad * normed, axis=0, keepdims=True)
    sum_ref[1:2] += jnp.sum(grad, axis=0, keepdims=True)


def norm_back(summands, parts, gain, past):
    rows, width = past.shape
    block = min(64, rows // 2)
    of_rows = pl.BlockSpec((block, width), lambda i: (i, 0))
    of_gain = pl.BlockSpec((1, width), lambda i: (0, 0))
    shape = jax.ShapeDtypeStruct
    return pl.pallas_call(
        partial(norm_back_kernel, len(summands)),
        grid=(rows // block,),
        in_specs=[of_rows] * (len(summands) + len(parts)) + [of_gain, of_rows],
        out_specs=halves_specs(block, width, rows // block)
        + [of_rows, pl.BlockSpec((2, width), lambda i: (0, 0))],
        out_shape=halves_shapes(rows, width) + [shape((rows, width), f32), shape((2, width), f32)],
        cost_estimate=LIGHT,
        name="norm_back",
    )(*summands, *parts, gain[None], past)


def rope_tables(positions):
    half = ROT // 2
    lane = jnp.arange(2 * HD, dtype=jnp.int32) % HD
    power = (lane % half).astype(f32) * (-2.0 * math.log(10000.0) / ROT)
    inverse_freq = jnp.where(lane < ROT, jnp.exp(power), 0.0)
    angles = positions.astype(f32)[..., None] * inverse_freq
    return jnp.cos(angles), jnp.sin(angles)


def turn(values, cosine, sine):
    half = ROT // 2
    lane = lax.broadcasted_iota(jnp.int32, (1, 2 * HD), 1) % HD
    ahead = pltpu.roll(values, 2 * HD - half, 1)
    behind = pltpu.roll(values, half, 1)
    return values * cosine + jnp.where(lane < half, -ahead, behind) * sine


def allowed_keys(row_ref, col_ref):
    row_seg, parent_one, parent_two, row_id = [row_ref[0, i : i + 1, :] for i in range(4)]
    key_seg = col_ref[0, :, 0:1]
    key_id = col_ref[0, :, 1:2]
    related = (key_seg == row_seg) | (key_seg == parent_one) | (key_seg == parent_two)
    return (related & (key_id <= row_id)) | (key_id == row_id)


def dot_nt(a, b):
    return lax.dot_general(a, b, (((1,), (1,)), ((), ())), preferred_element_type=f32)


def dot_nn(a, b):
    return jnp.dot(a, b, preferred_element_type=f32)


def head_lanes(head):
    lane = lax.broadcasted_iota(jnp.int32, (1, 2 * HD), 1)
    return lane < HD if head == 0 else lane >= HD


def forward_kernel(
    core_ref, other_ref, weight_ref, bias_ref, row_ref, col_ref, keep_ref, cos_ref, sin_ref,
    qkv_ref, context_ref, log_ref, core_out_ref, other_out_ref, linear,
):
    half = core_ref.shape[0]
    width = context_ref.shape[3]
    linear[:half] = dot_nn(core_ref[...], weight_ref[:, : 3 * width]) + bias_ref[...]
    linear[half:] = dot_nn(other_ref[...], weight_ref[:, : 3 * width]) + bias_ref[...]
    mask = allowed_keys(row_ref, col_ref)
    cosine, sine = cos_ref[0], sin_ref[0]
    for pair in range(width // (2 * HD)):
        at = pair * 2 * HD
        lanes = slice(at, at + 2 * HD)
        query = turn(linear[:, lanes], cosine, sine).astype(bf16)
        key = turn(linear[:, width + at : width + at + 2 * HD], cosine, sine).astype(bf16)
        value = linear[:, 2 * width + at : 2 * width + at + 2 * HD]
        value_t = value.T.astype(bf16)
        value = value.astype(bf16)
        for core in range(2):
            rows = slice(core * half, (core + 1) * half)
            qkv_ref[core, 0, :, lanes] = query[rows]
            qkv_ref[core, 0, :, width + at : width + at + 2 * HD] = key[rows]
            qkv_ref[core, 0, :, 2 * width + at : 2 * width + at + 2 * HD] = value[rows]
        context_t = []
        for head in range(2):
            mine = jnp.where(head_lanes(head), query, jnp.zeros_like(query))
            scores = jnp.where(mask, dot_nt(key, mine) * score_scale, masked_fill)
            row_max = jnp.max(scores, axis=0, keepdims=True)
            exponent = jnp.exp(scores - row_max)
            row_sum = jnp.sum(exponent, axis=0, keepdims=True)
            log_ref[0, 2 * pair + head : 2 * pair + head + 1, :] = row_max + jnp.log(row_sum)
            context_t.append(
                dot_nn(value_t[head * HD : (head + 1) * HD], exponent.astype(bf16)) / row_sum
            )
        context = (jnp.concatenate(context_t, axis=0).T * keep_ref[0]).astype(bf16)
        for core in range(2):
            context_ref[core, 0, :, lanes] = context[core * half : (core + 1) * half]
    for core, out_ref in enumerate((core_out_ref, other_out_ref)):
        out_ref[...] = dot_nt(context_ref[core, 0], weight_ref[:, 3 * width :]).astype(bf16)


def backward_kernel(
    core_ref, other_ref, weight_ref, qkv_ref, row_ref, col_ref, keep_ref, cos_ref, sin_ref, log_ref,
    grad_ref, bias_ref, core_out_ref, other_out_ref, grads,
):
    half = core_ref.shape[0]
    width = weight_ref.shape[1] // 4
    grads[:half] = dot_nn(core_ref[...], weight_ref[:, 3 * width :])
    grads[half:] = dot_nn(other_ref[...], weight_ref[:, 3 * width :])
    mask = allowed_keys(row_ref, col_ref)
    cosine, sine = cos_ref[0], sin_ref[0]

    def both(at):
        return jnp.concatenate([qkv_ref[core, 0, :, at : at + 2 * HD] for core in range(2)], axis=0)

    for pair in range(width // (2 * HD)):
        at = pair * 2 * HD
        query, key, value = both(at), both(width + at), both(2 * width + at)
        key_t = key.astype(f32).T.astype(bf16)
        d_context = (grads[:, at : at + 2 * HD] * keep_ref[0]).astype(bf16)
        d_query_t = []
        d_key = jnp.zeros(query.shape, f32)
        d_value = jnp.zeros(query.shape, f32)
        for head in range(2):
            lanes = head_lanes(head)
            my_query = jnp.where(lanes, query, jnp.zeros_like(query))
            my_grad = jnp.where(lanes, d_context, jnp.zeros_like(d_context))
            log_total = log_ref[0, 2 * pair + head : 2 * pair + head + 1, :]
            scores = jnp.where(mask, dot_nt(key, my_query) * score_scale, masked_fill)
            probs = jnp.exp(scores - log_total)
            d_probs = dot_nt(value, my_grad)
            d_value = d_value + dot_nn(probs.astype(bf16), my_grad)
            inner = jnp.sum(probs * d_probs, axis=0, keepdims=True)
            d_scores = (probs * (d_probs - inner)).astype(bf16)
            d_key = d_key + dot_nn(d_scores, my_query)
            d_query_t.append(dot_nn(key_t[head * HD : (head + 1) * HD], d_scores))
        d_query = jnp.concatenate(d_query_t, axis=0).T * score_scale
        pieces = (
            turn(d_query, cosine, -sine).astype(bf16),
            turn(d_key * score_scale, cosine, -sine).astype(bf16),
            d_value.astype(bf16),
        )
        for kind, piece in enumerate(pieces):
            start = kind * width + at
            for core in range(2):
                grad_ref[core, 0, :, start : start + 2 * HD] = piece[core * half : (core + 1) * half]
            bias_ref[0, :, start : start + 2 * HD] = jnp.sum(
                piece.astype(f32), axis=0, keepdims=True
            )
    for core, out_ref in enumerate((core_out_ref, other_out_ref)):
        out_ref[...] = dot_nt(grad_ref[core, 0], weight_ref[:, : 3 * width]).astype(bf16)


def tree_block(*shape, first=0):
    return pl.BlockSpec((1,) + shape, lambda t: (first + t,) + (0,) * len(shape))


def row_block(rows, columns, first=0):
    return pl.BlockSpec((rows, columns), lambda t: (first + t, 0))


def core_block(rows, columns, first=0):
    return pl.BlockSpec((2, 1, rows, columns), lambda t: (0, first + t, 0, 0))


def whole_block(*shape):
    return pl.BlockSpec(shape, lambda t: (0,) * len(shape), pipeline_mode=pl.Buffered(1))


def attention_forward(cores, weights, bias, tree_info):
    row_info, col_info, keep, cosine, sine = tree_info
    model_width = weights.shape[0]
    width = weights.shape[1] // 4
    rows = cores[0].shape[0] // 4
    group = 2 * rows
    heads = width // HD
    shape = jax.ShapeDtypeStruct
    return pl.pallas_call(
        forward_kernel,
        grid=(4,),
        in_specs=[
            row_block(rows, model_width),
            row_block(rows, model_width),
            whole_block(*weights.shape),
            whole_block(1, 3 * width),
            tree_block(*row_info.shape[1:]),
            tree_block(*col_info.shape[1:]),
            tree_block(*keep.shape[1:]),
            tree_block(*cosine.shape[1:]),
            tree_block(*sine.shape[1:]),
        ],
        out_specs=[
            core_block(rows, 3 * width),
            core_block(rows, width),
            tree_block(heads, group),
            row_block(rows, model_width),
            row_block(rows, model_width),
        ],
        out_shape=[
            shape((2, 4, rows, 3 * width), bf16),
            shape((2, 4, rows, width), bf16),
            shape((4, heads, group), f32),
            shape((4 * rows, model_width), bf16),
            shape((4 * rows, model_width), bf16),
        ],
        scratch_shapes=[pltpu.VMEM((group, 3 * width), f32)],
        compiler_params=pltpu.CompilerParams(vmem_limit_bytes=48 << 20),
        cost_estimate=pl.CostEstimate(
            flops=16 * group * model_width * width * 2, bytes_accessed=32 << 20, transcendentals=4 << 20
        ),
        name="attention_forward",
    )(
        *cores,
        weights,
        bias,
        row_info,
        col_info,
        keep,
        cosine,
        sine,
    )


def attention_backward(cores, weights, qkv, log_totals, tree_info, first, count):
    row_info, col_info, keep, cosine, sine = tree_info
    model_width = weights.shape[0]
    width = weights.shape[1] // 4
    rows = cores[0].shape[0] // count
    group = 2 * rows
    heads = width // HD
    shape = jax.ShapeDtypeStruct
    return pl.pallas_call(
        backward_kernel,
        grid=(count,),
        in_specs=[
            row_block(rows, model_width),
            row_block(rows, model_width),
            whole_block(*weights.shape),
            core_block(rows, 3 * width, first=first),
            tree_block(*row_info.shape[1:], first=first),
            tree_block(*col_info.shape[1:], first=first),
            tree_block(*keep.shape[1:], first=first),
            tree_block(*cosine.shape[1:], first=first),
            tree_block(*sine.shape[1:], first=first),
            tree_block(heads, group, first=first),
        ],
        out_specs=[
            core_block(rows, 3 * width),
            tree_block(1, 3 * width),
            row_block(rows, model_width),
            row_block(rows, model_width),
        ],
        out_shape=[
            shape((2, count, rows, 3 * width), bf16),
            shape((count, 1, 3 * width), f32),
            shape((count * rows, model_width), bf16),
            shape((count * rows, model_width), bf16),
        ],
        scratch_shapes=[pltpu.VMEM((group, width), f32)],
        compiler_params=pltpu.CompilerParams(vmem_limit_bytes=48 << 20),
        cost_estimate=LIGHT
        if first == 3
        else pl.CostEstimate(
            flops=4 * count * group * model_width * width * 2,
            bytes_accessed=8 * count << 20,
            transcendentals=count << 20,
        ),
        name="attention_backward",
    )(
        *cores,
        weights,
        qkv,
        row_info,
        col_info,
        keep,
        cosine,
        sine,
        log_totals,
    )


def units_kernel(parts, *refs):
    main, mixed = parts
    x_refs, dy_refs, weight_ref = refs[0:2], refs[2:4], refs[4]
    before_refs, out_refs = refs[5:-4], refs[-2:]
    grad_ref, hidden_ref = refs[-4:-2]
    down = main + mixed
    for core in range(2):
        gate_up = dot_nn(x_refs[core][...], weight_ref[:, down:])
        d_hidden = dot_nn(dy_refs[core][...], weight_ref[:, :down])

        def unit(gate, up, grad):
            sigmoid = jax.nn.sigmoid(gate)
            active = gate * sigmoid
            d_gate = grad * up * sigmoid * (1.0 + gate * (1.0 - sigmoid))
            return active * up, d_gate, grad * active

        hidden, d_gate, d_up = unit(
            gate_up[:, :main], gate_up[:, main : 2 * main], d_hidden[:, :main]
        )
        hidden_ref[core, 0, :, :main] = hidden.astype(bf16)
        grad_ref[core, 0, :, :main] = d_gate.astype(bf16)
        grad_ref[core, 0, :, main : 2 * main] = d_up.astype(bf16)
        if mixed:
            both = gate_up[:, 2 * main :]
            hidden, d_gate, d_up = unit(both, pltpu.roll(both, 64, 1), d_hidden[:, main:])
            hidden_ref[core, 0, :, main:] = low_lanes(hidden, 0.0).astype(bf16)
            grad_ref[core, 0, :, 2 * main :] = low_lanes(d_gate, pltpu.roll(d_up, 64, 1)).astype(bf16)
        total = dot_nt(grad_ref[core, 0], weight_ref[:, down:])
        if before_refs:
            total = total + before_refs[core][...].astype(f32)
        out_refs[core][...] = total.astype(bf16)


def hidden_units(xs, dys, weights, parts, trees=(0, 4), before=()):
    first, count = trees
    model_width = weights.shape[0]
    main, mixed = parts
    wide = 2 * main + mixed
    rows = xs[0].shape[0] // 4
    shape = jax.ShapeDtypeStruct
    rows_of = row_block(rows, model_width)
    given = row_block(rows, model_width, first=first)
    return pl.pallas_call(
        partial(units_kernel, parts),
        grid=(count,),
        in_specs=[given] * 4 + [whole_block(*weights.shape)] + [given] * len(before),
        out_specs=[core_block(rows, wide), core_block(rows, main + mixed), rows_of, rows_of],
        out_shape=[
            shape((2, count, rows, wide), bf16),
            shape((2, count, rows, main + mixed), bf16),
            shape((count * rows, model_width), bf16),
            shape((count * rows, model_width), bf16),
        ],
        compiler_params=pltpu.CompilerParams(vmem_limit_bytes=56 << 20),
        cost_estimate=pl.CostEstimate(
            flops=4 * count * rows * model_width * 5 * main,
            bytes_accessed=8 * count << 20,
            transcendentals=count << 18,
        ),
        name="hidden_units",
    )(*xs, *dys, weights, *before)


def dot_tn(a, b):
    return lax.dot_general(a, b, (((0,), (0,)), ((), ())), preferred_element_type=f32)


def weight_kernel(counts, *refs):
    refs, out_ref = list(refs[:-1]), refs[-1]
    start = 0
    for left_count, right_count in counts:
        lefts, refs = refs[:left_count], refs[left_count:]
        rights, refs = refs[:right_count], refs[right_count:]
        columns = rights[0].shape[-1]
        rows = rights[0].shape[2]
        pieces = left_count // 2
        left_ends = [sum(left.shape[0] for left in lefts[: i + 1]) // rows for i in range(pieces)]
        right_ends = [sum(right.shape[1] for right in rights[: i + 1]) for i in range(right_count)]
        total = 0.0
        for core in range(2):
            tree = 0
            for end in sorted({*left_ends, *right_ends}):
                i = sum(tree >= left_end for left_end in left_ends)
                j = sum(tree >= right_end for right_end in right_ends)
                at = tree - ([0] + left_ends)[i]
                left = lefts[core * pieces + i][at * rows : (at + end - tree) * rows]
                at = tree - ([0] + right_ends)[j]
                right = rights[j][core, at : at + end - tree].reshape(-1, columns)
                total = total + dot_tn(left, right)
                tree = end
        out_ref[:, start : start + columns] = total.astype(bf16)
        start += columns


def weight_terms(*products):
    model_width = products[0][0][0].shape[1]
    block = 256
    total = sum(rights[0].shape[-1] for _, rights in products)
    operands, specs = [], []
    for lefts, rights in products:
        operands += [*lefts, *rights]
        specs += [pl.BlockSpec((left.shape[0], block), lambda i: (0, i)) for left in lefts]
        specs += [whole_block(*right.shape) for right in rights]
    return pl.pallas_call(
        partial(weight_kernel, [(len(lefts), len(rights)) for lefts, rights in products]),
        grid=(model_width // block,),
        in_specs=specs,
        out_specs=pl.BlockSpec((block, total), lambda i: (i, 0)),
        out_shape=jax.ShapeDtypeStruct((model_width, total), bf16),
        compiler_params=pltpu.CompilerParams(vmem_limit_bytes=60 << 20),
        cost_estimate=LIGHT,
        name="weight_terms",
    )(*operands)


def out_kernel(first_ref, second_ref, first_weight_ref, second_weight_ref, *out_refs):
    for core, out_ref in enumerate(out_refs):
        total = dot_nt(first_ref[core, 0], first_weight_ref[...])
        total = total + dot_nt(second_ref[core, 0], second_weight_ref[...])
        out_ref[...] = total.astype(bf16)


def units_out(hiddens, weights, first):
    _, count, rows, _ = hiddens[1].shape
    model_width = weights[0].shape[0]
    return pl.pallas_call(
        out_kernel,
        grid=(count,),
        in_specs=[
            core_block(rows, hiddens[0].shape[-1], first=first),
            core_block(rows, hiddens[1].shape[-1]),
        ]
        + [whole_block(model_width, hidden.shape[-1]) for hidden in hiddens],
        out_specs=[row_block(rows, model_width)] * 2,
        out_shape=[jax.ShapeDtypeStruct((count * rows, model_width), bf16)] * 2,
        compiler_params=pltpu.CompilerParams(vmem_limit_bytes=48 << 20),
        cost_estimate=LIGHT,
        name="units_out",
    )(*hiddens, *weights)


def shards(
    tokens,
    cotangent,
    seg_ids,
    parents,
    valid_mask,
    ln1_gain,
    ln1_bias,
    w_qkv,
    qkv_bias,
    w_out,
    ln2_gain,
    ln2_bias,
    w_gate_up,
    w_down,
):
    own_rows, model_width = tokens.shape
    group_rows = seg_ids.shape[0]
    tp_index = lax.axis_index(TP)
    quarter = place()
    local_width = w_qkv.shape[2]
    width = local_width // 4
    weight_rows, local_units = w_down.shape
    main_a, main_b, rest, _ = unit_columns(local_units)
    mixed = 128 if rest else 0
    always = valid_mask[0] >= 0

    pieces = on_place(
        pack_heads_kernel, "pack_heads", (w_qkv.transpose(1, 0, 2), w_out), [((weight_rows, 4 * width), bf16)] * 4
    )
    attn_pieces = exchange(pieces)
    (normed1,) = norm_rows(tokens, (), ln1_gain, ln1_bias)
    unit_pieces = on_place(
        pack_units_kernel,
        "pack_units",
        (w_gate_up, w_down),
        [((weight_rows, 3 * main_a), bf16)] * 4
        + [((weight_rows, 3 * main_b + 2 * mixed), bf16)] * 4,
    )
    attn_pieces, normed1, unit_pieces = lax.optimization_barrier(
        (attn_pieces, normed1, unit_pieces)
    )
    attn_spread = collected(attn_pieces)
    attn_full = gather_far(attn_spread)

    def prepare(attn_spread, normed1, unit_pieces, seg_ids, valid_mask, parents):
        spread1 = gather_rows(normed1)
        spread_a, spread_b = spread(unit_pieces[:4]), spread(unit_pieces[4:])
        ints = jnp.concatenate([seg_ids, valid_mask, parents[0]])
        plane_ints = plane_trees(ints)

        def halves(values):
            parts = values.reshape(4, 2, own_rows)
            return jnp.where(tp_index == 0, parts, parts[:, ::-1]).reshape(4, group_rows)

        plane_segs = halves(plane_ints[:, :group_rows])
        plane_valid = halves(plane_ints[:, group_rows : 2 * group_rows])
        plane_parents = plane_ints[:, 2 * group_rows :]
        row_ids = (jnp.arange(group_rows, dtype=jnp.int32) + tp_index * own_rows) % group_rows
        parent_one, parent_two, positions = jax.vmap(tree_rows, in_axes=(0, 0, 0, None))(
            plane_segs, plane_parents, plane_valid, row_ids
        )
        all_ids = jnp.broadcast_to(row_ids, plane_segs.shape)
        row_info = jnp.stack([plane_segs, parent_one, parent_two, all_ids], axis=1)
        col_info = jnp.stack([jnp.where(plane_valid > 0, plane_segs, -1), all_ids], axis=2)
        keep = plane_valid.astype(f32)[..., None]
        tree_info = (row_info, col_info, keep, *rope_tables(positions))
        return spread1, spread_a, spread_b, tree_info

    spread1, spread_a, spread_b, tree_info = stage(
        always, prepare, attn_spread, normed1, unit_pieces, seg_ids, valid_mask, parents
    )
    own_valid = tree_info[2][0, :own_rows]
    units_a = gather_far(spread_a)
    units_b = gather_far(spread_b)

    def attend(spread1, attn_full, tree_info):
        own_bias = lax.dynamic_slice(qkv_bias, (0, quarter * width), (3, width))
        return attention_forward(spread1, attn_full, own_bias.reshape(1, -1), tree_info)

    dy_state = gather_begin(after(cotangent, spread1, spread_a, spread_b))
    qkv, context, log_totals, *attn_partial = stage(always, attend, spread1, attn_full, tree_info)

    def renorm(attn_partial, dy_state, tokens):
        dy_diagonal = gather_diagonal(dy_state)
        others, low, high = scatter_cores(*attn_partial)
        middle = scatter_middle(low, high)
        middle, dy_state, dy_diagonal = lax.optimization_barrier((middle, dy_state, dy_diagonal))
        spread_dy = gather_end(dy_state, dy_diagonal)
        parts = attn_partial[0], others, *scatter_end(attn_partial[0], others, 1, middle)
        normed2, attn_out = norm_rows(tokens, parts, ln2_gain, ln2_bias)
        return attn_out, gather_rows(normed2), spread_dy

    attn_out, spread2, spread_dy = stage(always, renorm, attn_partial, dy_state, tokens)

    d_units_a, hidden_a, *d_normed2 = hidden_units(spread2, spread_dy, units_a, (main_a, 0))
    terms_a = weight_terms((spread_dy, (hidden_a,)), (spread2, (d_units_a,)))
    grads_a = scatter_far(terms_a)

    def finish_units(terms_a, spread2, spread_dy, units_a, units_b, d_normed2, hidden_a, attn_out, tokens, cotangent):
        def run(xs, first, count):
            return hidden_units(xs, spread_dy, units_b, (main_b, mixed), (first, count), d_normed2)

        def out(hidden, first):
            return units_out((hidden_a, hidden), (units_a, units_b), first)

        last = run(spread2, 3, 1)
        low, high = add_halves(last[2], swap(last[3], TP))
        xs, low, high = lax.optimization_barrier((spread2, low, high))
        middle = scatter_middle(low, high)
        sides = run(xs, 1, 2)
        middle, sides = lax.optimization_barrier((middle, sides))
        others = swap(sides[3], TP)
        mlp_last = out(last[1], 3)
        others, mlp_last = lax.optimization_barrier((others, mlp_last))
        near, mid = side_sums(sides[2], others, 0, middle)
        xs, near, mid = lax.optimization_barrier((spread2, near, mid))
        near, mid = swap(near, NEAR), swap(mid, MID)
        own = run(xs, 0, 1)
        own_others = swap(own[3], TP)
        units = own, sides, last
        terms_b = weight_terms(
            (spread_dy, [u[1] for u in units]), (spread2, [u[0] for u in units])
        )
        mlp_own, mlp_sides = out(own[1], 0), out(sides[1], 1)
        mlp_cores = add_halves(mlp_last[0], swap(mlp_last[1], TP))
        near, mid, terms_b, mlp_cores, mlp_own, mlp_sides = lax.optimization_barrier(
            (near, mid, terms_b, mlp_cores, mlp_own, mlp_sides)
        )
        mlp_middle = scatter_middle(*mlp_cores)
        parts = own[2], own_others, near, mid
        *d_low, d_residual, norm2_grads = norm_back(
            (tokens, attn_out), parts, ln2_gain, cotangent
        )
        return (mlp_own, mlp_sides, mlp_middle), terms_b, d_residual, d_low, norm2_grads

    mlp, terms_b, d_residual, d_low, norm2_grads = stage(
        always, finish_units, terms_a, spread2, spread_dy, units_a, units_b, d_normed2, hidden_a, attn_out, tokens, cotangent
    )
    grads_a, d_low = lax.optimization_barrier((grads_a, d_low))
    grads_b = scatter_far(terms_b)

    def attend_back(terms_b, d_low, attn_full, qkv, log_totals, tree_info, spread1, context, mlp):
        mlp_own, mlp_sides, mlp_middle = mlp

        def back(cores, first, count):
            return attention_backward(cores, attn_full, qkv, log_totals, tree_info, first, count)

        state = halves_begin(d_low[1:])
        own = d_low[0], swap(d_low[0], TP)
        own_back = back(own, 0, 1)
        mlp_others = swap(mlp_own[1], TP), swap(mlp_sides[1], TP)
        near, mid = side_sums(mlp_sides[0], mlp_others[1], 0, mlp_middle)
        state, own_back, near, mid = lax.optimization_barrier((state, own_back, near, mid))
        diagonal = halves_diagonal(state)
        sides = joined(state)
        sides_back = back(sides, 1, 2)
        diagonal, sides_back, near, mid = lax.optimization_barrier((diagonal, sides_back, near, mid))
        mlp_parts = swap(near, NEAR), swap(mid, MID)
        last = joined(diagonal)
        last_back = back(last, 3, 1)
        backs = own_back, sides_back, last_back
        terms = weight_terms(
            (spread1, [back[0] for back in backs]), (row_pieces(own, sides, last), (context,))
        )
        low, high = add_halves(last_back[2], swap(last_back[3], TP))
        bias_terms = sum(jnp.sum(back[1], axis=0) for back in backs)
        d_normed1 = own_back[2:], sides_back[2:], (low, high)
        return terms, bias_terms, d_normed1, (mlp_own[0], mlp_others[0], *mlp_parts)

    attn_terms, bias_terms, d_normed1, mlp_parts = stage(
        always, attend_back, terms_b, d_low, attn_full, qkv, log_totals, tree_info, spread1, context, mlp
    )
    attn_grads = scatter_far(attn_terms)

    def finish(attn_terms, d_normed1, mlp_parts, grads_a, d_residual, attn_out, tokens, bias_terms, norm2_grads, own_valid):
        own, sides, last = d_normed1
        middle = scatter_middle(*last)
        own_others, sides_others = swap(own[1], TP), swap(sides[1], TP)
        pieces_a = returned(grads_a)
        parts = own[0], own_others, *scatter_end(sides[0], sides_others, 0, middle)
        *_, tokens_grad, norm1_grads = norm_back((tokens,), parts, ln1_gain, d_residual)
        mlp_out = sum(part.astype(f32) for part in mlp_parts)
        stream_out = tokens.astype(f32) + attn_out + mlp_out
        output = stream_out.astype(bf16)
        squares = jnp.stack(
            [
                jnp.sum(own_valid * stream_out * stream_out),
                jnp.sum(own_valid * attn_out * attn_out),
                jnp.sum(own_valid * mlp_out * mlp_out),
                jnp.sum(own_valid),
            ]
        )
        bias_spread = lax.dynamic_update_slice(
            jnp.zeros((3, model_width), f32),
            bias_terms.reshape(3, width),
            (0, tp_index * local_width + quarter * width),
        )
        sums = jnp.concatenate(
            [norm1_grads, norm2_grads, bias_spread, jnp.pad(squares, (0, model_width - 4))[None]]
        )
        return output, tokens_grad, pieces_a, sums

    output, tokens_grad, pieces_a, sums = stage(
        always, finish, attn_terms, d_normed1, mlp_parts, grads_a, d_residual, attn_out, tokens, bias_terms, norm2_grads, own_valid
    )
    pieces_b = returned(after(grads_b, sums))
    sums = sum_over(sums, (TP, NEAR, MID))
    attn_grads, sums, pieces_b = lax.optimization_barrier((attn_grads, sums, pieces_b))
    gate_up_grad, down_grad = on_place(
        unpack_units_kernel,
        "unpack_units",
        (*pieces_a, *pieces_b),
        [(w_gate_up.shape, f32), (w_down.shape, f32)],
    )
    sums = sum_over(sums, (FAR,))
    qkv_grad, out_grad = on_place(
        unpack_heads_kernel,
        "unpack_heads",
        returned(attn_grads),
        [((3, weight_rows, local_width), f32), (w_out.shape, f32)],
    )
    qkv_grad = qkv_grad.transpose(1, 0, 2)
    norm_sums, bias_sums, square_sums = sums[:4], sums[4:7], sums[7]
    stream_rms = jnp.sqrt(square_sums[:3] / (square_sums[3] * model_width))
    qkv_bias_grad = lax.dynamic_slice(bias_sums, (0, tp_index * local_width), (3, local_width))
    return (
        output,
        tokens_grad,
        norm_sums[0],
        norm_sums[1],
        qkv_grad,
        qkv_bias_grad,
        out_grad,
        norm_sums[2],
        norm_sums[3],
        gate_up_grad,
        down_grad,
        stream_rms,
    )


def solution(mesh):
    planes = mesh.shape["fsdp"] // 4
    grid = Mesh(mesh.devices.reshape(planes, 2, 2, mesh.shape["tp"]), ALL)
    fsdp = (FAR, MID, NEAR)
    return jax.shard_map(
        shards,
        mesh=grid,
        in_specs=(
            P(ALL, None),
            P(ALL, None),
            P(fsdp),
            P(fsdp, None),
            P(fsdp),
            P(),
            P(),
            P(fsdp, None, TP),
            P(None, TP),
            P(fsdp, TP),
            P(),
            P(),
            P(fsdp, None, TP),
            P(fsdp, TP),
        ),
        out_specs=(
            P(ALL, None),
            P(ALL, None),
            P(),
            P(),
            P(fsdp, None, TP),
            P(None, TP),
            P(fsdp, TP),
            P(),
            P(),
            P(fsdp, None, TP),
            P(fsdp, TP),
            P(),
        ),
        check_vma=False,
    )
```

```python
from functools import partial
import math

import jax
import jax.numpy as jnp
from jax import lax
from jax.experimental import pallas as pl
from jax.experimental.pallas import tpu as pltpu
from jax.sharding import Mesh, PartitionSpec as P

HD = 64
ROT = 16

epsilon = 1e-05
score_scale = 0.125
masked_fill = -1e30

FAR, MID, NEAR, TP = "far", "mid", "near", "tp"
ALL = (FAR, MID, NEAR, TP)
f32 = jnp.float32
bf16 = jnp.bfloat16
LIGHT = pl.CostEstimate(flops=0, bytes_accessed=0, transcendentals=0)


def swap(values, axis):
    return lax.ppermute(values, axis, [(0, 1), (1, 0)])


def place():
    return lax.axis_index(MID) * 2 + lax.axis_index(NEAR)


def swap_diagonal(values):
    return lax.ppermute(values, (MID, NEAR), [(0, 3), (1, 2), (2, 1), (3, 0)])


def after(values, *others):
    return lax.optimization_barrier((values,) + others)[0]


def crossed(pieces):
    other = lax.axis_index(NEAR) == 1
    p = [jnp.where(other, pieces[i ^ 1], pieces[i]) for i in range(4)]
    other = lax.axis_index(MID) == 1
    return [jnp.where(other, p[i ^ 2], p[i]) for i in range(4)]


def exchange(pieces):
    return [pieces[0], swap(pieces[1], NEAR), swap(pieces[2], MID), swap_diagonal(pieces[3])]


def place():
    return lax.axis_index(MID) * 2 + lax.axis_index(NEAR)


def quarter_parts(width):
    tiles, rest = divmod(width // 4, 128)
    return tiles - tiles // 2, tiles // 2, rest


def half_tile(values, odd):
    values = values.astype(f32)
    return jnp.where(odd, pltpu.roll(values, 64, 1), values)


def low_lanes(low, high):
    lane = lax.broadcasted_iota(jnp.int32, (1, 128), 1)
    return jnp.where(lane < 64, low, high)


def pack_heads_kernel(place_ref, stack_ref, last_ref, *piece_refs):
    width = last_ref.shape[1] // 4
    for i, piece_ref in enumerate(piece_refs):
        part = pl.ds(pl.multiple_of((place_ref[0] ^ i) * width, 128), width)
        for kind in range(4):
            piece_ref[:, kind * width : (kind + 1) * width] = (
                stack_ref[kind, :, part] if kind < 3 else last_ref[:, part]
            )


def unpack_heads_kernel(place_ref, *refs):
    piece_refs, stack_ref, last_ref = refs[:4], refs[4], refs[5]
    width = last_ref.shape[1] // 4
    for i, piece_ref in enumerate(piece_refs):
        part = pl.ds(pl.multiple_of((place_ref[0] ^ i) * width, 128), width)
        for kind in range(4):
            piece = piece_ref[:, kind * width : (kind + 1) * width].astype(f32)
            if kind < 3:
                stack_ref[kind, :, part] = piece
            else:
                last_ref[:, part] = piece


def unit_columns(width):
    first, second, rest = quarter_parts(width)
    return first * 128, second * 128, rest, 4 * 128 * (first + second)


def pack_units_kernel(place_ref, stack_ref, last_ref, *piece_refs):
    first, second, rest, rest_start = unit_columns(last_ref.shape[1])

    def read(kind, part):
        return stack_ref[:, kind, part] if kind < 2 else last_ref[:, part]

    for i in range(4):
        chip = place_ref[0] ^ i
        first_ref, second_ref = piece_refs[i], piece_refs[4 + i]
        part = pl.ds(pl.multiple_of(chip * first, 128), first)
        for slot, kind in enumerate((2, 0, 1)):
            first_ref[:, slot * first : (slot + 1) * first] = read(kind, part)
        part = pl.ds(pl.multiple_of(4 * first + chip * second, 128), second)
        gates = second + (128 if rest else 0)
        mixed = gates + 2 * second
        for kind, start in enumerate((gates, gates + second, 0)):
            second_ref[:, start : start + second] = read(kind, part)
        if rest:
            part = pl.ds(pl.multiple_of(rest_start + (chip // 2) * 128, 128), 128)
            gate, up, last = [half_tile(read(kind, part), chip % 2 == 1) for kind in range(3)]
            second_ref[:, mixed : mixed + 128] = low_lanes(gate, pltpu.roll(up, 64, 1)).astype(bf16)
            second_ref[:, second:gates] = low_lanes(last, 0.0).astype(bf16)


def unpack_units_kernel(place_ref, *refs):
    piece_refs, stack_ref, last_ref = refs[:8], refs[8], refs[9]
    first, second, rest, rest_start = unit_columns(last_ref.shape[1])

    def write(kind, part, values):
        if kind < 2:
            stack_ref[:, kind, part] = values
        else:
            last_ref[:, part] = values

    for i in range(4):
        chip = place_ref[0] ^ i
        first_ref, second_ref = piece_refs[i], piece_refs[4 + i]
        part = pl.ds(pl.multiple_of(chip * first, 128), first)
        for slot, kind in enumerate((2, 0, 1)):
            write(kind, part, first_ref[:, slot * first : (slot + 1) * first].astype(f32))
        part = pl.ds(pl.multiple_of(4 * first + chip * second, 128), second)
        gates = second + (128 if rest else 0)
        mixed = gates + 2 * second
        for kind, start in enumerate((gates, gates + second, 0)):
            write(kind, part, second_ref[:, start : start + second].astype(f32))
        if rest:
            part = pl.ds(pl.multiple_of(rest_start + (chip // 2) * 128, 128), 128)
            odd = chip % 2 == 1
            lane = lax.broadcasted_iota(jnp.int32, (1, 128), 1)
            mine = (lane >= 64) == odd
            both = second_ref[:, mixed : mixed + 128].astype(f32)
            turned = pltpu.roll(both, 64, 1)
            last = second_ref[:, second:gates].astype(f32)
            last = jnp.where(odd, pltpu.roll(last, 64, 1), last)
            for kind, values in enumerate(
                (jnp.where(odd, turned, both), jnp.where(odd, both, turned), last)
            ):
                held = stack_ref[:, kind, part] if kind < 2 else last_ref[:, part]
                write(kind, part, jnp.where(mine, values, held))


def on_place(kernel, name, operands, outs):
    vmem = pl.BlockSpec(memory_space=pltpu.VMEM)
    return pl.pallas_call(
        kernel,
        in_specs=[pl.BlockSpec(memory_space=pltpu.SMEM)] + [vmem] * len(operands),
        out_specs=[vmem] * len(outs),
        out_shape=[jax.ShapeDtypeStruct(*out) for out in outs],
        compiler_params=pltpu.CompilerParams(vmem_limit_bytes=16 << 20),
        cost_estimate=LIGHT,
        name=name,
    )(place().reshape(1), *operands)


def collected(pieces):
    return jnp.concatenate(crossed(pieces), axis=0)


def spread(pieces):
    return collected(exchange(pieces))


def split_kernel(place_ref, values_ref, *piece_refs):
    rows = piece_refs[0].shape[0]
    for i, piece_ref in enumerate(piece_refs):
        start = pl.multiple_of((place_ref[0] ^ i) * rows, rows)
        piece_ref[...] = values_ref[pl.ds(start, rows), :]


def returned(values):
    shape = (values.shape[0] // 4, values.shape[1])
    return exchange(on_place(split_kernel, "split_rows", (values,), [(shape, bf16)] * 4))


def gather_begin(own):
    return own, swap(own, NEAR), swap(own, MID)


def gather_diagonal(state):
    own, near, mid = state
    half = own.shape[0] // 2
    return swap(near[:half], MID), swap(mid[half:], NEAR)


def gather_end(state, diagonal):
    core = jnp.concatenate([*state, *diagonal], axis=0)
    return core, swap(core, TP)


def halves_begin(halves):
    return [swap(half, axis) for axis in (NEAR, MID) for half in halves]


def halves_diagonal(sides):
    return swap(sides[0], MID), swap(sides[3], NEAR)


def joined(pieces):
    rows = jnp.concatenate(pieces, axis=0)
    return rows, swap(rows, TP)


def row_pieces(*pairs):
    return [pair[core] for core in range(2) for pair in pairs]


def gather_rows(own):
    state = gather_begin(own)
    return gather_end(state, gather_diagonal(state))


def add_low(*values):
    return sum(value.astype(f32) for value in values).astype(bf16)


def add_halves(mine, others):
    half = mine.shape[0] // 2
    return add_low(mine[:half], others[:half]), add_low(mine[half:], others[half:])


def scatter_cores(mine, others):
    others = swap(others, TP)
    start = 3 * (mine.shape[0] // 4)
    return others, *add_halves(mine[start:], others[start:])


def scatter_middle(low, high):
    return swap(low, MID), swap(high, NEAR)


def side_sums(mine, others, first, middle):
    half = middle[0].shape[0]
    start = 2 * half * first
    near, mid = slice(start, start + 2 * half), slice(start + 2 * half, start + 4 * half)
    near = add_low(mine[near], others[near], jnp.pad(middle[0], ((0, half), (0, 0))))
    mid = add_low(mine[mid], others[mid], jnp.pad(middle[1], ((half, 0), (0, 0))))
    return near, mid


def scatter_end(mine, others, first, middle):
    near, mid = side_sums(mine, others, first, middle)
    return swap(near, NEAR), swap(mid, MID)


def stage(always, step, *operands):
    shapes = jax.eval_shape(step, *operands)

    def never(*_):
        return jax.tree.map(lambda s: jnp.zeros(s.shape, s.dtype), shapes)

    return lax.cond(always, step, never, *operands)


def gather_far(values):
    return lax.all_gather(values, FAR, axis=0, tiled=True)


def scatter_far(values):
    return lax.psum_scatter(values, FAR, scatter_dimension=0, tiled=True)


def plane_trees(values):
    return jnp.stack(exchange([values] * 4))


def sum_steps(values, axis, first=0, last=None):
    size = lax.axis_size(axis)
    if size & (size - 1):
        return lax.psum(values, axis) if first == 0 else values
    for i in range(size.bit_length() - 1)[first:last]:
        pairs = [(j, j ^ (1 << i)) for j in range(size)]
        values = values + lax.ppermute(values, axis, pairs)
    return values


def sum_over(values, axes):
    for axis in axes:
        values = sum_steps(values, axis)
    return values


def tree_rows(seg_ids, parents, valid_mask, row_ids):
    labels = jnp.arange(parents.shape[0], dtype=jnp.int32)
    parent_one = jnp.sum(
        jnp.where(seg_ids[:, None] == labels[None, :], parents[None, :], 0), axis=1
    )
    parent_two = jnp.sum(
        jnp.where(parent_one[:, None] == labels[None, :], parents[None, :], 0), axis=1
    )
    key_segs = seg_ids[None, :]
    related = (
        (key_segs == seg_ids[:, None])
        | (key_segs == parent_one[:, None])
        | (key_segs == parent_two[:, None])
    )
    allowed = related & (row_ids[None, :] <= row_ids[:, None]) & (valid_mask[None, :] > 0)
    allowed = allowed | (row_ids[None, :] == row_ids[:, None])
    positions = jnp.sum(allowed.astype(jnp.int32), axis=1) - 1
    return (parent_one, parent_two, positions)


def normalised(values):
    centre = values - jnp.mean(values, axis=-1, keepdims=True)
    inverse = lax.rsqrt(jnp.mean(centre * centre, axis=-1, keepdims=True) + epsilon)
    return centre * inverse, inverse


def write_halves(refs, values):
    whole_ref, low_ref, high_ref = refs
    values = values.astype(bf16)
    whole_ref[...] = values
    half = pl.num_programs(0) // 2

    @pl.when(pl.program_id(0) < half)
    def _():
        low_ref[...] = values

    @pl.when(pl.program_id(0) >= half)
    def _():
        high_ref[...] = values


def halves_specs(block, width, steps):
    half = steps // 2
    return [
        pl.BlockSpec((block, width), lambda i: (i, 0)),
        pl.BlockSpec((block, width), lambda i: (jnp.minimum(i, half - 1), 0)),
        pl.BlockSpec((block, width), lambda i: (jnp.maximum(i - half, 0), 0)),
    ]


def halves_shapes(rows, width):
    return [jax.ShapeDtypeStruct((size, width), bf16) for size in (rows, rows // 2, rows // 2)]


def norm_kernel(*refs):
    row_ref, part_refs, gain_ref, shift_ref = refs[0], refs[1:-4], refs[-4], refs[-3]
    if len(refs) == 4:
        row_ref, gain_ref, shift_ref, normed_ref = refs
        part_refs = ()
    else:
        normed_ref, added_ref = refs[-2:]
    values = row_ref[...].astype(f32)
    if part_refs:
        added = sum(ref[...].astype(f32) for ref in part_refs)
        added_ref[...] = added
        values = values + added
    normed_ref[...] = (normalised(values)[0] * gain_ref[...] + shift_ref[...]).astype(bf16)


def norm_rows(tokens, parts, gain, shift):
    rows, width = tokens.shape
    block = min(64, rows)
    of_rows = pl.BlockSpec((block, width), lambda i: (i, 0))
    of_gain = pl.BlockSpec((1, width), lambda i: (0, 0))
    kinds = [bf16] + [f32] * bool(parts)
    return pl.pallas_call(
        norm_kernel,
        grid=(rows // block,),
        in_specs=[of_rows] * (1 + len(parts)) + [of_gain] * 2,
        out_specs=[of_rows] * len(kinds),
        out_shape=[jax.ShapeDtypeStruct((rows, width), kind) for kind in kinds],
        compiler_params=pltpu.CompilerParams(vmem_limit_bytes=12 << 20),
        cost_estimate=LIGHT,
        name="norm_rows",
    )(tokens, *parts, gain[None], shift[None])


def norm_back_kernel(count, *refs):
    row_refs, part_refs = refs[:count], refs[count:-7]
    gain_ref, past_ref, *low_refs, grad_ref, sum_ref = refs[-7:]
    normed, inverse = normalised(sum(ref[...].astype(f32) for ref in row_refs))
    grad = sum(ref[...].astype(f32) for ref in part_refs)
    scaled = grad * gain_ref[...]
    centred = (
        scaled
        - jnp.mean(scaled, axis=-1, keepdims=True)
        - normed * jnp.mean(scaled * normed, axis=-1, keepdims=True)
    )
    total = past_ref[...].astype(f32) + inverse * centred
    grad_ref[...] = total
    write_halves(low_refs, total)

    @pl.when(pl.program_id(0) == 0)
    def _():
        sum_ref[...] = jnp.zeros_like(sum_ref)

    sum_ref[0:1] += jnp.sum(grad * normed, axis=0, keepdims=True)
    sum_ref[1:2] += jnp.sum(grad, axis=0, keepdims=True)


def norm_back(summands, parts, gain, past):
    rows, width = past.shape
    block = min(64, rows // 2)
    of_rows = pl.BlockSpec((block, width), lambda i: (i, 0))
    of_gain = pl.BlockSpec((1, width), lambda i: (0, 0))
    shape = jax.ShapeDtypeStruct
    return pl.pallas_call(
        partial(norm_back_kernel, len(summands)),
        grid=(rows // block,),
        in_specs=[of_rows] * (len(summands) + len(parts)) + [of_gain, of_rows],
        out_specs=halves_specs(block, width, rows // block)
        + [of_rows, pl.BlockSpec((2, width), lambda i: (0, 0))],
        out_shape=halves_shapes(rows, width) + [shape((rows, width), f32), shape((2, width), f32)],
        compiler_params=pltpu.CompilerParams(vmem_limit_bytes=12 << 20),
        cost_estimate=LIGHT,
        name="norm_back",
    )(*summands, *parts, gain[None], past)


def rope_tables(positions):
    half = ROT // 2
    lane = jnp.arange(2 * HD, dtype=jnp.int32) % HD
    power = (lane % half).astype(f32) * (-2.0 * math.log(10000.0) / ROT)
    inverse_freq = jnp.where(lane < ROT, jnp.exp(power), 0.0)
    angles = positions.astype(f32)[..., None] * inverse_freq
    return jnp.cos(angles), jnp.sin(angles)


def turn(values, cosine, sine):
    half = ROT // 2
    lane = lax.broadcasted_iota(jnp.int32, (1, 2 * HD), 1) % HD
    ahead = pltpu.roll(values, 2 * HD - half, 1)
    behind = pltpu.roll(values, half, 1)
    return values * cosine + jnp.where(lane < half, -ahead, behind) * sine


def allowed_keys(row_ref, col_ref):
    row_seg, parent_one, parent_two, row_id = [row_ref[0, i : i + 1, :] for i in range(4)]
    key_seg = col_ref[0, :, 0:1]
    key_id = col_ref[0, :, 1:2]
    related = (key_seg == row_seg) | (key_seg == parent_one) | (key_seg == parent_two)
    return (related & (key_id <= row_id)) | (key_id == row_id)


def dot_nt(a, b):
    return lax.dot_general(a, b, (((1,), (1,)), ((), ())), preferred_element_type=f32)


def dot_nn(a, b):
    return jnp.dot(a, b, preferred_element_type=f32)


def head_lanes(head):
    lane = lax.broadcasted_iota(jnp.int32, (1, 2 * HD), 1)
    return lane < HD if head == 0 else lane >= HD


def forward_kernel(
    core_ref, other_ref, weight_ref, bias_ref, row_ref, col_ref, keep_ref, cos_ref, sin_ref,
    qkv_ref, context_ref, log_ref, core_out_ref, other_out_ref, linear,
):
    half = core_ref.shape[0]
    width = context_ref.shape[3]
    linear[:half] = dot_nn(core_ref[...], weight_ref[:, : 3 * width]) + bias_ref[...]
    linear[half:] = dot_nn(other_ref[...], weight_ref[:, : 3 * width]) + bias_ref[...]
    mask = allowed_keys(row_ref, col_ref)
    cosine, sine = cos_ref[0], sin_ref[0]
    for pair in range(width // (2 * HD)):
        at = pair * 2 * HD
        lanes = slice(at, at + 2 * HD)
        query = turn(linear[:, lanes], cosine, sine).astype(bf16)
        key = turn(linear[:, width + at : width + at + 2 * HD], cosine, sine).astype(bf16)
        value = linear[:, 2 * width + at : 2 * width + at + 2 * HD]
        value_t = value.T.astype(bf16)
        value = value.astype(bf16)
        for core in range(2):
            rows = slice(core * half, (core + 1) * half)
            qkv_ref[core, 0, :, lanes] = query[rows]
            qkv_ref[core, 0, :, width + at : width + at + 2 * HD] = key[rows]
            qkv_ref[core, 0, :, 2 * width + at : 2 * width + at + 2 * HD] = value[rows]
        context_t = []
        for head in range(2):
            mine = jnp.where(head_lanes(head), query, jnp.zeros_like(query))
            scores = jnp.where(mask, dot_nt(key, mine) * score_scale, masked_fill)
            row_max = jnp.max(scores, axis=0, keepdims=True)
            exponent = jnp.exp(scores - row_max)
            row_sum = jnp.sum(exponent, axis=0, keepdims=True)
            log_ref[0, 2 * pair + head : 2 * pair + head + 1, :] = row_max + jnp.log(row_sum)
            context_t.append(
                dot_nn(value_t[head * HD : (head + 1) * HD], exponent.astype(bf16)) / row_sum
            )
        context = (jnp.concatenate(context_t, axis=0).T * keep_ref[0]).astype(bf16)
        for core in range(2):
            context_ref[core, 0, :, lanes] = context[core * half : (core + 1) * half]
    for core, out_ref in enumerate((core_out_ref, other_out_ref)):
        out_ref[...] = dot_nt(context_ref[core, 0], weight_ref[:, 3 * width :]).astype(bf16)


def backward_kernel(
    core_ref, other_ref, weight_ref, qkv_ref, row_ref, col_ref, keep_ref, cos_ref, sin_ref, log_ref,
    grad_ref, bias_ref, core_out_ref, other_out_ref, grads,
):
    half = core_ref.shape[0]
    width = weight_ref.shape[1] // 4
    grads[:half] = dot_nn(core_ref[...], weight_ref[:, 3 * width :])
    grads[half:] = dot_nn(other_ref[...], weight_ref[:, 3 * width :])
    mask = allowed_keys(row_ref, col_ref)
    cosine, sine = cos_ref[0], sin_ref[0]

    def both(at):
        return jnp.concatenate([qkv_ref[core, 0, :, at : at + 2 * HD] for core in range(2)], axis=0)

    for pair in range(width // (2 * HD)):
        at = pair * 2 * HD
        query, key, value = both(at), both(width + at), both(2 * width + at)
        key_t = key.astype(f32).T.astype(bf16)
        d_context = (grads[:, at : at + 2 * HD] * keep_ref[0]).astype(bf16)
        d_query_t = []
        d_key = jnp.zeros(query.shape, f32)
        d_value = jnp.zeros(query.shape, f32)
        for head in range(2):
            lanes = head_lanes(head)
            my_query = jnp.where(lanes, query, jnp.zeros_like(query))
            my_grad = jnp.where(lanes, d_context, jnp.zeros_like(d_context))
            log_total = log_ref[0, 2 * pair + head : 2 * pair + head + 1, :]
            scores = jnp.where(mask, dot_nt(key, my_query) * score_scale, masked_fill)
            probs = jnp.exp(scores - log_total)
            d_probs = dot_nt(value, my_grad)
            d_value = d_value + dot_nn(probs.astype(bf16), my_grad)
            inner = jnp.sum(probs * d_probs, axis=0, keepdims=True)
            d_scores = (probs * (d_probs - inner)).astype(bf16)
            d_key = d_key + dot_nn(d_scores, my_query)
            d_query_t.append(dot_nn(key_t[head * HD : (head + 1) * HD], d_scores))
        d_query = jnp.concatenate(d_query_t, axis=0).T * score_scale
        pieces = (
            turn(d_query, cosine, -sine).astype(bf16),
            turn(d_key * score_scale, cosine, -sine).astype(bf16),
            d_value.astype(bf16),
        )
        for kind, piece in enumerate(pieces):
            start = kind * width + at
            for core in range(2):
                grad_ref[core, 0, :, start : start + 2 * HD] = piece[core * half : (core + 1) * half]
            bias_ref[0, :, start : start + 2 * HD] = jnp.sum(
                piece.astype(f32), axis=0, keepdims=True
            )
    for core, out_ref in enumerate((core_out_ref, other_out_ref)):
        out_ref[...] = dot_nt(grad_ref[core, 0], weight_ref[:, : 3 * width]).astype(bf16)


def tree_block(*shape, first=0):
    return pl.BlockSpec((1,) + shape, lambda t: (first + t,) + (0,) * len(shape))


def row_block(rows, columns, first=0):
    return pl.BlockSpec((rows, columns), lambda t: (first + t, 0))


def core_block(rows, columns, first=0):
    return pl.BlockSpec((2, 1, rows, columns), lambda t: (0, first + t, 0, 0))


def whole_block(*shape):
    return pl.BlockSpec(shape, lambda t: (0,) * len(shape), pipeline_mode=pl.Buffered(1))


def attention_forward(cores, weights, bias, tree_info):
    row_info, col_info, keep, cosine, sine = tree_info
    model_width = weights.shape[0]
    width = weights.shape[1] // 4
    rows = cores[0].shape[0] // 4
    group = 2 * rows
    heads = width // HD
    shape = jax.ShapeDtypeStruct
    return pl.pallas_call(
        forward_kernel,
        grid=(4,),
        in_specs=[
            row_block(rows, model_width),
            row_block(rows, model_width),
            whole_block(*weights.shape),
            whole_block(1, 3 * width),
            tree_block(*row_info.shape[1:]),
            tree_block(*col_info.shape[1:]),
            tree_block(*keep.shape[1:]),
            tree_block(*cosine.shape[1:]),
            tree_block(*sine.shape[1:]),
        ],
        out_specs=[
            core_block(rows, 3 * width),
            core_block(rows, width),
            tree_block(heads, group),
            row_block(rows, model_width),
            row_block(rows, model_width),
        ],
        out_shape=[
            shape((2, 4, rows, 3 * width), bf16),
            shape((2, 4, rows, width), bf16),
            shape((4, heads, group), f32),
            shape((4 * rows, model_width), bf16),
            shape((4 * rows, model_width), bf16),
        ],
        scratch_shapes=[pltpu.VMEM((group, 3 * width), f32)],
        compiler_params=pltpu.CompilerParams(vmem_limit_bytes=24 << 20),
        cost_estimate=pl.CostEstimate(
            flops=16 * group * model_width * width * 2, bytes_accessed=32 << 20, transcendentals=4 << 20
        ),
        name="attention_forward",
    )(
        *cores,
        weights,
        bias,
        row_info,
        col_info,
        keep,
        cosine,
        sine,
    )


def attention_backward(cores, weights, qkv, log_totals, tree_info, first, count):
    row_info, col_info, keep, cosine, sine = tree_info
    model_width = weights.shape[0]
    width = weights.shape[1] // 4
    rows = cores[0].shape[0] // count
    group = 2 * rows
    heads = width // HD
    shape = jax.ShapeDtypeStruct
    return pl.pallas_call(
        backward_kernel,
        grid=(count,),
        in_specs=[
            row_block(rows, model_width),
            row_block(rows, model_width),
            whole_block(*weights.shape),
            core_block(rows, 3 * width, first=first),
            tree_block(*row_info.shape[1:], first=first),
            tree_block(*col_info.shape[1:], first=first),
            tree_block(*keep.shape[1:], first=first),
            tree_block(*cosine.shape[1:], first=first),
            tree_block(*sine.shape[1:], first=first),
            tree_block(heads, group, first=first),
        ],
        out_specs=[
            core_block(rows, 3 * width),
            tree_block(1, 3 * width),
            row_block(rows, model_width),
            row_block(rows, model_width),
        ],
        out_shape=[
            shape((2, count, rows, 3 * width), bf16),
            shape((count, 1, 3 * width), f32),
            shape((count * rows, model_width), bf16),
            shape((count * rows, model_width), bf16),
        ],
        scratch_shapes=[pltpu.VMEM((group, width), f32)],
        compiler_params=pltpu.CompilerParams(vmem_limit_bytes=24 << 20),
        cost_estimate=LIGHT
        if first == 3
        else pl.CostEstimate(
            flops=4 * count * group * model_width * width * 2,
            bytes_accessed=8 * count << 20,
            transcendentals=count << 20,
        ),
        name="attention_backward",
    )(
        *cores,
        weights,
        qkv,
        row_info,
        col_info,
        keep,
        cosine,
        sine,
        log_totals,
    )


def units_kernel(parts, *refs):
    main, mixed = parts
    x_refs, dy_refs, weight_ref = refs[0:2], refs[2:4], refs[4]
    before_refs, out_refs = refs[5:-4], refs[-2:]
    grad_ref, hidden_ref = refs[-4:-2]
    down = main + mixed
    for core in range(2):
        gate_up = dot_nn(x_refs[core][...], weight_ref[:, down:])
        d_hidden = dot_nn(dy_refs[core][...], weight_ref[:, :down])

        def unit(gate, up, grad):
            sigmoid = jax.nn.sigmoid(gate)
            active = gate * sigmoid
            d_gate = grad * up * sigmoid * (1.0 + gate * (1.0 - sigmoid))
            return active * up, d_gate, grad * active

        hidden, d_gate, d_up = unit(
            gate_up[:, :main], gate_up[:, main : 2 * main], d_hidden[:, :main]
        )
        hidden_ref[core, 0, :, :main] = hidden.astype(bf16)
        grad_ref[core, 0, :, :main] = d_gate.astype(bf16)
        grad_ref[core, 0, :, main : 2 * main] = d_up.astype(bf16)
        if mixed:
            both = gate_up[:, 2 * main :]
            hidden, d_gate, d_up = unit(both, pltpu.roll(both, 64, 1), d_hidden[:, main:])
            hidden_ref[core, 0, :, main:] = low_lanes(hidden, 0.0).astype(bf16)
            grad_ref[core, 0, :, 2 * main :] = low_lanes(d_gate, pltpu.roll(d_up, 64, 1)).astype(bf16)
        total = dot_nt(grad_ref[core, 0], weight_ref[:, down:])
        if before_refs:
            total = total + before_refs[core][...].astype(f32)
        out_refs[core][...] = total.astype(bf16)


def hidden_units(xs, dys, weights, parts, trees=(0, 4), before=()):
    first, count = trees
    model_width = weights.shape[0]
    main, mixed = parts
    wide = 2 * main + mixed
    rows = xs[0].shape[0] // 4
    shape = jax.ShapeDtypeStruct
    rows_of = row_block(rows, model_width)
    given = row_block(rows, model_width, first=first)
    return pl.pallas_call(
        partial(units_kernel, parts),
        grid=(count,),
        in_specs=[given] * 4 + [whole_block(*weights.shape)] + [given] * len(before),
        out_specs=[core_block(rows, wide), core_block(rows, main + mixed), rows_of, rows_of],
        out_shape=[
            shape((2, count, rows, wide), bf16),
            shape((2, count, rows, main + mixed), bf16),
            shape((count * rows, model_width), bf16),
            shape((count * rows, model_width), bf16),
        ],
        compiler_params=pltpu.CompilerParams(vmem_limit_bytes=28 << 20),
        cost_estimate=pl.CostEstimate(
            flops=4 * count * rows * model_width * 5 * main,
            bytes_accessed=8 * count << 20,
            transcendentals=count << 18,
        ),
        name="hidden_units",
    )(*xs, *dys, weights, *before)


def dot_tn(a, b):
    return lax.dot_general(a, b, (((0,), (0,)), ((), ())), preferred_element_type=f32)


def weight_kernel(counts, *refs):
    refs, out_ref = list(refs[:-1]), refs[-1]
    start = 0
    for left_count, right_count in counts:
        lefts, refs = refs[:left_count], refs[left_count:]
        rights, refs = refs[:right_count], refs[right_count:]
        columns = rights[0].shape[-1]
        rows = rights[0].shape[2]
        pieces = left_count // 2
        left_ends = [sum(left.shape[0] for left in lefts[: i + 1]) // rows for i in range(pieces)]
        right_ends = [sum(right.shape[1] for right in rights[: i + 1]) for i in range(right_count)]
        total = 0.0
        for core in range(2):
            tree = 0
            for end in sorted({*left_ends, *right_ends}):
                i = sum(tree >= left_end for left_end in left_ends)
                j = sum(tree >= right_end for right_end in right_ends)
                at = tree - ([0] + left_ends)[i]
                left = lefts[core * pieces + i][at * rows : (at + end - tree) * rows]
                at = tree - ([0] + right_ends)[j]
                right = rights[j][core, at : at + end - tree].reshape(-1, columns)
                total = total + dot_tn(left, right)
                tree = end
        out_ref[:, start : start + columns] = total.astype(bf16)
        start += columns


def weight_terms(*products):
    model_width = products[0][0][0].shape[1]
    block = 256
    total = sum(rights[0].shape[-1] for _, rights in products)
    operands, specs = [], []
    for lefts, rights in products:
        operands += [*lefts, *rights]
        specs += [pl.BlockSpec((left.shape[0], block), lambda i: (0, i)) for left in lefts]
        specs += [whole_block(*right.shape) for right in rights]
    return pl.pallas_call(
        partial(weight_kernel, [(len(lefts), len(rights)) for lefts, rights in products]),
        grid=(model_width // block,),
        in_specs=specs,
        out_specs=pl.BlockSpec((block, total), lambda i: (i, 0)),
        out_shape=jax.ShapeDtypeStruct((model_width, total), bf16),
        compiler_params=pltpu.CompilerParams(vmem_limit_bytes=20 << 20),
        cost_estimate=LIGHT,
        name="weight_terms",
    )(*operands)


def out_kernel(first_ref, second_ref, first_weight_ref, second_weight_ref, *out_refs):
    for core, out_ref in enumerate(out_refs):
        total = dot_nt(first_ref[core, 0], first_weight_ref[...])
        total = total + dot_nt(second_ref[core, 0], second_weight_ref[...])
        out_ref[...] = total.astype(bf16)


def units_out(hiddens, weights, first):
    _, count, rows, _ = hiddens[1].shape
    model_width = weights[0].shape[0]
    return pl.pallas_call(
        out_kernel,
        grid=(count,),
        in_specs=[
            core_block(rows, hiddens[0].shape[-1], first=first),
            core_block(rows, hiddens[1].shape[-1]),
        ]
        + [whole_block(model_width, hidden.shape[-1]) for hidden in hiddens],
        out_specs=[row_block(rows, model_width)] * 2,
        out_shape=[jax.ShapeDtypeStruct((count * rows, model_width), bf16)] * 2,
        compiler_params=pltpu.CompilerParams(vmem_limit_bytes=14 << 20),
        cost_estimate=LIGHT,
        name="units_out",
    )(*hiddens, *weights)


def shards(
    tokens,
    cotangent,
    seg_ids,
    parents,
    valid_mask,
    ln1_gain,
    ln1_bias,
    w_qkv,
    qkv_bias,
    w_out,
    ln2_gain,
    ln2_bias,
    w_gate_up,
    w_down,
):
    own_rows, model_width = tokens.shape
    group_rows = seg_ids.shape[0]
    tp_index = lax.axis_index(TP)
    quarter = place()
    local_width = w_qkv.shape[2]
    width = local_width // 4
    weight_rows, local_units = w_down.shape
    main_a, main_b, rest, _ = unit_columns(local_units)
    mixed = 128 if rest else 0
    always = valid_mask[0] >= 0

    pieces = on_place(
        pack_heads_kernel, "pack_heads", (w_qkv.transpose(1, 0, 2), w_out), [((weight_rows, 4 * width), bf16)] * 4
    )
    attn_pieces = exchange(pieces)
    (normed1,) = norm_rows(tokens, (), ln1_gain, ln1_bias)
    unit_pieces = on_place(
        pack_units_kernel,
        "pack_units",
        (w_gate_up, w_down),
        [((weight_rows, 3 * main_a), bf16)] * 4
        + [((weight_rows, 3 * main_b + 2 * mixed), bf16)] * 4,
    )
    attn_pieces, normed1, unit_pieces = lax.optimization_barrier(
        (attn_pieces, normed1, unit_pieces)
    )
    attn_spread = collected(attn_pieces)
    attn_full = gather_far(attn_spread)

    def prepare(attn_spread, normed1, unit_pieces, seg_ids, valid_mask, parents):
        spread1 = gather_rows(normed1)
        spread_a, spread_b = spread(unit_pieces[:4]), spread(unit_pieces[4:])
        ints = jnp.concatenate([seg_ids, valid_mask, parents[0]])
        plane_ints = plane_trees(ints)

        def halves(values):
            parts = values.reshape(4, 2, own_rows)
            return jnp.where(tp_index == 0, parts, parts[:, ::-1]).reshape(4, group_rows)

        plane_segs = halves(plane_ints[:, :group_rows])
        plane_valid = halves(plane_ints[:, group_rows : 2 * group_rows])
        plane_parents = plane_ints[:, 2 * group_rows :]
        row_ids = (jnp.arange(group_rows, dtype=jnp.int32) + tp_index * own_rows) % group_rows
        parent_one, parent_two, positions = jax.vmap(tree_rows, in_axes=(0, 0, 0, None))(
            plane_segs, plane_parents, plane_valid, row_ids
        )
        all_ids = jnp.broadcast_to(row_ids, plane_segs.shape)
        row_info = jnp.stack([plane_segs, parent_one, parent_two, all_ids], axis=1)
        col_info = jnp.stack([jnp.where(plane_valid > 0, plane_segs, -1), all_ids], axis=2)
        keep = plane_valid.astype(f32)[..., None]
        tree_info = (row_info, col_info, keep, *rope_tables(positions))
        return spread1, spread_a, spread_b, tree_info

    spread1, spread_a, spread_b, tree_info = stage(
        always, prepare, attn_spread, normed1, unit_pieces, seg_ids, valid_mask, parents
    )
    own_valid = tree_info[2][0, :own_rows]
    units_a = gather_far(spread_a)
    units_b = gather_far(spread_b)

    def attend(spread1, attn_full, tree_info):
        own_bias = lax.dynamic_slice(qkv_bias, (0, quarter * width), (3, width))
        return attention_forward(spread1, attn_full, own_bias.reshape(1, -1), tree_info)

    dy_state = gather_begin(after(cotangent, spread1, spread_a, spread_b))
    qkv, context, log_totals, *attn_partial = stage(always, attend, spread1, attn_full, tree_info)

    def renorm(attn_partial, dy_state, tokens):
        dy_diagonal = gather_diagonal(dy_state)
        others, low, high = scatter_cores(*attn_partial)
        middle = scatter_middle(low, high)
        middle, dy_state, dy_diagonal = lax.optimization_barrier((middle, dy_state, dy_diagonal))
        spread_dy = gather_end(dy_state, dy_diagonal)
        parts = attn_partial[0], others, *scatter_end(attn_partial[0], others, 1, middle)
        normed2, attn_out = norm_rows(tokens, parts, ln2_gain, ln2_bias)
        return attn_out, gather_rows(normed2), spread_dy

    attn_out, spread2, spread_dy = stage(always, renorm, attn_partial, dy_state, tokens)

    d_units_a, hidden_a, *d_normed2 = hidden_units(spread2, spread_dy, units_a, (main_a, 0))
    terms_a = weight_terms((spread_dy, (hidden_a,)), (spread2, (d_units_a,)))
    grads_a = scatter_far(terms_a)

    def finish_units(terms_a, spread2, spread_dy, units_a, units_b, d_normed2, hidden_a, attn_out, tokens, cotangent):
        def run(xs, first, count):
            return hidden_units(xs, spread_dy, units_b, (main_b, mixed), (first, count), d_normed2)

        def out(hidden, first):
            return units_out((hidden_a, hidden), (units_a, units_b), first)

        last = run(spread2, 3, 1)
        low, high = add_halves(last[2], swap(last[3], TP))
        xs, low, high = lax.optimization_barrier((spread2, low, high))
        middle = scatter_middle(low, high)
        sides = run(xs, 1, 2)
        middle, sides = lax.optimization_barrier((middle, sides))
        others = swap(sides[3], TP)
        mlp_last = out(last[1], 3)
        others, mlp_last = lax.optimization_barrier((others, mlp_last))
        near, mid = side_sums(sides[2], others, 0, middle)
        xs, near, mid = lax.optimization_barrier((spread2, near, mid))
        near, mid = swap(near, NEAR), swap(mid, MID)
        own = run(xs, 0, 1)
        own_others = swap(own[3], TP)
        units = own, sides, last
        mlp_own, mlp_sides = out(own[1], 0), out(sides[1], 1)
        mlp_cores = add_halves(mlp_last[0], swap(mlp_last[1], TP))
        near, mid, mlp_cores, mlp_own, mlp_sides, units = lax.optimization_barrier(
            (near, mid, mlp_cores, mlp_own, mlp_sides, units)
        )
        mlp_middle = scatter_middle(*mlp_cores)
        terms_b = weight_terms(
            (spread_dy, [u[1] for u in units]), (spread2, [u[0] for u in units])
        )
        mlp_middle, terms_b, near, mid = lax.optimization_barrier((mlp_middle, terms_b, near, mid))
        parts = own[2], own_others, near, mid
        *d_low, d_residual, norm2_grads = norm_back(
            (tokens, attn_out), parts, ln2_gain, cotangent
        )
        return (mlp_own, mlp_sides, mlp_middle), terms_b, d_residual, d_low, norm2_grads

    mlp, terms_b, d_residual, d_low, norm2_grads = stage(
        always, finish_units, terms_a, spread2, spread_dy, units_a, units_b, d_normed2, hidden_a, attn_out, tokens, cotangent
    )
    grads_a, d_low = lax.optimization_barrier((grads_a, d_low))
    grads_b = scatter_far(terms_b)

    def attend_back(terms_b, d_low, attn_full, qkv, log_totals, tree_info, spread1, context, mlp, grads_a):
        mlp_own, mlp_sides, mlp_middle = mlp

        def back(cores, first, count):
            return attention_backward(cores, attn_full, qkv, log_totals, tree_info, first, count)

        state = halves_begin(d_low[1:])
        own = d_low[0], swap(d_low[0], TP)
        own_back = back(own, 0, 1)
        mlp_others = swap(mlp_own[1], TP), swap(mlp_sides[1], TP)
        near, mid = side_sums(mlp_sides[0], mlp_others[1], 0, mlp_middle)
        state, own_back, near, mid = lax.optimization_barrier((state, own_back, near, mid))
        diagonal = halves_diagonal(state)
        sides = joined(state)
        sides_back = back(sides, 1, 2)
        diagonal, sides_back, near, mid, grads_a = lax.optimization_barrier(
            (diagonal, sides_back, near, mid, grads_a)
        )
        pieces_a = returned(grads_a)
        last = joined(diagonal)
        last_back = back(last, 3, 1)
        last_back, pieces_a, near, mid = lax.optimization_barrier((last_back, pieces_a, near, mid))
        mlp_parts = swap(near, NEAR), swap(mid, MID)
        backs = own_back, sides_back, last_back
        terms = weight_terms(
            (spread1, [back[0] for back in backs]), (row_pieces(own, sides, last), (context,))
        )
        low, high = add_halves(last_back[2], swap(last_back[3], TP))
        bias_terms = sum(jnp.sum(back[1], axis=0) for back in backs)
        d_normed1 = own_back[2:], sides_back[2:], (low, high)
        return terms, bias_terms, d_normed1, (mlp_own[0], mlp_others[0], *mlp_parts), pieces_a

    attn_terms, bias_terms, d_normed1, mlp_parts, pieces_a = stage(
        always, attend_back, terms_b, d_low, attn_full, qkv, log_totals, tree_info, spread1, context, mlp, grads_a
    )
    attn_grads = scatter_far(attn_terms)

    def finish(attn_terms, d_normed1, mlp_parts, grads_b, d_residual, attn_out, tokens, bias_terms, norm2_grads, own_valid):
        own, sides, last = d_normed1
        middle = scatter_middle(*last)
        own_others, sides_others = swap(own[1], TP), swap(sides[1], TP)
        from_sides = scatter_end(sides[0], sides_others, 0, middle)
        from_sides, grads_b = lax.optimization_barrier((from_sides, grads_b))
        pieces_b = returned(grads_b)
        parts = own[0], own_others, *from_sides
        *_, tokens_grad, norm1_grads = norm_back((tokens,), parts, ln1_gain, d_residual)
        mlp_out = sum(part.astype(f32) for part in mlp_parts)
        stream_out = tokens.astype(f32) + attn_out + mlp_out
        output = stream_out.astype(bf16)
        squares = jnp.stack(
            [
                jnp.sum(own_valid * stream_out * stream_out),
                jnp.sum(own_valid * attn_out * attn_out),
                jnp.sum(own_valid * mlp_out * mlp_out),
                jnp.sum(own_valid),
            ]
        )
        bias_spread = lax.dynamic_update_slice(
            jnp.zeros((3, model_width), f32),
            bias_terms.reshape(3, width),
            (0, tp_index * local_width + quarter * width),
        )
        sums = jnp.concatenate(
            [norm1_grads, norm2_grads, bias_spread, jnp.pad(squares, (0, model_width - 4))[None]]
        )
        return output, tokens_grad, pieces_b, sum_over(sums, (TP,))

    output, tokens_grad, pieces_b, sums = stage(
        always, finish, attn_terms, d_normed1, mlp_parts, grads_b, d_residual, attn_out, tokens, bias_terms, norm2_grads, own_valid
    )
    sums = sum_over(sums, (NEAR, MID))
    far_sums = sum_steps(sums, FAR, 0, 1)
    gate_up_grad, down_grad = on_place(
        unpack_units_kernel,
        "unpack_units",
        (*pieces_a, *pieces_b),
        [(w_gate_up.shape, f32), (w_down.shape, f32)],
    )
    sums, gate_up_grad, down_grad = lax.optimization_barrier((far_sums, gate_up_grad, down_grad))
    sums = sum_steps(sums, FAR, 1)
    attn_grads, sums = lax.optimization_barrier((attn_grads, sums))
    attn_pieces = returned(attn_grads)
    qkv_grad, out_grad = on_place(
        unpack_heads_kernel,
        "unpack_heads",
        attn_pieces,
        [((3, weight_rows, local_width), f32), (w_out.shape, f32)],
    )
    qkv_grad = qkv_grad.transpose(1, 0, 2)
    norm_sums, bias_sums, square_sums = sums[:4], sums[4:7], sums[7]
    stream_rms = jnp.sqrt(square_sums[:3] / (square_sums[3] * model_width))
    qkv_bias_grad = lax.dynamic_slice(bias_sums, (0, tp_index * local_width), (3, local_width))
    return (
        output,
        tokens_grad,
        norm_sums[0],
        norm_sums[1],
        qkv_grad,
        qkv_bias_grad,
        out_grad,
        norm_sums[2],
        norm_sums[3],
        gate_up_grad,
        down_grad,
        stream_rms,
    )


def solution(mesh):
    planes = mesh.shape["fsdp"] // 4
    grid = Mesh(mesh.devices.reshape(planes, 2, 2, mesh.shape["tp"]), ALL)
    fsdp = (FAR, MID, NEAR)
    return jax.shard_map(
        shards,
        mesh=grid,
        in_specs=(
            P(ALL, None),
            P(ALL, None),
            P(fsdp),
            P(fsdp, None),
            P(fsdp),
            P(),
            P(),
            P(fsdp, None, TP),
            P(None, TP),
            P(fsdp, TP),
            P(),
            P(),
            P(fsdp, None, TP),
            P(fsdp, TP),
        ),
        out_specs=(
            P(ALL, None),
            P(ALL, None),
            P(),
            P(),
            P(fsdp, None, TP),
            P(None, TP),
            P(fsdp, TP),
            P(),
            P(),
            P(fsdp, None, TP),
            P(fsdp, TP),
            P(),
        ),
        check_vma=False,
    )
```

```python
from functools import partial
import math

import jax
import jax.numpy as jnp
from jax import lax
from jax.experimental import pallas as pl
from jax.experimental.pallas import tpu as pltpu
from jax.sharding import Mesh, PartitionSpec as P

HD = 64
ROT = 16

epsilon = 1e-05
score_scale = 0.125
masked_fill = -1e30

FAR, MID, NEAR, TP = "far", "mid", "near", "tp"
ALL = (FAR, MID, NEAR, TP)
f32 = jnp.float32
bf16 = jnp.bfloat16
LIGHT = pl.CostEstimate(flops=0, bytes_accessed=0, transcendentals=0)


def swap(values, axis):
    return lax.ppermute(values, axis, [(0, 1), (1, 0)])


def place():
    return lax.axis_index(MID) * 2 + lax.axis_index(NEAR)


def swap_diagonal(values):
    return lax.ppermute(values, (MID, NEAR), [(0, 3), (1, 2), (2, 1), (3, 0)])


def after(values, *others):
    return lax.optimization_barrier((values,) + others)[0]


def crossed(pieces):
    other = lax.axis_index(NEAR) == 1
    p = [jnp.where(other, pieces[i ^ 1], pieces[i]) for i in range(4)]
    other = lax.axis_index(MID) == 1
    return [jnp.where(other, p[i ^ 2], p[i]) for i in range(4)]


def exchange(pieces):
    return [pieces[0], swap(pieces[1], NEAR), swap(pieces[2], MID), swap_diagonal(pieces[3])]


def place():
    return lax.axis_index(MID) * 2 + lax.axis_index(NEAR)


def quarter_parts(width):
    tiles, rest = divmod(width // 4, 128)
    return tiles - tiles // 2, tiles // 2, rest


def half_tile(values, odd):
    values = values.astype(f32)
    return jnp.where(odd, pltpu.roll(values, 64, 1), values)


def low_lanes(low, high):
    lane = lax.broadcasted_iota(jnp.int32, (1, 128), 1)
    return jnp.where(lane < 64, low, high)


def pack_heads_kernel(place_ref, stack_ref, last_ref, *piece_refs):
    width = last_ref.shape[1] // 4
    for i, piece_ref in enumerate(piece_refs):
        part = pl.ds(pl.multiple_of((place_ref[0] ^ i) * width, 128), width)
        for kind in range(4):
            piece_ref[:, kind * width : (kind + 1) * width] = (
                stack_ref[kind, :, part] if kind < 3 else last_ref[:, part]
            )


def unpack_heads_kernel(place_ref, *refs):
    piece_refs, stack_ref, last_ref = refs[:4], refs[4], refs[5]
    width = last_ref.shape[1] // 4
    for i, piece_ref in enumerate(piece_refs):
        part = pl.ds(pl.multiple_of((place_ref[0] ^ i) * width, 128), width)
        for kind in range(4):
            piece = piece_ref[:, kind * width : (kind + 1) * width].astype(f32)
            if kind < 3:
                stack_ref[kind, :, part] = piece
            else:
                last_ref[:, part] = piece


def unit_columns(width):
    first, second, rest = quarter_parts(width)
    return first * 128, second * 128, rest, 4 * 128 * (first + second)


def pack_units_kernel(place_ref, stack_ref, last_ref, *piece_refs):
    first, second, rest, rest_start = unit_columns(last_ref.shape[1])

    def read(kind, part):
        return stack_ref[:, kind, part] if kind < 2 else last_ref[:, part]

    for i in range(4):
        chip = place_ref[0] ^ i
        first_ref, second_ref = piece_refs[i], piece_refs[4 + i]
        part = pl.ds(pl.multiple_of(chip * first, 128), first)
        for slot, kind in enumerate((2, 0, 1)):
            first_ref[:, slot * first : (slot + 1) * first] = read(kind, part)
        part = pl.ds(pl.multiple_of(4 * first + chip * second, 128), second)
        gates = second + (128 if rest else 0)
        mixed = gates + 2 * second
        for kind, start in enumerate((gates, gates + second, 0)):
            second_ref[:, start : start + second] = read(kind, part)
        if rest:
            part = pl.ds(pl.multiple_of(rest_start + (chip // 2) * 128, 128), 128)
            gate, up, last = [half_tile(read(kind, part), chip % 2 == 1) for kind in range(3)]
            second_ref[:, mixed : mixed + 128] = low_lanes(gate, pltpu.roll(up, 64, 1)).astype(bf16)
            second_ref[:, second:gates] = low_lanes(last, 0.0).astype(bf16)


def unpack_units_kernel(place_ref, *refs):
    piece_refs, stack_ref, last_ref = refs[:8], refs[8], refs[9]
    first, second, rest, rest_start = unit_columns(last_ref.shape[1])

    def write(kind, part, values):
        if kind < 2:
            stack_ref[:, kind, part] = values
        else:
            last_ref[:, part] = values

    for i in range(4):
        chip = place_ref[0] ^ i
        first_ref, second_ref = piece_refs[i], piece_refs[4 + i]
        part = pl.ds(pl.multiple_of(chip * first, 128), first)
        for slot, kind in enumerate((2, 0, 1)):
            write(kind, part, first_ref[:, slot * first : (slot + 1) * first].astype(f32))
        part = pl.ds(pl.multiple_of(4 * first + chip * second, 128), second)
        gates = second + (128 if rest else 0)
        mixed = gates + 2 * second
        for kind, start in enumerate((gates, gates + second, 0)):
            write(kind, part, second_ref[:, start : start + second].astype(f32))
        if rest:
            part = pl.ds(pl.multiple_of(rest_start + (chip // 2) * 128, 128), 128)
            odd = chip % 2 == 1
            lane = lax.broadcasted_iota(jnp.int32, (1, 128), 1)
            mine = (lane >= 64) == odd
            both = second_ref[:, mixed : mixed + 128].astype(f32)
            turned = pltpu.roll(both, 64, 1)
            last = second_ref[:, second:gates].astype(f32)
            last = jnp.where(odd, pltpu.roll(last, 64, 1), last)
            for kind, values in enumerate(
                (jnp.where(odd, turned, both), jnp.where(odd, both, turned), last)
            ):
                held = stack_ref[:, kind, part] if kind < 2 else last_ref[:, part]
                write(kind, part, jnp.where(mine, values, held))


def on_place(kernel, name, operands, outs):
    vmem = pl.BlockSpec(memory_space=pltpu.VMEM)
    return pl.pallas_call(
        kernel,
        in_specs=[pl.BlockSpec(memory_space=pltpu.SMEM)] + [vmem] * len(operands),
        out_specs=[vmem] * len(outs),
        out_shape=[jax.ShapeDtypeStruct(*out) for out in outs],
        compiler_params=pltpu.CompilerParams(vmem_limit_bytes=16 << 20),
        cost_estimate=LIGHT,
        name=name,
    )(place().reshape(1), *operands)


def collected(pieces):
    return jnp.concatenate(crossed(pieces), axis=0)


def spread(pieces):
    return collected(exchange(pieces))


def split_kernel(place_ref, values_ref, *piece_refs):
    rows = piece_refs[0].shape[0]
    for i, piece_ref in enumerate(piece_refs):
        start = pl.multiple_of((place_ref[0] ^ i) * rows, rows)
        piece_ref[...] = values_ref[pl.ds(start, rows), :]


def returned(values):
    shape = (values.shape[0] // 4, values.shape[1])
    return exchange(on_place(split_kernel, "split_rows", (values,), [(shape, bf16)] * 4))


def gather_begin(own):
    return own, swap(own, NEAR), swap(own, MID)


def gather_diagonal(state):
    own, near, mid = state
    half = own.shape[0] // 2
    return swap(near[:half], MID), swap(mid[half:], NEAR)


def gather_end(state, diagonal):
    core = jnp.concatenate([*state, *diagonal], axis=0)
    return core, swap(core, TP)


def halves_begin(halves):
    return [swap(half, axis) for axis in (NEAR, MID) for half in halves]


def halves_diagonal(sides):
    return swap(sides[0], MID), swap(sides[3], NEAR)


def joined(pieces):
    rows = jnp.concatenate(pieces, axis=0)
    return rows, swap(rows, TP)


def row_pieces(*pairs):
    return [pair[core] for core in range(2) for pair in pairs]


def gather_rows(own):
    state = gather_begin(own)
    return gather_end(state, gather_diagonal(state))


def add_low(*values):
    return sum(value.astype(f32) for value in values).astype(bf16)


def add_halves(mine, others):
    half = mine.shape[0] // 2
    return add_low(mine[:half], others[:half]), add_low(mine[half:], others[half:])


def scatter_cores(mine, others):
    others = swap(others, TP)
    start = 3 * (mine.shape[0] // 4)
    return others, *add_halves(mine[start:], others[start:])


def scatter_middle(low, high):
    return swap(low, MID), swap(high, NEAR)


def side_sums(mine, others, first, middle):
    half = middle[0].shape[0]
    start = 2 * half * first
    near, mid = slice(start, start + 2 * half), slice(start + 2 * half, start + 4 * half)
    near = add_low(mine[near], others[near], jnp.pad(middle[0], ((0, half), (0, 0))))
    mid = add_low(mine[mid], others[mid], jnp.pad(middle[1], ((half, 0), (0, 0))))
    return near, mid


def scatter_end(mine, others, first, middle):
    near, mid = side_sums(mine, others, first, middle)
    return swap(near, NEAR), swap(mid, MID)


def stage(always, step, *operands):
    shapes = jax.eval_shape(step, *operands)

    def never(*_):
        return jax.tree.map(lambda s: jnp.zeros(s.shape, s.dtype), shapes)

    return lax.cond(always, step, never, *operands)


def gather_far(values):
    return lax.all_gather(values, FAR, axis=0, tiled=True)


def scatter_far(values):
    return lax.psum_scatter(values, FAR, scatter_dimension=0, tiled=True)


def plane_trees(values):
    return jnp.stack(exchange([values] * 4))


def sum_steps(values, axis, first=0, last=None):
    size = lax.axis_size(axis)
    if size & (size - 1):
        return lax.psum(values, axis) if first == 0 else values
    for i in range(size.bit_length() - 1)[first:last]:
        pairs = [(j, j ^ (1 << i)) for j in range(size)]
        values = values + lax.ppermute(values, axis, pairs)
    return values


def sum_over(values, axes):
    for axis in axes:
        values = sum_steps(values, axis)
    return values


def tree_rows(seg_ids, parents, valid_mask, row_ids):
    labels = jnp.arange(parents.shape[0], dtype=jnp.int32)
    parent_one = jnp.sum(
        jnp.where(seg_ids[:, None] == labels[None, :], parents[None, :], 0), axis=1
    )
    parent_two = jnp.sum(
        jnp.where(parent_one[:, None] == labels[None, :], parents[None, :], 0), axis=1
    )
    key_segs = seg_ids[None, :]
    related = (
        (key_segs == seg_ids[:, None])
        | (key_segs == parent_one[:, None])
        | (key_segs == parent_two[:, None])
    )
    allowed = related & (row_ids[None, :] <= row_ids[:, None]) & (valid_mask[None, :] > 0)
    allowed = allowed | (row_ids[None, :] == row_ids[:, None])
    positions = jnp.sum(allowed.astype(jnp.int32), axis=1) - 1
    return (parent_one, parent_two, positions)


def normalised(values):
    centre = values - jnp.mean(values, axis=-1, keepdims=True)
    inverse = lax.rsqrt(jnp.mean(centre * centre, axis=-1, keepdims=True) + epsilon)
    return centre * inverse, inverse


def write_halves(refs, values):
    whole_ref, low_ref, high_ref = refs
    values = values.astype(bf16)
    whole_ref[...] = values
    half = pl.num_programs(0) // 2

    @pl.when(pl.program_id(0) < half)
    def _():
        low_ref[...] = values

    @pl.when(pl.program_id(0) >= half)
    def _():
        high_ref[...] = values


def halves_specs(block, width, steps):
    half = steps // 2
    return [
        pl.BlockSpec((block, width), lambda i: (i, 0)),
        pl.BlockSpec((block, width), lambda i: (jnp.minimum(i, half - 1), 0)),
        pl.BlockSpec((block, width), lambda i: (jnp.maximum(i - half, 0), 0)),
    ]


def halves_shapes(rows, width):
    return [jax.ShapeDtypeStruct((size, width), bf16) for size in (rows, rows // 2, rows // 2)]


def norm_kernel(*refs):
    row_ref, part_refs, gain_ref, shift_ref = refs[0], refs[1:-4], refs[-4], refs[-3]
    if len(refs) == 4:
        row_ref, gain_ref, shift_ref, normed_ref = refs
        part_refs = ()
    else:
        normed_ref, added_ref = refs[-2:]
    values = row_ref[...].astype(f32)
    if part_refs:
        added = sum(ref[...].astype(f32) for ref in part_refs)
        added_ref[...] = added
        values = values + added
    normed_ref[...] = (normalised(values)[0] * gain_ref[...] + shift_ref[...]).astype(bf16)


def norm_rows(tokens, parts, gain, shift):
    rows, width = tokens.shape
    block = min(64, rows)
    of_rows = pl.BlockSpec((block, width), lambda i: (i, 0))
    of_gain = pl.BlockSpec((1, width), lambda i: (0, 0))
    kinds = [bf16] + [f32] * bool(parts)
    return pl.pallas_call(
        norm_kernel,
        grid=(rows // block,),
        in_specs=[of_rows] * (1 + len(parts)) + [of_gain] * 2,
        out_specs=[of_rows] * len(kinds),
        out_shape=[jax.ShapeDtypeStruct((rows, width), kind) for kind in kinds],
        compiler_params=pltpu.CompilerParams(vmem_limit_bytes=12 << 20),
        cost_estimate=LIGHT,
        name="norm_rows",
    )(tokens, *parts, gain[None], shift[None])


def norm_back_kernel(count, *refs):
    row_refs, part_refs = refs[:count], refs[count:-7]
    gain_ref, past_ref, *low_refs, grad_ref, sum_ref = refs[-7:]
    normed, inverse = normalised(sum(ref[...].astype(f32) for ref in row_refs))
    grad = sum(ref[...].astype(f32) for ref in part_refs)
    scaled = grad * gain_ref[...]
    centred = (
        scaled
        - jnp.mean(scaled, axis=-1, keepdims=True)
        - normed * jnp.mean(scaled * normed, axis=-1, keepdims=True)
    )
    total = past_ref[...].astype(f32) + inverse * centred
    grad_ref[...] = total
    write_halves(low_refs, total)

    @pl.when(pl.program_id(0) == 0)
    def _():
        sum_ref[...] = jnp.zeros_like(sum_ref)

    sum_ref[0:1] += jnp.sum(grad * normed, axis=0, keepdims=True)
    sum_ref[1:2] += jnp.sum(grad, axis=0, keepdims=True)


def norm_back(summands, parts, gain, past):
    rows, width = past.shape
    block = min(64, rows // 2)
    of_rows = pl.BlockSpec((block, width), lambda i: (i, 0))
    of_gain = pl.BlockSpec((1, width), lambda i: (0, 0))
    shape = jax.ShapeDtypeStruct
    return pl.pallas_call(
        partial(norm_back_kernel, len(summands)),
        grid=(rows // block,),
        in_specs=[of_rows] * (len(summands) + len(parts)) + [of_gain, of_rows],
        out_specs=halves_specs(block, width, rows // block)
        + [of_rows, pl.BlockSpec((2, width), lambda i: (0, 0))],
        out_shape=halves_shapes(rows, width) + [shape((rows, width), f32), shape((2, width), f32)],
        compiler_params=pltpu.CompilerParams(vmem_limit_bytes=12 << 20),
        cost_estimate=LIGHT,
        name="norm_back",
    )(*summands, *parts, gain[None], past)


def rope_tables(positions):
    half = ROT // 2
    lane = jnp.arange(2 * HD, dtype=jnp.int32) % HD
    power = (lane % half).astype(f32) * (-2.0 * math.log(10000.0) / ROT)
    inverse_freq = jnp.where(lane < ROT, jnp.exp(power), 0.0)
    angles = positions.astype(f32)[..., None] * inverse_freq
    return jnp.cos(angles), jnp.sin(angles)


def turn(values, cosine, sine):
    half = ROT // 2
    lane = lax.broadcasted_iota(jnp.int32, (1, 2 * HD), 1) % HD
    ahead = pltpu.roll(values, 2 * HD - half, 1)
    behind = pltpu.roll(values, half, 1)
    return values * cosine + jnp.where(lane < half, -ahead, behind) * sine


def allowed_keys(row_ref, col_ref):
    row_seg, parent_one, parent_two, row_id = [row_ref[0, i : i + 1, :] for i in range(4)]
    key_seg = col_ref[0, :, 0:1]
    key_id = col_ref[0, :, 1:2]
    related = (key_seg == row_seg) | (key_seg == parent_one) | (key_seg == parent_two)
    return (related & (key_id <= row_id)) | (key_id == row_id)


def dot_nt(a, b):
    return lax.dot_general(a, b, (((1,), (1,)), ((), ())), preferred_element_type=f32)


def dot_nn(a, b):
    return jnp.dot(a, b, preferred_element_type=f32)


def head_lanes(head):
    lane = lax.broadcasted_iota(jnp.int32, (1, 2 * HD), 1)
    return lane < HD if head == 0 else lane >= HD


def forward_kernel(
    core_ref, other_ref, weight_ref, bias_ref, row_ref, col_ref, keep_ref, cos_ref, sin_ref,
    qkv_ref, context_ref, log_ref, core_out_ref, other_out_ref, linear,
):
    half = core_ref.shape[0]
    width = context_ref.shape[3]
    linear[:half] = dot_nn(core_ref[...], weight_ref[:, : 3 * width]) + bias_ref[...]
    linear[half:] = dot_nn(other_ref[...], weight_ref[:, : 3 * width]) + bias_ref[...]
    mask = allowed_keys(row_ref, col_ref)
    cosine, sine = cos_ref[0], sin_ref[0]
    for pair in range(width // (2 * HD)):
        at = pair * 2 * HD
        lanes = slice(at, at + 2 * HD)
        query = turn(linear[:, lanes], cosine, sine).astype(bf16)
        key = turn(linear[:, width + at : width + at + 2 * HD], cosine, sine).astype(bf16)
        value = linear[:, 2 * width + at : 2 * width + at + 2 * HD]
        value_t = value.T.astype(bf16)
        value = value.astype(bf16)
        for core in range(2):
            rows = slice(core * half, (core + 1) * half)
            qkv_ref[core, 0, :, lanes] = query[rows]
            qkv_ref[core, 0, :, width + at : width + at + 2 * HD] = key[rows]
            qkv_ref[core, 0, :, 2 * width + at : 2 * width + at + 2 * HD] = value[rows]
        context_t = []
        for head in range(2):
            mine = jnp.where(head_lanes(head), query, jnp.zeros_like(query))
            scores = jnp.where(mask, dot_nt(key, mine) * score_scale, masked_fill)
            row_max = jnp.max(scores, axis=0, keepdims=True)
            exponent = jnp.exp(scores - row_max)
            row_sum = jnp.sum(exponent, axis=0, keepdims=True)
            log_ref[0, 2 * pair + head : 2 * pair + head + 1, :] = row_max + jnp.log(row_sum)
            context_t.append(
                dot_nn(value_t[head * HD : (head + 1) * HD], exponent.astype(bf16)) / row_sum
            )
        context = (jnp.concatenate(context_t, axis=0).T * keep_ref[0]).astype(bf16)
        for core in range(2):
            context_ref[core, 0, :, lanes] = context[core * half : (core + 1) * half]
    for core, out_ref in enumerate((core_out_ref, other_out_ref)):
        out_ref[...] = dot_nt(context_ref[core, 0], weight_ref[:, 3 * width :]).astype(bf16)


def backward_kernel(
    core_ref, other_ref, weight_ref, qkv_ref, row_ref, col_ref, keep_ref, cos_ref, sin_ref, log_ref,
    grad_ref, bias_ref, core_out_ref, other_out_ref, grads,
):
    half = core_ref.shape[0]
    width = weight_ref.shape[1] // 4
    grads[:half] = dot_nn(core_ref[...], weight_ref[:, 3 * width :])
    grads[half:] = dot_nn(other_ref[...], weight_ref[:, 3 * width :])
    mask = allowed_keys(row_ref, col_ref)
    cosine, sine = cos_ref[0], sin_ref[0]

    def both(at):
        return jnp.concatenate([qkv_ref[core, 0, :, at : at + 2 * HD] for core in range(2)], axis=0)

    for pair in range(width // (2 * HD)):
        at = pair * 2 * HD
        query, key, value = both(at), both(width + at), both(2 * width + at)
        key_t = key.astype(f32).T.astype(bf16)
        d_context = (grads[:, at : at + 2 * HD] * keep_ref[0]).astype(bf16)
        d_query_t = []
        d_key = jnp.zeros(query.shape, f32)
        d_value = jnp.zeros(query.shape, f32)
        for head in range(2):
            lanes = head_lanes(head)
            my_query = jnp.where(lanes, query, jnp.zeros_like(query))
            my_grad = jnp.where(lanes, d_context, jnp.zeros_like(d_context))
            log_total = log_ref[0, 2 * pair + head : 2 * pair + head + 1, :]
            scores = jnp.where(mask, dot_nt(key, my_query) * score_scale, masked_fill)
            probs = jnp.exp(scores - log_total)
            d_probs = dot_nt(value, my_grad)
            d_value = d_value + dot_nn(probs.astype(bf16), my_grad)
            inner = jnp.sum(probs * d_probs, axis=0, keepdims=True)
            d_scores = (probs * (d_probs - inner)).astype(bf16)
            d_key = d_key + dot_nn(d_scores, my_query)
            d_query_t.append(dot_nn(key_t[head * HD : (head + 1) * HD], d_scores))
        d_query = jnp.concatenate(d_query_t, axis=0).T * score_scale
        pieces = (
            turn(d_query, cosine, -sine).astype(bf16),
            turn(d_key * score_scale, cosine, -sine).astype(bf16),
            d_value.astype(bf16),
        )
        for kind, piece in enumerate(pieces):
            start = kind * width + at
            for core in range(2):
                grad_ref[core, 0, :, start : start + 2 * HD] = piece[core * half : (core + 1) * half]
            bias_ref[0, :, start : start + 2 * HD] = jnp.sum(
                piece.astype(f32), axis=0, keepdims=True
            )
    for core, out_ref in enumerate((core_out_ref, other_out_ref)):
        out_ref[...] = dot_nt(grad_ref[core, 0], weight_ref[:, : 3 * width]).astype(bf16)


def tree_block(*shape, first=0):
    return pl.BlockSpec((1,) + shape, lambda t: (first + t,) + (0,) * len(shape))


def row_block(rows, columns, first=0):
    return pl.BlockSpec((rows, columns), lambda t: (first + t, 0))


def core_block(rows, columns, first=0):
    return pl.BlockSpec((2, 1, rows, columns), lambda t: (0, first + t, 0, 0))


def whole_block(*shape):
    return pl.BlockSpec(shape, lambda t: (0,) * len(shape), pipeline_mode=pl.Buffered(1))


def attention_forward(cores, weights, bias, tree_info):
    row_info, col_info, keep, cosine, sine = tree_info
    model_width = weights.shape[0]
    width = weights.shape[1] // 4
    rows = cores[0].shape[0] // 4
    group = 2 * rows
    heads = width // HD
    shape = jax.ShapeDtypeStruct
    return pl.pallas_call(
        forward_kernel,
        grid=(4,),
        in_specs=[
            row_block(rows, model_width),
            row_block(rows, model_width),
            whole_block(*weights.shape),
            whole_block(1, 3 * width),
            tree_block(*row_info.shape[1:]),
            tree_block(*col_info.shape[1:]),
            tree_block(*keep.shape[1:]),
            tree_block(*cosine.shape[1:]),
            tree_block(*sine.shape[1:]),
        ],
        out_specs=[
            core_block(rows, 3 * width),
            core_block(rows, width),
            tree_block(heads, group),
            row_block(rows, model_width),
            row_block(rows, model_width),
        ],
        out_shape=[
            shape((2, 4, rows, 3 * width), bf16),
            shape((2, 4, rows, width), bf16),
            shape((4, heads, group), f32),
            shape((4 * rows, model_width), bf16),
            shape((4 * rows, model_width), bf16),
        ],
        scratch_shapes=[pltpu.VMEM((group, 3 * width), f32)],
        compiler_params=pltpu.CompilerParams(vmem_limit_bytes=24 << 20),
        cost_estimate=pl.CostEstimate(
            flops=16 * group * model_width * width * 2, bytes_accessed=32 << 20, transcendentals=4 << 20
        ),
        name="attention_forward",
    )(
        *cores,
        weights,
        bias,
        row_info,
        col_info,
        keep,
        cosine,
        sine,
    )


def attention_backward(cores, weights, qkv, log_totals, tree_info, first, count):
    row_info, col_info, keep, cosine, sine = tree_info
    model_width = weights.shape[0]
    width = weights.shape[1] // 4
    rows = cores[0].shape[0] // count
    group = 2 * rows
    heads = width // HD
    shape = jax.ShapeDtypeStruct
    return pl.pallas_call(
        backward_kernel,
        grid=(count,),
        in_specs=[
            row_block(rows, model_width),
            row_block(rows, model_width),
            whole_block(*weights.shape),
            core_block(rows, 3 * width, first=first),
            tree_block(*row_info.shape[1:], first=first),
            tree_block(*col_info.shape[1:], first=first),
            tree_block(*keep.shape[1:], first=first),
            tree_block(*cosine.shape[1:], first=first),
            tree_block(*sine.shape[1:], first=first),
            tree_block(heads, group, first=first),
        ],
        out_specs=[
            core_block(rows, 3 * width),
            tree_block(1, 3 * width),
            row_block(rows, model_width),
            row_block(rows, model_width),
        ],
        out_shape=[
            shape((2, count, rows, 3 * width), bf16),
            shape((count, 1, 3 * width), f32),
            shape((count * rows, model_width), bf16),
            shape((count * rows, model_width), bf16),
        ],
        scratch_shapes=[pltpu.VMEM((group, width), f32)],
        compiler_params=pltpu.CompilerParams(vmem_limit_bytes=24 << 20),
        cost_estimate=LIGHT
        if first == 3
        else pl.CostEstimate(
            flops=4 * count * group * model_width * width * 2,
            bytes_accessed=8 * count << 20,
            transcendentals=count << 20,
        ),
        name="attention_backward",
    )(
        *cores,
        weights,
        qkv,
        row_info,
        col_info,
        keep,
        cosine,
        sine,
        log_totals,
    )


def units_kernel(parts, *refs):
    main, mixed = parts
    x_refs, dy_refs, weight_ref = refs[0:2], refs[2:4], refs[4]
    before_refs, out_refs = refs[5:-4], refs[-2:]
    grad_ref, hidden_ref = refs[-4:-2]
    down = main + mixed
    for core in range(2):
        gate_up = dot_nn(x_refs[core][...], weight_ref[:, down:])
        d_hidden = dot_nn(dy_refs[core][...], weight_ref[:, :down])

        def unit(gate, up, grad):
            sigmoid = jax.nn.sigmoid(gate)
            active = gate * sigmoid
            d_gate = grad * up * sigmoid * (1.0 + gate * (1.0 - sigmoid))
            return active * up, d_gate, grad * active

        hidden, d_gate, d_up = unit(
            gate_up[:, :main], gate_up[:, main : 2 * main], d_hidden[:, :main]
        )
        hidden_ref[core, 0, :, :main] = hidden.astype(bf16)
        grad_ref[core, 0, :, :main] = d_gate.astype(bf16)
        grad_ref[core, 0, :, main : 2 * main] = d_up.astype(bf16)
        if mixed:
            both = gate_up[:, 2 * main :]
            hidden, d_gate, d_up = unit(both, pltpu.roll(both, 64, 1), d_hidden[:, main:])
            hidden_ref[core, 0, :, main:] = low_lanes(hidden, 0.0).astype(bf16)
            grad_ref[core, 0, :, 2 * main :] = low_lanes(d_gate, pltpu.roll(d_up, 64, 1)).astype(bf16)
        total = dot_nt(grad_ref[core, 0], weight_ref[:, down:])
        if before_refs:
            total = total + before_refs[core][...].astype(f32)
        out_refs[core][...] = total.astype(bf16)


def hidden_units(xs, dys, weights, parts, trees=(0, 4), before=()):
    first, count = trees
    model_width = weights.shape[0]
    main, mixed = parts
    wide = 2 * main + mixed
    rows = xs[0].shape[0] // 4
    shape = jax.ShapeDtypeStruct
    rows_of = row_block(rows, model_width)
    given = row_block(rows, model_width, first=first)
    return pl.pallas_call(
        partial(units_kernel, parts),
        grid=(count,),
        in_specs=[given] * 4 + [whole_block(*weights.shape)] + [given] * len(before),
        out_specs=[core_block(rows, wide), core_block(rows, main + mixed), rows_of, rows_of],
        out_shape=[
            shape((2, count, rows, wide), bf16),
            shape((2, count, rows, main + mixed), bf16),
            shape((count * rows, model_width), bf16),
            shape((count * rows, model_width), bf16),
        ],
        compiler_params=pltpu.CompilerParams(vmem_limit_bytes=28 << 20),
        cost_estimate=pl.CostEstimate(
            flops=4 * count * rows * model_width * 5 * main,
            bytes_accessed=8 * count << 20,
            transcendentals=count << 18,
        ),
        name="hidden_units",
    )(*xs, *dys, weights, *before)


def dot_tn(a, b):
    return lax.dot_general(a, b, (((0,), (0,)), ((), ())), preferred_element_type=f32)


def weight_kernel(counts, *refs):
    refs, out_ref = list(refs[:-1]), refs[-1]
    start = 0
    for left_count, right_count in counts:
        lefts, refs = refs[:left_count], refs[left_count:]
        rights, refs = refs[:right_count], refs[right_count:]
        columns = rights[0].shape[-1]
        rows = rights[0].shape[2]
        pieces = left_count // 2
        left_ends = [sum(left.shape[0] for left in lefts[: i + 1]) // rows for i in range(pieces)]
        right_ends = [sum(right.shape[1] for right in rights[: i + 1]) for i in range(right_count)]
        total = 0.0
        for core in range(2):
            tree = 0
            for end in sorted({*left_ends, *right_ends}):
                i = sum(tree >= left_end for left_end in left_ends)
                j = sum(tree >= right_end for right_end in right_ends)
                at = tree - ([0] + left_ends)[i]
                left = lefts[core * pieces + i][at * rows : (at + end - tree) * rows]
                at = tree - ([0] + right_ends)[j]
                right = rights[j][core, at : at + end - tree].reshape(-1, columns)
                total = total + dot_tn(left, right)
                tree = end
        out_ref[:, start : start + columns] = total.astype(bf16)
        start += columns


def weight_terms(*products, grant=20):
    model_width = products[0][0][0].shape[1]
    block = 256
    total = sum(rights[0].shape[-1] for _, rights in products)
    operands, specs = [], []
    for lefts, rights in products:
        operands += [*lefts, *rights]
        specs += [pl.BlockSpec((left.shape[0], block), lambda i: (0, i)) for left in lefts]
        specs += [whole_block(*right.shape) for right in rights]
    return pl.pallas_call(
        partial(weight_kernel, [(len(lefts), len(rights)) for lefts, rights in products]),
        grid=(model_width // block,),
        in_specs=specs,
        out_specs=pl.BlockSpec((block, total), lambda i: (i, 0)),
        out_shape=jax.ShapeDtypeStruct((model_width, total), bf16),
        compiler_params=pltpu.CompilerParams(vmem_limit_bytes=grant << 20),
        cost_estimate=LIGHT,
        name="weight_terms",
    )(*operands)


def out_kernel(first_ref, second_ref, first_weight_ref, second_weight_ref, *out_refs):
    for core, out_ref in enumerate(out_refs):
        total = dot_nt(first_ref[core, 0], first_weight_ref[...])
        total = total + dot_nt(second_ref[core, 0], second_weight_ref[...])
        out_ref[...] = total.astype(bf16)


def units_out(hiddens, weights, first):
    _, count, rows, _ = hiddens[1].shape
    model_width = weights[0].shape[0]
    return pl.pallas_call(
        out_kernel,
        grid=(count,),
        in_specs=[
            core_block(rows, hiddens[0].shape[-1], first=first),
            core_block(rows, hiddens[1].shape[-1]),
        ]
        + [whole_block(model_width, hidden.shape[-1]) for hidden in hiddens],
        out_specs=[row_block(rows, model_width)] * 2,
        out_shape=[jax.ShapeDtypeStruct((count * rows, model_width), bf16)] * 2,
        compiler_params=pltpu.CompilerParams(vmem_limit_bytes=14 << 20),
        cost_estimate=LIGHT,
        name="units_out",
    )(*hiddens, *weights)


def shards(
    tokens,
    cotangent,
    seg_ids,
    parents,
    valid_mask,
    ln1_gain,
    ln1_bias,
    w_qkv,
    qkv_bias,
    w_out,
    ln2_gain,
    ln2_bias,
    w_gate_up,
    w_down,
):
    own_rows, model_width = tokens.shape
    group_rows = seg_ids.shape[0]
    tp_index = lax.axis_index(TP)
    quarter = place()
    local_width = w_qkv.shape[2]
    width = local_width // 4
    weight_rows, local_units = w_down.shape
    main_a, main_b, rest, _ = unit_columns(local_units)
    mixed = 128 if rest else 0
    always = valid_mask[0] >= 0

    pieces = on_place(
        pack_heads_kernel, "pack_heads", (w_qkv.transpose(1, 0, 2), w_out), [((weight_rows, 4 * width), bf16)] * 4
    )
    attn_pieces = exchange(pieces)
    (normed1,) = norm_rows(tokens, (), ln1_gain, ln1_bias)
    unit_pieces = on_place(
        pack_units_kernel,
        "pack_units",
        (w_gate_up, w_down),
        [((weight_rows, 3 * main_a), bf16)] * 4
        + [((weight_rows, 3 * main_b + 2 * mixed), bf16)] * 4,
    )
    attn_pieces, normed1, unit_pieces = lax.optimization_barrier(
        (attn_pieces, normed1, unit_pieces)
    )
    attn_spread = collected(attn_pieces)
    attn_full = gather_far(attn_spread)

    def prepare(attn_spread, normed1, unit_pieces, seg_ids, valid_mask, parents):
        spread1 = gather_rows(normed1)
        spread_a, spread_b = spread(unit_pieces[:4]), spread(unit_pieces[4:])
        ints = jnp.concatenate([seg_ids, valid_mask, parents[0]])
        plane_ints = plane_trees(ints)

        def halves(values):
            parts = values.reshape(4, 2, own_rows)
            return jnp.where(tp_index == 0, parts, parts[:, ::-1]).reshape(4, group_rows)

        plane_segs = halves(plane_ints[:, :group_rows])
        plane_valid = halves(plane_ints[:, group_rows : 2 * group_rows])
        plane_parents = plane_ints[:, 2 * group_rows :]
        row_ids = (jnp.arange(group_rows, dtype=jnp.int32) + tp_index * own_rows) % group_rows
        parent_one, parent_two, positions = jax.vmap(tree_rows, in_axes=(0, 0, 0, None))(
            plane_segs, plane_parents, plane_valid, row_ids
        )
        all_ids = jnp.broadcast_to(row_ids, plane_segs.shape)
        row_info = jnp.stack([plane_segs, parent_one, parent_two, all_ids], axis=1)
        col_info = jnp.stack([jnp.where(plane_valid > 0, plane_segs, -1), all_ids], axis=2)
        keep = plane_valid.astype(f32)[..., None]
        tree_info = (row_info, col_info, keep, *rope_tables(positions))
        return spread1, spread_a, spread_b, tree_info

    spread1, spread_a, spread_b, tree_info = stage(
        always, prepare, attn_spread, normed1, unit_pieces, seg_ids, valid_mask, parents
    )
    own_valid = tree_info[2][0, :own_rows]
    units_a = gather_far(spread_a)
    units_b = gather_far(spread_b)

    def attend(spread1, attn_full, tree_info):
        own_bias = lax.dynamic_slice(qkv_bias, (0, quarter * width), (3, width))
        return attention_forward(spread1, attn_full, own_bias.reshape(1, -1), tree_info)

    dy_state = gather_begin(after(cotangent, spread1, spread_a, spread_b))
    qkv, context, log_totals, *attn_partial = stage(always, attend, spread1, attn_full, tree_info)

    def renorm(attn_partial, dy_state, tokens):
        dy_diagonal = gather_diagonal(dy_state)
        others, low, high = scatter_cores(*attn_partial)
        middle = scatter_middle(low, high)
        middle, dy_state, dy_diagonal = lax.optimization_barrier((middle, dy_state, dy_diagonal))
        spread_dy = gather_end(dy_state, dy_diagonal)
        parts = attn_partial[0], others, *scatter_end(attn_partial[0], others, 1, middle)
        normed2, attn_out = norm_rows(tokens, parts, ln2_gain, ln2_bias)
        return attn_out, gather_rows(normed2), spread_dy

    attn_out, spread2, spread_dy = stage(always, renorm, attn_partial, dy_state, tokens)

    d_units_a, hidden_a, *d_normed2 = hidden_units(spread2, spread_dy, units_a, (main_a, 0))
    terms_a = weight_terms((spread_dy, (hidden_a,)), (spread2, (d_units_a,)))
    grads_a = scatter_far(terms_a)

    def finish_units(terms_a, spread2, spread_dy, units_a, units_b, d_normed2, hidden_a, attn_out, tokens, cotangent):
        def run(xs, first, count):
            return hidden_units(xs, spread_dy, units_b, (main_b, mixed), (first, count), d_normed2)

        def out(hidden, first):
            return units_out((hidden_a, hidden), (units_a, units_b), first)

        last = run(spread2, 3, 1)
        low, high = add_halves(last[2], swap(last[3], TP))
        xs, low, high = lax.optimization_barrier((spread2, low, high))
        middle = scatter_middle(low, high)
        sides = run(xs, 1, 2)
        middle, sides = lax.optimization_barrier((middle, sides))
        others = swap(sides[3], TP)
        mlp_last = out(last[1], 3)
        others, mlp_last = lax.optimization_barrier((others, mlp_last))
        near, mid = side_sums(sides[2], others, 0, middle)
        xs, near, mid = lax.optimization_barrier((spread2, near, mid))
        near, mid = swap(near, NEAR), swap(mid, MID)
        own = run(xs, 0, 1)
        own_others = swap(own[3], TP)
        units = own, sides, last
        mlp_own, mlp_sides = out(own[1], 0), out(sides[1], 1)
        mlp_cores = add_halves(mlp_last[0], swap(mlp_last[1], TP))
        near, mid, mlp_cores, mlp_own, mlp_sides, units = lax.optimization_barrier(
            (near, mid, mlp_cores, mlp_own, mlp_sides, units)
        )
        mlp_middle = scatter_middle(*mlp_cores)
        terms_b = weight_terms(
            (spread_dy, [u[1] for u in units]), (spread2, [u[0] for u in units])
        )
        mlp_middle, terms_b, near, mid = lax.optimization_barrier((mlp_middle, terms_b, near, mid))
        parts = own[2], own_others, near, mid
        *d_low, d_residual, norm2_grads = norm_back(
            (tokens, attn_out), parts, ln2_gain, cotangent
        )
        return (mlp_own, mlp_sides, mlp_middle), terms_b, d_residual, d_low, norm2_grads

    mlp, terms_b, d_residual, d_low, norm2_grads = stage(
        always, finish_units, terms_a, spread2, spread_dy, units_a, units_b, d_normed2, hidden_a, attn_out, tokens, cotangent
    )
    grads_a, d_low = lax.optimization_barrier((grads_a, d_low))
    grads_b = scatter_far(terms_b)

    def attend_back(terms_b, d_low, attn_full, qkv, log_totals, tree_info, spread1, context, mlp, grads_a):
        mlp_own, mlp_sides, mlp_middle = mlp

        def back(cores, first, count):
            return attention_backward(cores, attn_full, qkv, log_totals, tree_info, first, count)

        state = halves_begin(d_low[1:])
        own = d_low[0], swap(d_low[0], TP)
        own_back = back(own, 0, 1)
        mlp_others = swap(mlp_own[1], TP), swap(mlp_sides[1], TP)
        near, mid = side_sums(mlp_sides[0], mlp_others[1], 0, mlp_middle)
        state, own_back, near, mid = lax.optimization_barrier((state, own_back, near, mid))
        diagonal = halves_diagonal(state)
        sides = joined(state)
        sides_back = back(sides, 1, 2)
        diagonal, sides_back, near, mid, grads_a = lax.optimization_barrier(
            (diagonal, sides_back, near, mid, grads_a)
        )
        pieces_a = returned(grads_a)
        last = joined(diagonal)
        last_back = back(last, 3, 1)
        last_back, pieces_a, near, mid = lax.optimization_barrier((last_back, pieces_a, near, mid))
        mlp_parts = swap(near, NEAR), swap(mid, MID)
        backs = own_back, sides_back, last_back
        terms = weight_terms(
            (spread1, [back[0] for back in backs]), (row_pieces(own, sides, last), (context,)),
            grant=48,
        )
        low, high = add_halves(last_back[2], swap(last_back[3], TP))
        bias_terms = sum(jnp.sum(back[1], axis=0) for back in backs)
        d_normed1 = own_back[2:], sides_back[2:], (low, high)
        return terms, bias_terms, d_normed1, (mlp_own[0], mlp_others[0], *mlp_parts), pieces_a

    attn_terms, bias_terms, d_normed1, mlp_parts, pieces_a = stage(
        always, attend_back, terms_b, d_low, attn_full, qkv, log_totals, tree_info, spread1, context, mlp, grads_a
    )
    attn_grads = scatter_far(attn_terms)

    def finish(attn_terms, d_normed1, mlp_parts, grads_b, d_residual, attn_out, tokens, bias_terms, norm2_grads, own_valid):
        own, sides, last = d_normed1
        middle = scatter_middle(*last)
        own_others, sides_others = swap(own[1], TP), swap(sides[1], TP)
        from_sides = scatter_end(sides[0], sides_others, 0, middle)
        from_sides, grads_b = lax.optimization_barrier((from_sides, grads_b))
        pieces_b = returned(grads_b)
        parts = own[0], own_others, *from_sides
        *_, tokens_grad, norm1_grads = norm_back((tokens,), parts, ln1_gain, d_residual)
        mlp_out = sum(part.astype(f32) for part in mlp_parts)
        stream_out = tokens.astype(f32) + attn_out + mlp_out
        output = stream_out.astype(bf16)
        squares = jnp.stack(
            [
                jnp.sum(own_valid * stream_out * stream_out),
                jnp.sum(own_valid * attn_out * attn_out),
                jnp.sum(own_valid * mlp_out * mlp_out),
                jnp.sum(own_valid),
            ]
        )
        bias_spread = lax.dynamic_update_slice(
            jnp.zeros((3, model_width), f32),
            bias_terms.reshape(3, width),
            (0, tp_index * local_width + quarter * width),
        )
        sums = jnp.concatenate(
            [norm1_grads, norm2_grads, bias_spread, jnp.pad(squares, (0, model_width - 4))[None]]
        )
        return output, tokens_grad, pieces_b, sum_over(sums, (TP,))

    output, tokens_grad, pieces_b, sums = stage(
        always, finish, attn_terms, d_normed1, mlp_parts, grads_b, d_residual, attn_out, tokens, bias_terms, norm2_grads, own_valid
    )
    sums = sum_over(sums, (NEAR, MID))
    far_sums = sum_steps(sums, FAR, 0, 1)
    gate_up_grad, down_grad = on_place(
        unpack_units_kernel,
        "unpack_units",
        (*pieces_a, *pieces_b),
        [(w_gate_up.shape, f32), (w_down.shape, f32)],
    )
    sums, gate_up_grad, down_grad = lax.optimization_barrier((far_sums, gate_up_grad, down_grad))
    sums = sum_steps(sums, FAR, 1)
    attn_grads, sums = lax.optimization_barrier((attn_grads, sums))
    attn_pieces = returned(attn_grads)
    qkv_grad, out_grad = on_place(
        unpack_heads_kernel,
        "unpack_heads",
        attn_pieces,
        [((3, weight_rows, local_width), f32), (w_out.shape, f32)],
    )
    qkv_grad = qkv_grad.transpose(1, 0, 2)
    norm_sums, bias_sums, square_sums = sums[:4], sums[4:7], sums[7]
    stream_rms = jnp.sqrt(square_sums[:3] / (square_sums[3] * model_width))
    qkv_bias_grad = lax.dynamic_slice(bias_sums, (0, tp_index * local_width), (3, local_width))
    return (
        output,
        tokens_grad,
        norm_sums[0],
        norm_sums[1],
        qkv_grad,
        qkv_bias_grad,
        out_grad,
        norm_sums[2],
        norm_sums[3],
        gate_up_grad,
        down_grad,
        stream_rms,
    )


def solution(mesh):
    planes = mesh.shape["fsdp"] // 4
    grid = Mesh(mesh.devices.reshape(planes, 2, 2, mesh.shape["tp"]), ALL)
    fsdp = (FAR, MID, NEAR)
    return jax.shard_map(
        shards,
        mesh=grid,
        in_specs=(
            P(ALL, None),
            P(ALL, None),
            P(fsdp),
            P(fsdp, None),
            P(fsdp),
            P(),
            P(),
            P(fsdp, None, TP),
            P(None, TP),
            P(fsdp, TP),
            P(),
            P(),
            P(fsdp, None, TP),
            P(fsdp, TP),
        ),
        out_specs=(
            P(ALL, None),
            P(ALL, None),
            P(),
            P(),
            P(fsdp, None, TP),
            P(None, TP),
            P(fsdp, TP),
            P(),
            P(),
            P(fsdp, None, TP),
            P(fsdp, TP),
            P(),
        ),
        check_vma=False,
    )
```
